32 devices in a mesh: blk: 2 (over y), dp: 16 (over z, x, core).
Axes of the slice: x: 2, y: 2, z: 4, core: 2. Of those that a mesh axis runs over, the one named last changes fastest.
Arguments:
- global_tokens: bfloat16 [16, 196, 768], P('dp', 'blk'), may hold values from -6 to 6
- local_tokens: bfloat16 [1024, 37, 768], P(('blk', 'dp')), may hold values from -6 to 6
- local_count: int32 [32], P(('blk', 'dp')), may hold values from 16 to 32, as said below
- first_gain: float32 [768], replicated, may hold values from 0.5 to 1.5
- first_shift: float32 [768], replicated, may hold values from -1.5 to 1.5
- qkv_weight: bfloat16 [768, 2304], replicated, may hold values from -0.21875 to 0.21875
- query_bias: float32 [768], replicated, may hold values from -2.5 to 2.5
- value_bias: float32 [768], replicated, may hold values from -1.5 to 1.5
- out_weight: bfloat16 [768, 768], replicated, may hold values from -0.75 to 0.75
- out_bias: float32 [768], replicated, may hold values from -1.5 to 1.5
- second_gain: float32 [768], replicated, may hold values from 0.5 to 1.5
- second_shift: float32 [768], replicated, may hold values from -1.5 to 1.5
- up_weight: bfloat16 [768, 3072], replicated, may hold values from -0.21875 to 0.21875
- up_bias: float32 [3072], replicated, may hold values from -1.5 to 1.5
- down_weight: bfloat16 [3072, 768], replicated, may hold values from -0.109375 to 0.109375
- mlp_down_bias: float32 [768], replicated, may hold values from -1.5 to 1.5
- global_cotan: bfloat16 [16, 196, 768], P('dp', 'blk'), may hold values from -6 to 6
- local_cotan: bfloat16 [1024, 37, 768], P(('blk', 'dp')), may hold values from -6 to 6
Outputs:
- global_out: bfloat16 [16, 196, 768], P('dp', 'blk')
- local_out: bfloat16 [1024, 37, 768], P(('blk', 'dp'))
- global_grad: bfloat16 [16, 196, 768], P('dp', 'blk')
- local_grad: bfloat16 [1024, 37, 768], P(('blk', 'dp'))
- first_gain_grad: float32 [768], replicated
- first_shift_grad: float32 [768], replicated
- qkv_weight_grad: float32 [768, 2304], replicated
- query_bias_gradient: float32 [768], replicated
- value_bias_grad: float32 [768], replicated
- out_weight_grad: float32 [768, 768], replicated
- out_bias_grad: float32 [768], replicated
- second_gain_grad: float32 [768], replicated
- second_shift_grad: float32 [768], replicated
- up_weight_grad: float32 [768, 3072], replicated
- up_bias_grad: float32 [3072], replicated
- down_weight_grad: float32 [3072, 768], replicated
- down_bias_grad: float32 [768], replicated
The draws below stay inside these ranges and needn't reach their ends.
Inputs may be any that keep to these rules, and one draw needn't show every extreme that they name: The live slots of a device are its first local_count slots; some device has all 32 live.
All inputs are finite; a program needn't handle non-finite values.
Results may differ from the reference program's by a relative error of at most 0.013.
Values may be sent and summed in bfloat16 or wider, within the bound.
No kernel may reach another device: no remote copies, remote signals or barrier semaphores. Data moves between devices by JAX's collectives and lax.ppermute only.
A program may use at most 256 MiB of HBM per device.

```python
import math
import jax
import jax.numpy as jnp
from jax import lax

D = 768
HEADS = 12
HEAD_DIM = 64
FF = 3072
GC_DEV = 1
LLEN = 37
LSLOT = 32
GLEN = 196
GCROPS = 16
LSLOTS = 1024
DEVICES = 32


def draw_local_count(key, part):
    key = jax.random.fold_in(key, 11)
    first_key, second_key = jax.random.split(key)
    least = max(1, LSLOT // 2)
    counts = jax.random.randint(first_key, (DEVICES,), least, LSLOT + 1)
    chosen = jax.random.randint(second_key, (), 0, DEVICES)
    return jnp.where(jnp.arange(DEVICES) == chosen, LSLOT, counts).astype(jnp.int32)


def block_scale(stream_key, shape, cuts, low, top_value):
    def one(axis_at, blocks):
        draws = jax.random.uniform(jax.random.fold_in(jax.random.fold_in(stream_key, 6), axis_at), (blocks,), jnp.float32, low / len(cuts), top_value / len(cuts))
        return jnp.repeat(jnp.exp(draws), shape[axis_at] // blocks).reshape((-1,) + (1,) * (len(shape) - axis_at - 1))

    loudness = one(*cuts[0])
    for cut in cuts[1:]:
        loudness = loudness * one(*cut)
    return loudness


def scatter_about(own_key, shape, scale, most, cuts=(), kind=jnp.bfloat16):
    array = scale * jax.random.normal(own_key, shape, jnp.float32)
    if cuts:
        array = array * block_scale(own_key, shape, cuts, -0.22, 0.18)
    return jnp.clip(array, -most, most).astype(kind)


def setup_inputs(seed: int = 0) -> dict:
    splits = jax.random.split(jax.random.key(seed), 19)
    return {
        "global_tokens": scatter_about(splits[0], (GCROPS, GLEN, D), 1.0, 6.0, ((0, 16), (1, 2))),
        "local_tokens": scatter_about(splits[1], (LSLOTS, LLEN, D), 1.0, 6.0, ((0, 32),)),
        "local_count": draw_local_count(jax.random.fold_in(splits[18], 71), 0),
        "first_gain": jnp.clip(1.0 + 0.1 * jax.random.normal(splits[3], (D,), jnp.float32), 0.5, 1.5),
        "first_shift": scatter_about(splits[4], (D,), 0.3, 1.5, (), jnp.float32),
        "qkv_weight": scatter_about(splits[5], (D, 3 * D), D ** -0.5, 0.21875),
        "query_bias": scatter_about(splits[6], (D,), 0.5, 2.5, (), jnp.float32),
        "value_bias": scatter_about(splits[7], (D,), 0.3, 1.5, (), jnp.float32),
        "out_weight": scatter_about(splits[8], (D, D), (D // 12) ** -0.5, 0.75),
        "out_bias": scatter_about(splits[9], (D,), 0.3, 1.5, (), jnp.float32),
        "second_gain": jnp.clip(1.0 + 0.1 * jax.random.normal(splits[10], (D,), jnp.float32), 0.5, 1.5),
        "second_shift": scatter_about(splits[11], (D,), 0.3, 1.5, (), jnp.float32),
        "up_weight": scatter_about(splits[12], (D, FF), D ** -0.5, 0.21875),
        "up_bias": scatter_about(splits[13], (FF,), 0.3, 1.5, (), jnp.float32),
        "down_weight": scatter_about(splits[14], (FF, D), FF ** -0.5, 0.109375),
        "mlp_down_bias": scatter_about(splits[15], (D,), 0.3, 1.5, (), jnp.float32),
        "global_cotan": scatter_about(splits[16], (GCROPS, GLEN, D), 1.0, 6.0, ((0, 16), (1, 2))),
        "local_cotan": scatter_about(splits[17], (LSLOTS, LLEN, D), 1.0, 6.0, ((0, 32),)),
    }


EPS = 1e-06

@jax.custom_vjp
def low(v):
    return lax.optimization_barrier(v.astype(jnp.bfloat16)).astype(jnp.float32)

@jax.custom_vjp
def low_back(v):
    return v

def low_keep(v):
    return (low(v), None)

def low_pass(kept, grad):
    return (grad,)

def back_keep(v):
    return (v, None)

def back_low(kept, grad):
    return (low(grad),)
low.defvjp(low_keep, low_pass)
low_back.defvjp(back_keep, back_low)

def norm_apply(layer_inputs, norm_gain, offset):
    center = layer_inputs - lax.optimization_barrier(jnp.mean(layer_inputs, axis=-1, keepdims=True))
    spread = lax.optimization_barrier(jnp.mean(center * center, axis=-1, keepdims=True))
    return center * lax.rsqrt(spread + EPS) * norm_gain + offset

def rounded_both(layer_inputs):
    return low_back(low(layer_inputs))

def project(layer_inputs, weight_matrix):
    return jnp.einsum('hbm,mi->hbi', layer_inputs, weight_matrix, precision=lax.Precision.HIGHEST)

def layer_forward(params, layer_inputs):
    first_gain, first_shift, qkv_weight, query_bias, value_bias, out_weight, out_bias, second_gain, second_shift, up_weight, up_bias, down_weight, mlp_down_bias = params
    seq_count, seq_len = (layer_inputs.shape[0], layer_inputs.shape[1])
    shape = (seq_count, seq_len, HEADS, HEAD_DIM)
    normed = low(norm_apply(layer_inputs, first_gain, first_shift))
    projected = project(normed, qkv_weight)
    queries = rounded_both(projected[..., :D] + query_bias)
    key_rows = rounded_both(projected[..., D:2 * D])
    value_rows = rounded_both(projected[..., 2 * D:] + value_bias)
    scores = jnp.einsum('sqhe,skhe->shqk', queries.reshape(shape), key_rows.reshape(shape), precision=lax.Precision.HIGHEST)
    scores = low_back(scores * (1.0 / math.sqrt(HEAD_DIM)))
    lifted = jnp.exp(scores - lax.optimization_barrier(jnp.max(scores, axis=-1, keepdims=True)))
    chances = lifted / lax.optimization_barrier(jnp.sum(lifted, axis=-1, keepdims=True))
    mixed = jnp.einsum('shqk,skhe->sqhe', low(chances), value_rows.reshape(shape), precision=lax.Precision.HIGHEST).reshape(seq_count, seq_len, D)
    middle = layer_inputs + low_back(project(rounded_both(mixed), out_weight) + out_bias)
    hidden = low_back(project(low(norm_apply(middle, second_gain, second_shift)), up_weight) + up_bias)
    return middle + project(low(jax.nn.gelu(hidden, approximate=False)), down_weight) + mlp_down_bias

def reference(global_tokens, local_tokens, local_count, first_gain, first_shift, qkv_weight, query_bias, value_bias, out_weight, out_bias, second_gain, second_shift, up_weight, up_bias, down_weight, mlp_down_bias, global_cotan, local_cotan):
    params = tuple((item.astype(jnp.float32) for item in (first_gain, first_shift, qkv_weight, query_bias, value_bias, out_weight, out_bias, second_gain, second_shift, up_weight, up_bias, down_weight, mlp_down_bias)))
    groups = GCROPS // GC_DEV
    glob_inputs = global_tokens.astype(jnp.float32).reshape(groups, GC_DEV, GLEN, D)
    glob_cot = global_cotan.astype(jnp.float32).reshape(groups, GC_DEV, GLEN, D)
    glob_live = jnp.ones((groups, GC_DEV), jnp.float32)
    local_inputs = local_tokens.astype(jnp.float32).reshape(DEVICES, LSLOT, LLEN, D)
    local_cot = local_cotan.astype(jnp.float32).reshape(DEVICES, LSLOT, LLEN, D)
    local_live = (jnp.arange(LSLOT, dtype=jnp.int32)[None, :] < local_count[:, None]).astype(jnp.float32)
    zeros = jax.tree.map(jnp.zeros_like, params)

    def group_step(summed, item):
        layer_inputs, cotangent, slot_live = item

        def forward(weights, rows):
            return layer_forward(weights, rows) * slot_live[:, None, None]
        outputs, pull = jax.vjp(forward, params, layer_inputs)
        weight_grads, input_grads = pull(cotangent)
        summed = jax.tree.map(jnp.add, summed, weight_grads)
        return (summed, (outputs.astype(jnp.bfloat16), input_grads.astype(jnp.bfloat16)))
    summed, (glob_out, glob_grad) = lax.scan(group_step, zeros, (glob_inputs, glob_cot, glob_live))
    summed, (loc_out, loc_grad) = lax.scan(group_step, summed, (local_inputs, local_cot, local_live))
    return (glob_out.reshape(GCROPS, GLEN, D), loc_out.reshape(LSLOTS, LLEN, D), glob_grad.reshape(GCROPS, GLEN, D), loc_grad.reshape(LSLOTS, LLEN, D), summed[0], summed[1], summed[2], summed[3], summed[4], summed[5], summed[6], summed[7], summed[8], summed[9], summed[10], summed[11], summed[12])
```

```python
import math

import jax
import jax.numpy as jnp
import numpy as np
from jax import lax
from jax.experimental import pallas as pl
from jax.experimental.pallas import tpu as pltpu
from jax.sharding import PartitionSpec as P

HEADS = 12
EPS = 1e-06
bf16 = jnp.bfloat16
f32 = jnp.float32
CHUNK = 48
BLANK = -1e30


def nn(a, b):
    return lax.dot_general(a, b, (((1,), (0,)), ((), ())), preferred_element_type=f32)


def nt(a, b):
    return lax.dot_general(a, b, (((1,), (1,)), ((), ())), preferred_element_type=f32)


def tn(a, b):
    return lax.dot_general(a, b, (((0,), (0,)), ((), ())), preferred_element_type=f32)


def normal(x):
    center = x - jnp.mean(x, axis=-1, keepdims=True)
    r = lax.rsqrt(jnp.mean(center * center, axis=-1, keepdims=True) + EPS)
    return center * r, r


def norm_back(n, r, dh, gain):
    e = dh * gain
    return r * (e - jnp.mean(e, axis=-1, keepdims=True) - n * jnp.mean(e * n, axis=-1, keepdims=True))


def fold(x):
    return jnp.sum(x.reshape(x.shape[0] // 8, 8, x.shape[1]), axis=0)


def head_masks():
    lane = lax.broadcasted_iota(jnp.int32, (1, 256), 1)
    return [((lane >= 64 * i) & (lane < 64 * i + 64)).astype(f32).astype(bf16) for i in range(4)]


def stack_heads(t, masks):
    return jnp.concatenate([t * m for m in masks], axis=0)


def pick_heads(t, n):
    low = lax.broadcasted_iota(jnp.int32, (n, 128), 1) < 64
    return jnp.concatenate(
        [
            jnp.where(low, t[0:n, 0:128], t[n : 2 * n, 0:128]),
            jnp.where(low, t[2 * n : 3 * n, 128:256], t[3 * n : 4 * n, 128:256]),
        ],
        axis=1,
    )


def attend(q, k, v, mask, masks, n):
    s = nt(stack_heads(q, masks), k) + mask
    p = jnp.exp(s - jnp.max(s, axis=-1, keepdims=True))
    p = (p * (1.0 / jnp.sum(p, axis=-1, keepdims=True))).astype(bf16)
    return p, pick_heads(nn(p, v), n)


def attend_back(q, k, v, p, do, masks, n):
    d = stack_heads(do, masks)
    pf = p.astype(f32)
    dp = nt(d, v)
    ds = (pf * (dp - jnp.sum(pf * dp, axis=-1, keepdims=True))).astype(bf16)
    dv = tn(p, d)
    dk = tn(ds, stack_heads(q, masks))
    dq = pick_heads(nn(ds, k), n) * 0.125
    return dq, dk, dv


def call(kernel, ins, outs, flops, scratch=(), vmem=40, aliases=None, smem=0):
    whole = pl.BlockSpec(memory_space=pltpu.VMEM)
    scalars = pl.BlockSpec(memory_space=pltpu.SMEM)
    size = sum(x.size * x.dtype.itemsize for x in ins) + sum(
        math.prod(s) * jnp.dtype(d).itemsize for s, d in outs
    )
    return pl.pallas_call(
        kernel,
        in_specs=[scalars] * smem + [whole] * (len(ins) - smem),
        out_specs=[whole] * len(outs),
        out_shape=[jax.ShapeDtypeStruct(s, d) for s, d in outs],
        scratch_shapes=list(scratch),
        compiler_params=pltpu.CompilerParams(vmem_limit_bytes=vmem * 2**20),
        cost_estimate=pl.CostEstimate(flops=flops, bytes_accessed=size, transcendentals=0),
    )(*ins)


def per_device(
    global_tokens,
    local_tokens,
    local_count,
    first_gain,
    first_shift,
    qkv_weight,
    query_bias,
    value_bias,
    out_weight,
    out_bias,
    second_gain,
    second_shift,
    up_weight,
    up_bias,
    down_weight,
    mlp_down_bias,
    global_cotan,
    local_cotan,
):
    crops, glen, D = global_tokens.shape
    slots, llen, _ = local_tokens.shape
    F = up_weight.shape[1]
    lpad = -(-llen // 8) * 8
    gpad = -(-glen // 16) * 16
    step = 4
    assert crops == 1 and D == 768 and lpad * 2 % 16 == 0 and slots % step == 0
    LR = slots * lpad
    R = LR + gpad
    SR = step * lpad
    pair = 2 * lpad
    nblk, ndp = lax.axis_size("blk"), lax.axis_size("dp")
    blk, dp = lax.axis_index("blk"), lax.axis_index("dp")
    assert nblk == 2 and ndp % 16 == 0
    nf = F // D
    quads = D // 256
    row = lambda t: t.reshape(1, -1)

    bit_of = {"c": 0, "x": 1, "z0": 2, "z1": 3, "y": 4}

    def swap(v, b):
        if b == "y":
            return lax.ppermute(v, "blk", [(0, 1), (1, 0)])
        m = b if isinstance(b, int) else 1 << bit_of[b]
        return lax.ppermute(v, "dp", [(i, i ^ m) for i in range(ndp)])

    me = (dp & 15) + 16 * blk
    relative = jnp.arange(32, dtype=jnp.int32) ^ me.astype(jnp.int32)

    def places(order):
        pos = jnp.zeros_like(relative)
        for b in order:
            pos = 2 * pos + ((relative >> bit_of[b]) & 1)
        return pos * CHUNK

    ORDERS = (("c", "x", "y", "z0", "z1"), ("c", "y", "x", "z0", "z1"))
    PLACES = [places(o) for o in ORDERS]

    xg = global_tokens.reshape(glen, D)
    xg_other = swap(xg, "y")

    def pad_slots(ref, xs, i):
        for j in range(step):
            xs[j * lpad : j * lpad + llen, :] = ref[step * i + j].astype(f32)
        return xs[...]

    lmask = np.full((4 * pair, pair), BLANK, np.float32)
    for r in range(4 * pair):
        s = (r % pair) // lpad
        lmask[r, s * lpad : s * lpad + llen] = 0.0
    gmask = np.full((8, 2 * gpad), BLANK, np.float32)
    gmask[:, :glen] = 0.0
    gmask[:, gpad : gpad + glen] = 0.0
    lmask = jnp.asarray(lmask)
    gmask = jnp.asarray(gmask[:1])

    def local_front(x_r, g_r, c_r, w_r, qb_r, vb_r, m_r, h_o, qkv_o, p_o, o_o, xs):
        xs[...] = jnp.zeros_like(xs)

        def norm_step(i, carry):
            x = pad_slots(x_r, xs, i)
            n, _ = normal(x)
            h_o[pl.ds(pl.multiple_of(i * SR, SR), SR), :] = (n * g_r[...] + c_r[...]).astype(bf16)
            return carry

        lax.fori_loop(0, slots // step, norm_step, 0)
        q = nn(h_o[...], w_r[:, 0:D]) + qb_r[...]
        qkv_o[:, 0:D] = q.astype(bf16) * jnp.asarray(0.125, bf16)
        qkv_o[:, D : 2 * D] = nn(h_o[...], w_r[:, D : 2 * D]).astype(bf16)
        qkv_o[:, 2 * D :] = (nn(h_o[...], w_r[:, 2 * D :]) + vb_r[...]).astype(bf16)

        masks = head_masks()

        def attn_step(i, carry):
            rows = pl.ds(pl.multiple_of(i * pair, pair), pair)
            for t in range(quads):
                a = 256 * t
                p, o = attend(
                    qkv_o[rows, a : a + 256],
                    qkv_o[rows, D + a : D + a + 256],
                    qkv_o[rows, 2 * D + a : 2 * D + a + 256],
                    m_r[...],
                    masks,
                    pair,
                )
                p_o[i * quads + t] = p
                o_o[rows, a : a + 256] = o.astype(bf16)
            return carry

        lax.fori_loop(0, slots // 2, attn_step, 0)

    h_l, qkv_l, p_l, o_l = call(
        local_front,
        [local_tokens, row(first_gain), row(first_shift), qkv_weight, row(query_bias), row(value_bias), lmask],
        [
            ((LR, D), bf16),
            ((LR, 3 * D), bf16),
            ((slots // 2 * quads, 4 * pair, pair), bf16),
            ((LR, D), bf16),
        ],
        2 * LR * D * 3 * D * 2,
        scratch=[pltpu.VMEM((SR, D), f32)],
    )

    def middle(
        n_r, x_r, dl_r, xg_r, xo_r, dg_r, g_r, c_r, w_r, qb_r, vb_r, m_r, ol_r, wo_r, bo_r, g2_r, c2_r,
        h_o, qkv_o, kv_o, p_o, og_o, x1_o, h2_o, dy_o, db_o, xs, gs, acc,
    ):
        masks = head_masks()
        gs[...] = jnp.zeros_like(gs)
        gs[0:glen, :] = xg_r[...].astype(f32)
        gs[gpad : gpad + glen, :] = xo_r[...].astype(f32)
        n, _ = normal(gs[...])
        h = (n * g_r[...] + c_r[...]).astype(bf16)
        h_o[...] = h[0:gpad]
        q = nn(h[0:gpad], w_r[:, 0:D]) + qb_r[...]
        qkv_o[:, 0:D] = q.astype(bf16) * jnp.asarray(0.125, bf16)
        k = nn(h, w_r[:, D : 2 * D]).astype(bf16)
        v = (nn(h, w_r[:, 2 * D :]) + vb_r[...]).astype(bf16)
        qkv_o[:, D : 2 * D] = k[0:gpad]
        qkv_o[:, 2 * D :] = v[0:gpad]
        kv_o[:, 0:D] = k[gpad:]
        kv_o[:, D:] = v[gpad:]
        for t in range(quads):
            a = 256 * t
            p, o = attend(qkv_o[:, a : a + 256], k[:, a : a + 256], v[:, a : a + 256], m_r[...], masks, gpad)
            p_o[t] = p
            og_o[:, a : a + 256] = o.astype(bf16)

        x1_o[0:LR, :] = nn(ol_r[...], wo_r[...]) + bo_r[...]
        x1g = nn(og_o[...], wo_r[...]) + bo_r[...] + gs[0:gpad, :]
        x1_o[LR:R, :] = x1g
        n2, _ = normal(x1g)
        h2_o[LR:R, :] = (n2 * g2_r[...] + c2_r[...]).astype(bf16)
        gs[0:glen, :] = dg_r[...].astype(f32)
        dy_o[LR:R, :] = gs[0:gpad, :].astype(bf16)
        acc[...] = fold(gs[0:gpad, :])
        xs[...] = jnp.zeros_like(xs)

        def rows_step(i, carry):
            rows = pl.ds(pl.multiple_of(i * SR, SR), SR)
            x1 = x1_o[rows, :] + pad_slots(x_r, xs, i)
            x1_o[rows, :] = x1
            n2, _ = normal(x1)
            h2_o[rows, :] = (n2 * g2_r[...] + c2_r[...]).astype(bf16)
            for j in range(step):
                live = jnp.where(step * i + j < n_r[0], 1.0, 0.0)
                xs[j * lpad : j * lpad + llen, :] = dl_r[step * i + j].astype(f32) * live
            dy = xs[...]
            dy_o[rows, :] = dy.astype(bf16)
            acc[...] += fold(dy)
            return carry

        lax.fori_loop(0, slots // step, rows_step, 0)
        db_o[...] = jnp.sum(acc[...], axis=0, keepdims=True)

    h_g, qkv_g, kv_x, p_g, o_g, x1, h2, dy, d_down_bias = call(
        middle,
        [
            local_count, local_tokens, local_cotan, xg, xg_other, global_cotan.reshape(glen, D),
            row(first_gain), row(first_shift), qkv_weight, row(query_bias), row(value_bias), gmask,
            o_l, out_weight, row(out_bias), row(second_gain), row(second_shift),
        ],
        [
            ((gpad, D), bf16), ((gpad, 3 * D), bf16), ((gpad, 2 * D), bf16),
            ((quads, 4 * gpad, 2 * gpad), bf16), ((gpad, D), bf16),
            ((R, D), f32), ((R, D), bf16), ((R, D), bf16), ((1, D), f32),
        ],
        2 * R * D * D * 2,
        scratch=[pltpu.VMEM((SR, D), f32), pltpu.VMEM((2 * gpad, D), f32), pltpu.VMEM((8, D), f32)],
        smem=1,
    )

    cuts = 3 if R % 48 == 0 else 1
    cut = R // cuts

    def put(g_o, pos_r, half, value):
        per = 32 // 2
        for j in range(per):
            g_o[pl.ds(pl.multiple_of(pos_r[half * per + j], 16), CHUNK), :] = value[
                j * CHUNK : (j + 1) * CHUNK, :
            ]

    def mlp(pos_r, h_r, d_r, u_r, b_r, w_r, a_o, du_o, g_o, ub_o):
        acc = jnp.zeros((8, D), f32)
        for i in range(cuts):
            rows = slice(i * cut, (i + 1) * cut)
            u = nn(h_r[rows, :], u_r[...]) + b_r[...]
            da = nt(d_r[rows, :], w_r[...])
            cdf = 0.5 + 0.5 * lax.erf(u * math.sqrt(0.5))
            a_o[rows, :] = (u * cdf).astype(bf16)
            slope = cdf + u * (jnp.exp(u * u * -0.5) * (1.0 / math.sqrt(2 * math.pi)))
            du = (da * slope).astype(bf16)
            du_o[rows, :] = du
            acc = acc + fold(du.astype(f32))
        ub_o[...] = jnp.sum(acc, axis=0, keepdims=True)
        put(g_o, pos_r, 0, tn(a_o[...], d_r[...]).astype(bf16))
        put(g_o, pos_r, 1, tn(h_r[...], du_o[...]).astype(bf16))

    acts, dus, groups, up_parts = [], [], [], []
    for f in range(nf):
        cols = slice(f * D, (f + 1) * D)
        a, du, g, ub = call(
            mlp,
            [PLACES[f % 2], h2, dy, up_weight[:, cols], row(up_bias[cols]), down_weight[cols, :]],
            [((R, D), bf16), ((R, D), bf16), ((2 * D, D), bf16), ((1, D), f32)],
            2 * R * D * D * 4,
            smem=1,
        )
        acts.append(a)
        dus.append(du)
        groups.append(g)
        up_parts.append(ub)

    def second_back(x1_r, dy_r, g2_r, wo_r, ol_r, og_r, wu_r, *rest):
        du_rs, (dx_o, do_o, wg_o, sm_o, acc) = rest[:nf], rest[nf:]
        for k in range(3):
            acc[k] = jnp.zeros((8, D), f32)
        for i in range(cuts):
            rows = slice(i * cut, (i + 1) * cut)
            dh = nt(du_rs[0][rows, :], wu_r[:, 0:D])
            for f in range(1, nf):
                dh = dh + nt(du_rs[f][rows, :], wu_r[:, f * D : (f + 1) * D])
            n, r = normal(x1_r[rows, :])
            dx = dy_r[rows, :].astype(f32) + norm_back(n, r, dh, g2_r[...])
            dx_o[rows, :] = dx
            g = dx.astype(bf16)
            do_o[rows, :] = g
            acc[0] += fold(dh * n)
            acc[1] += fold(dh)
            acc[2] += fold(g.astype(f32))
        wg = tn(ol_r[...], do_o[0:LR, :]) + tn(og_r[...], do_o[LR:R, :])
        wg_o[...] = wg.astype(bf16)
        do_o[...] = nt(do_o[...], wo_r[...]).astype(bf16)
        for k in range(3):
            sm_o[k : k + 1, :] = jnp.sum(acc[k], axis=0, keepdims=True)

    dx1, do, g_out, sums2 = call(
        second_back,
        [x1, dy, row(second_gain), out_weight, o_l, o_g, up_weight, *dus],
        [((R, D), f32), ((R, D), bf16), ((D, D), bf16), ((8, D), f32)],
        2 * R * D * D * (nf + 2),
        scratch=[pltpu.VMEM((3, 8, D), f32)],
        vmem=56,
    )

    do_g = do[LR:R]

    def global_back(q_r, kx_r, p_r, d_r, dq_o, own_o, other_o):
        masks = head_masks()
        for t in range(quads):
            a = 256 * t
            k = jnp.concatenate([q_r[:, D + a : D + a + 256], kx_r[:, a : a + 256]], axis=0)
            v = jnp.concatenate([q_r[:, 2 * D + a : 2 * D + a + 256], kx_r[:, D + a : D + a + 256]], axis=0)
            dq, dk, dv = attend_back(q_r[:, a : a + 256], k, v, p_r[t], d_r[:, a : a + 256], masks, gpad)
            dq_o[:, a : a + 256] = dq.astype(bf16)
            own_o[:, a : a + 256] = dk[0:gpad]
            own_o[:, D + a : D + a + 256] = dv[0:gpad]
            other_o[:, a : a + 256] = dk[gpad:].astype(bf16)
            other_o[:, D + a : D + a + 256] = dv[gpad:].astype(bf16)

    dq_g, kv_own, kv_other = call(
        global_back,
        [qkv_g, kv_x, p_g, do_g],
        [((gpad, D), bf16), ((gpad, 2 * D), f32), ((gpad, 2 * D), bf16)],
        2 * 4 * gpad * 2 * gpad * D * 6,
    )
    kv_back = swap(kv_other, "y")

    def local_back(q_r, p_r, d_r, o_r):
        masks = head_masks()

        def attn_step(i, carry):
            rows = pl.ds(pl.multiple_of(i * pair, pair), pair)
            for t in range(quads):
                a = 256 * t
                dq, dk, dv = attend_back(
                    q_r[rows, a : a + 256],
                    q_r[rows, D + a : D + a + 256],
                    q_r[rows, 2 * D + a : 2 * D + a + 256],
                    p_r[i * quads + t],
                    d_r[rows, a : a + 256],
                    masks,
                    pair,
                )
                o_r[rows, a : a + 256] = dq.astype(bf16)
                o_r[rows, D + a : D + a + 256] = dk.astype(bf16)
                o_r[rows, 2 * D + a : 2 * D + a + 256] = dv.astype(bf16)
            return carry

        lax.fori_loop(0, slots // 2, attn_step, 0)

    (dqkv_l,) = call(local_back, [qkv_l, p_l, do], [((LR, 3 * D), bf16)], 2 * LR * 4 * pair * D * 6)

    def qkv_back(pa_r, pb_r, hl_r, hg_r, dl_r, dq_r, own_r, got_r, gout_r, ga_o, gb_o, dg_o, sm_o):
        dg_o[:, 0:D] = dq_r[...]
        dg_o[:, D:] = (own_r[...] + got_r[...].astype(f32)).astype(bf16)
        put(ga_o, pa_r, 0, gout_r[...])
        for k, (g_o, p_r, half) in enumerate(((ga_o, pa_r, 1), (gb_o, pb_r, 0), (gb_o, pb_r, 1))):
            cols = slice(k * D, (k + 1) * D)
            w = tn(hl_r[...], dl_r[:, cols]) + tn(hg_r[...], dg_o[:, cols])
            put(g_o, p_r, half, w.astype(bf16))
            if k != 1:
                s = fold(dl_r[:, cols].astype(f32)) + fold(dg_o[:, cols].astype(f32))
                sm_o[k : k + 1, :] = jnp.sum(s, axis=0, keepdims=True)

    g_a, g_b, dqkv_g, sums_qkv = call(
        qkv_back,
        [PLACES[0], PLACES[1], h_l, h_g, dqkv_l, dq_g, kv_own, kv_back, g_out],
        [((2 * D, D), bf16), ((2 * D, D), bf16), ((gpad, 3 * D), bf16), ((8, D), f32)],
        2 * R * D * D * 3,
        smem=2,
    )

    def first_back(x_r, xg_r, g_r, w_r, dl_r, dg_r, dx_r, lo_o, go_o, sm_o, xs, gs, dh_s, acc):
        gs[...] = jnp.zeros_like(gs)
        gs[0:glen, :] = xg_r[...].astype(f32)
        n, r = normal(gs[...])
        dh = nt(dg_r[...], w_r[...])
        t = dx_r[LR:R, :] + norm_back(n, r, dh, g_r[...])
        go_o[...] = t[0:glen].astype(bf16)
        acc[0] = fold(dh * n)
        acc[1] = fold(dh)
        dh_s[...] = nt(dl_r[...], w_r[...])
        xs[...] = jnp.zeros_like(xs)

        def rows_step(i, carry):
            rows = pl.ds(pl.multiple_of(i * SR, SR), SR)
            n, r = normal(pad_slots(x_r, xs, i))
            dh = dh_s[rows, :]
            t = dx_r[rows, :] + norm_back(n, r, dh, g_r[...])
            for j in range(step):
                lo_o[step * i + j] = t[j * lpad : j * lpad + llen].astype(bf16)
            acc[0] += fold(dh * n)
            acc[1] += fold(dh)
            return carry

        lax.fori_loop(0, slots // step, rows_step, 0)
        for k in range(2):
            sm_o[k : k + 1, :] = jnp.sum(acc[k], axis=0, keepdims=True)

    local_grad, global_grad, sums1 = call(
        first_back,
        [local_tokens, xg, row(first_gain), qkv_weight, dqkv_l, dqkv_g, dx1],
        [((slots, llen, D), bf16), ((glen, D), bf16), ((8, D), f32)],
        2 * R * D * D * 3,
        scratch=[
            pltpu.VMEM((SR, D), f32), pltpu.VMEM((gpad, D), f32), pltpu.VMEM((LR, D), f32),
            pltpu.VMEM((2, 8, D), f32),
        ],
    )

    def output(n_r, x1_r, b_r, w_r, *rest):
        a_rs, (lo_o, go_o, ys) = rest[:nf], rest[nf:]
        for i in range(cuts):
            rows = slice(i * cut, (i + 1) * cut)
            y = x1_r[rows, :] + b_r[...]
            for f in range(nf):
                y = y + nn(a_rs[f][rows, :], w_r[f * D : (f + 1) * D, :])
            ys[rows, :] = y
        go_o[...] = ys[LR : LR + glen, :].astype(bf16)

        def slot_step(i, carry):
            for j in range(step):
                s = step * i + j
                live = jnp.where(s < n_r[0], 1.0, 0.0)
                lo_o[s] = (ys[pl.ds(pl.multiple_of(s * lpad, 8), llen), :] * live).astype(bf16)
            return carry

        lax.fori_loop(0, slots // step, slot_step, 0)

    local_out, global_out = call(
        output,
        [local_count, x1, row(mlp_down_bias), down_weight, *acts],
        [((slots, llen, D), bf16), ((glen, D), bf16)],
        2 * R * D * D * nf,
        scratch=[pltpu.VMEM((R, D), f32)],
        vmem=56,
        smem=1,
    )

    def add(a, b):
        return (a.astype(f32) + b.astype(f32)).astype(bf16)

    def halve(v, b):
        h = v.shape[0] // 2
        return add(v[:h], swap(v[h:], b))

    def halve_two(a, b, bit):
        h = a.shape[0] // 2
        got = swap(jnp.concatenate([a[h:], b[h:]], axis=0), bit)
        return add(a[:h], got[:h]), add(b[:h], got[h:])

    def double(v, b):
        return jnp.concatenate([v, swap(v, b)], axis=0)

    def double_two(a, b, bit):
        h = a.shape[0]
        got = swap(jnp.concatenate([a, b], axis=0), bit)
        return jnp.concatenate([a, got[:h]], axis=0), jnp.concatenate([b, got[h:]], axis=0)

    def reduce_two(a, b):
        a, b = halve(a, "c"), halve(b, "c")
        a, b = halve(a, "x"), halve(b, "y")
        a, b = halve(a, "y"), halve(b, "x")
        a, b = halve_two(a, b, "z0")
        a, b = halve_two(a, b, "z1")
        m = 16
        while m < ndp:
            v = jnp.concatenate([a, b], axis=0)
            v = add(v, swap(v, m))
            a, b = v[: a.shape[0]], v[a.shape[0] :]
            m *= 2
        a, b = double_two(a, b, "z1")
        a, b = double_two(a, b, "z0")
        a, b = double(a, "y"), double(b, "x")
        a, b = double(a, "x"), double(b, "y")
        return (a, swap(a, "c")), (b, swap(b, "c"))

    def place(pos_r, own_r, got_r, half, out, across):
        rows = own_r.shape[0]
        for j in range(16):
            p = pos_r[half * 16 + j]
            mine = p < rows
            q = pl.multiple_of(jnp.where(mine, p, p - rows), 16)
            value = jnp.where(mine, own_r[pl.ds(q, CHUNK), :], got_r[pl.ds(q, CHUNK), :])
            out[j * CHUNK : (j + 1) * CHUNK, :] = value.astype(f32)

    def place_mlp(pa_r, pb_r, *rest):
        ins, (up_o, down_o) = rest[: 2 * nf], rest[2 * nf :]
        for f in range(nf):
            p_r = (pa_r, pb_r)[f % 2]
            cols = slice(f * D, (f + 1) * D)
            place(p_r, ins[2 * f], ins[2 * f + 1], 0, down_o.at[cols, :], 0)
            place(p_r, ins[2 * f], ins[2 * f + 1], 1, up_o.at[:, cols], 0)

    def place_attn(pa_r, pb_r, a0, a1, b0, b1, out_o, qkv_o):
        place(pa_r, a0, a1, 0, out_o, 0)
        place(pa_r, a0, a1, 1, qkv_o.at[:, 0:D], 0)
        place(pb_r, b0, b1, 0, qkv_o.at[:, D : 2 * D], 0)
        place(pb_r, b0, b1, 1, qkv_o.at[:, 2 * D :], 0)

    small = jnp.concatenate(
        [sums1[0:2], sums_qkv[0:1], sums_qkv[2:3], sums2[2:3], sums2[0:2], d_down_bias, *up_parts], axis=0
    )
    small = lax.psum(small, ("blk", "dp"))

    mlp_sums = []
    for f in range(0, nf, 2):
        mlp_sums.extend(reduce_two(groups[f], groups[f + 1]))
    attn_sums = reduce_two(g_a, g_b)
    up_grad, down_grad = call(
        place_mlp,
        PLACES + [t for s in mlp_sums for t in s],
        [((D, F), f32), ((F, D), f32)],
        0,
        smem=2,
    )
    out_grad, qkv_grad = call(
        place_attn, PLACES + [t for s in attn_sums for t in s], [((D, D), f32), ((D, 3 * D), f32)], 0, smem=2
    )

    return (
        global_out.reshape(1, glen, D),
        local_out,
        global_grad.reshape(1, glen, D),
        local_grad,
        small[0],
        small[1],
        qkv_grad,
        small[2],
        small[3],
        out_grad,
        small[4],
        small[5],
        small[6],
        up_grad,
        small[8 : 8 + nf].reshape(-1),
        down_grad,
        small[7],
    )


def solution(mesh):
    tokens = (P("dp", "blk", None), P(("blk", "dp"), None, None))
    return jax.shard_map(
        per_device,
        mesh=mesh,
        in_specs=(*tokens, P(("blk", "dp")), *([P()] * 13), *tokens),
        out_specs=(*tokens, *tokens, *([P()] * 13)),
        check_vma=False,
    )
```

```python
import math

import jax
import jax.numpy as jnp
import numpy as np
from jax import lax
from jax.experimental import pallas as pl
from jax.experimental.pallas import tpu as pltpu
from jax.sharding import PartitionSpec as P

HEADS = 12
EPS = 1e-06
bf16 = jnp.bfloat16
f32 = jnp.float32
CHUNK = 48
BLANK = -1e30


def nn(a, b):
    return lax.dot_general(a, b, (((1,), (0,)), ((), ())), preferred_element_type=f32)


def nt(a, b):
    return lax.dot_general(a, b, (((1,), (1,)), ((), ())), preferred_element_type=f32)


def tn(a, b):
    return lax.dot_general(a, b, (((0,), (0,)), ((), ())), preferred_element_type=f32)


def normal(x):
    center = x - jnp.mean(x, axis=-1, keepdims=True)
    r = lax.rsqrt(jnp.mean(center * center, axis=-1, keepdims=True) + EPS)
    return center * r, r


def norm_back(n, r, dh, gain):
    e = dh * gain
    return r * (e - jnp.mean(e, axis=-1, keepdims=True) - n * jnp.mean(e * n, axis=-1, keepdims=True))


def fold(x):
    return jnp.sum(x.reshape(x.shape[0] // 8, 8, x.shape[1]), axis=0)


def head_masks():
    lane = lax.broadcasted_iota(jnp.int32, (1, 256), 1)
    return [((lane >= 64 * i) & (lane < 64 * i + 64)).astype(f32).astype(bf16) for i in range(4)]


def stack_heads(t, masks):
    return jnp.concatenate([t * m for m in masks], axis=0)


def pick_heads(t, n):
    low = lax.broadcasted_iota(jnp.int32, (n, 128), 1) < 64
    return jnp.concatenate(
        [
            jnp.where(low, t[0:n, 0:128], t[n : 2 * n, 0:128]),
            jnp.where(low, t[2 * n : 3 * n, 128:256], t[3 * n : 4 * n, 128:256]),
        ],
        axis=1,
    )


def attend(q, k, v, mask, masks, n):
    s = nt(stack_heads(q, masks), k) + mask
    p = jnp.exp(s - jnp.max(s, axis=-1, keepdims=True))
    p = (p * (1.0 / jnp.sum(p, axis=-1, keepdims=True))).astype(bf16)
    return p, pick_heads(nn(p, v), n)


def attend_back(q, k, v, p, do, masks, n):
    d = stack_heads(do, masks)
    pf = p.astype(f32)
    dp = nt(d, v)
    ds = (pf * (dp - jnp.sum(pf * dp, axis=-1, keepdims=True))).astype(bf16)
    dv = tn(p, d)
    dk = tn(ds, stack_heads(q, masks))
    dq = pick_heads(nn(ds, k), n) * 0.125
    return dq, dk, dv


def call(kernel, ins, outs, flops, scratch=(), vmem=40, smem=0, far=0, far_out=0, aliases=None, after=()):
    whole = pl.BlockSpec(memory_space=pltpu.VMEM)
    scalars = pl.BlockSpec(memory_space=pltpu.SMEM)
    lying = pl.BlockSpec(memory_space=pl.ANY)
    used, body = len(ins), kernel
    if after:

        def body(*refs):
            kernel(*refs[:used], *refs[used + len(after) :])

    size = sum(x.size * x.dtype.itemsize for x in ins) + sum(
        math.prod(s) * jnp.dtype(d).itemsize for s, d in outs
    )
    return pl.pallas_call(
        body,
        in_specs=[scalars] * smem + [whole] * (used - smem - far) + [lying] * (far + len(after)),
        out_specs=[lying] * far_out + [whole] * (len(outs) - far_out),
        out_shape=[jax.ShapeDtypeStruct(s, d) for s, d in outs],
        scratch_shapes=list(scratch),
        input_output_aliases=aliases or {},
        compiler_params=pltpu.CompilerParams(vmem_limit_bytes=vmem * 2**20),
        cost_estimate=pl.CostEstimate(flops=flops, bytes_accessed=size, transcendentals=0),
    )(*ins, *after)


def per_device(
    global_tokens,
    local_tokens,
    local_count,
    first_gain,
    first_shift,
    qkv_weight,
    query_bias,
    value_bias,
    out_weight,
    out_bias,
    second_gain,
    second_shift,
    up_weight,
    up_bias,
    down_weight,
    mlp_down_bias,
    global_cotan,
    local_cotan,
):
    crops, glen, D = global_tokens.shape
    slots, llen, _ = local_tokens.shape
    F = up_weight.shape[1]
    lpad = -(-llen // 8) * 8
    gpad = -(-glen // 16) * 16
    step = 4
    assert crops == 1 and D == 768 and lpad * 2 % 16 == 0 and slots % step == 0
    LR = slots * lpad
    R = LR + gpad
    SR = step * lpad
    pair = 2 * lpad
    nblk, ndp = lax.axis_size("blk"), lax.axis_size("dp")
    blk, dp = lax.axis_index("blk"), lax.axis_index("dp")
    assert nblk == 2 and ndp % 16 == 0
    nf = F // D
    quads = D // 256
    row = lambda t: t.reshape(1, -1)

    bit_of = {"c": 0, "x": 1, "z0": 2, "z1": 3, "y": 4}

    def swap(v, b):
        if b == "y":
            return lax.ppermute(v, "blk", [(0, 1), (1, 0)])
        m = b if isinstance(b, int) else 1 << bit_of[b]
        return lax.ppermute(v, "dp", [(i, i ^ m) for i in range(ndp)])

    me = (dp & 15) + 16 * blk
    relative = jnp.arange(32, dtype=jnp.int32) ^ me.astype(jnp.int32)

    def places(order):
        pos = jnp.zeros_like(relative)
        for b in order:
            pos = 2 * pos + ((relative >> bit_of[b]) & 1)
        return pos * CHUNK

    ORDERS = (("c", "x", "y", "z0", "z1"), ("c", "y", "x", "z0", "z1"))
    PLACES = [places(o) for o in ORDERS]

    xg = global_tokens.reshape(glen, D)
    xg_other = swap(xg, "y")

    def pad_slots(ref, xs, i):
        for j in range(step):
            xs[j * lpad : j * lpad + llen, :] = ref[step * i + j].astype(f32)
        return xs[...]

    lmask = np.full((4 * pair, pair), BLANK, np.float32)
    for r in range(4 * pair):
        s = (r % pair) // lpad
        lmask[r, s * lpad : s * lpad + llen] = 0.0
    gmask = np.full((8, 2 * gpad), BLANK, np.float32)
    gmask[:, :glen] = 0.0
    gmask[:, gpad : gpad + glen] = 0.0
    lmask = jnp.asarray(lmask)
    gmask = jnp.asarray(gmask[:1])

    def local_front(x_r, g_r, c_r, w_r, qb_r, vb_r, m_r, h_o, qkv_o, p_o, o_o, xs):
        xs[...] = jnp.zeros_like(xs)

        def norm_step(i, carry):
            x = pad_slots(x_r, xs, i)
            n, _ = normal(x)
            h_o[pl.ds(pl.multiple_of(i * SR, SR), SR), :] = (n * g_r[...] + c_r[...]).astype(bf16)
            return carry

        lax.fori_loop(0, slots // step, norm_step, 0)
        q = nn(h_o[...], w_r[:, 0:D]) + qb_r[...]
        qkv_o[:, 0:D] = q.astype(bf16) * jnp.asarray(0.125, bf16)
        qkv_o[:, D : 2 * D] = nn(h_o[...], w_r[:, D : 2 * D]).astype(bf16)
        qkv_o[:, 2 * D :] = (nn(h_o[...], w_r[:, 2 * D :]) + vb_r[...]).astype(bf16)

        masks = head_masks()

        def attn_step(i, carry):
            rows = pl.ds(pl.multiple_of(i * pair, pair), pair)
            for t in range(quads):
                a = 256 * t
                p, o = attend(
                    qkv_o[rows, a : a + 256],
                    qkv_o[rows, D + a : D + a + 256],
                    qkv_o[rows, 2 * D + a : 2 * D + a + 256],
                    m_r[...],
                    masks,
                    pair,
                )
                p_o[i * quads + t] = p
                o_o[rows, a : a + 256] = o.astype(bf16)
            return carry

        lax.fori_loop(0, slots // 2, attn_step, 0)

    h_l, qkv_l, p_l, o_l = call(
        local_front,
        [local_tokens, row(first_gain), row(first_shift), qkv_weight, row(query_bias), row(value_bias), lmask],
        [
            ((LR, D), bf16),
            ((LR, 3 * D), bf16),
            ((slots // 2 * quads, 4 * pair, pair), bf16),
            ((LR, D), bf16),
        ],
        2 * LR * D * 3 * D * 2,
        scratch=[pltpu.VMEM((SR, D), f32)],
    )

    def middle(
        n_r, x_r, dl_r, xg_r, xo_r, dg_r, g_r, c_r, w_r, qb_r, vb_r, m_r, ol_r, wo_r, bo_r, g2_r, c2_r,
        h_o, qkv_o, kv_o, p_o, og_o, x1_o, h2_o, dy_o, db_o, xs, gs, acc,
    ):
        masks = head_masks()
        gs[...] = jnp.zeros_like(gs)
        gs[0:glen, :] = xg_r[...].astype(f32)
        gs[gpad : gpad + glen, :] = xo_r[...].astype(f32)
        n, _ = normal(gs[...])
        h = (n * g_r[...] + c_r[...]).astype(bf16)
        h_o[...] = h[0:gpad]
        q = nn(h[0:gpad], w_r[:, 0:D]) + qb_r[...]
        qkv_o[:, 0:D] = q.astype(bf16) * jnp.asarray(0.125, bf16)
        k = nn(h, w_r[:, D : 2 * D]).astype(bf16)
        v = (nn(h, w_r[:, 2 * D :]) + vb_r[...]).astype(bf16)
        qkv_o[:, D : 2 * D] = k[0:gpad]
        qkv_o[:, 2 * D :] = v[0:gpad]
        kv_o[:, 0:D] = k[gpad:]
        kv_o[:, D:] = v[gpad:]
        for t in range(quads):
            a = 256 * t
            p, o = attend(qkv_o[:, a : a + 256], k[:, a : a + 256], v[:, a : a + 256], m_r[...], masks, gpad)
            p_o[t] = p
            og_o[:, a : a + 256] = o.astype(bf16)

        x1_o[0:LR, :] = nn(ol_r[...], wo_r[...]) + bo_r[...]
        x1g = nn(og_o[...], wo_r[...]) + bo_r[...] + gs[0:gpad, :]
        x1_o[LR:R, :] = x1g
        n2, _ = normal(x1g)
        h2_o[LR:R, :] = (n2 * g2_r[...] + c2_r[...]).astype(bf16)
        gs[0:glen, :] = dg_r[...].astype(f32)
        dy_o[LR:R, :] = gs[0:gpad, :].astype(bf16)
        acc[...] = fold(gs[0:gpad, :])
        xs[...] = jnp.zeros_like(xs)

        def rows_step(i, carry):
            rows = pl.ds(pl.multiple_of(i * SR, SR), SR)
            x1 = x1_o[rows, :] + pad_slots(x_r, xs, i)
            x1_o[rows, :] = x1
            n2, _ = normal(x1)
            h2_o[rows, :] = (n2 * g2_r[...] + c2_r[...]).astype(bf16)
            for j in range(step):
                live = jnp.where(step * i + j < n_r[0], 1.0, 0.0)
                xs[j * lpad : j * lpad + llen, :] = dl_r[step * i + j].astype(f32) * live
            dy = xs[...]
            dy_o[rows, :] = dy.astype(bf16)
            acc[...] += fold(dy)
            return carry

        lax.fori_loop(0, slots // step, rows_step, 0)
        db_o[...] = jnp.sum(acc[...], axis=0, keepdims=True)

    h_g, qkv_g, kv_x, p_g, o_g, x1, h2, dy, d_down_bias = call(
        middle,
        [
            local_count, local_tokens, local_cotan, xg, xg_other, global_cotan.reshape(glen, D),
            row(first_gain), row(first_shift), qkv_weight, row(query_bias), row(value_bias), gmask,
            o_l, out_weight, row(out_bias), row(second_gain), row(second_shift),
        ],
        [
            ((gpad, D), bf16), ((gpad, 3 * D), bf16), ((gpad, 2 * D), bf16),
            ((quads, 4 * gpad, 2 * gpad), bf16), ((gpad, D), bf16),
            ((R, D), f32), ((R, D), bf16), ((R, D), bf16), ((1, D), f32),
        ],
        2 * R * D * D * 2,
        scratch=[pltpu.VMEM((SR, D), f32), pltpu.VMEM((2 * gpad, D), f32), pltpu.VMEM((8, D), f32)],
        smem=1,
    )

    cuts = 3 if R % 48 == 0 else 1
    cut = R // cuts

    def put(g_o, pos_r, half, value):
        for j in range(16):
            g_o[pl.ds(pl.multiple_of(pos_r[half * 16 + j], 16), CHUNK), :] = value[
                j * CHUNK : (j + 1) * CHUNK, :
            ]

    def mlp(f, after):
        cols = slice(f * D, (f + 1) * D)
        first = f == 0

        def kernel(pos_r, h_r, d_r, b_r, *rest):
            if not first:
                dh_r, *rest = rest
            u_h, w_h, a_h, g_o, ub_o, dh_o, u_r, w_r, a_r, du_r, sems = rest
            load_u = pltpu.make_async_copy(u_h.at[:, cols], u_r, sems.at[0])
            load_w = pltpu.make_async_copy(w_h.at[cols, :], w_r, sems.at[1])
            store_a = pltpu.make_async_copy(a_r, a_h, sems.at[2])
            load_u.start()
            load_w.start()
            load_u.wait()
            load_w.wait()
            acc = jnp.zeros((8, D), f32)
            for i in range(cuts):
                rows = slice(i * cut, (i + 1) * cut)
                u = nn(h_r[rows, :], u_r[...]) + b_r[...]
                da = nt(d_r[rows, :], w_r[...])
                cdf = 0.5 + 0.5 * lax.erf(u * math.sqrt(0.5))
                a_r[rows, :] = (u * cdf).astype(bf16)
                slope = cdf + u * (jnp.exp(u * u * -0.5) * (1.0 / math.sqrt(2 * math.pi)))
                du = (da * slope).astype(bf16)
                du_r[rows, :] = du
                acc = acc + fold(du.astype(f32))
            ub_o[...] = jnp.sum(acc, axis=0, keepdims=True)
            store_a.start()
            put(g_o, pos_r, 0, tn(a_r[...], d_r[...]).astype(bf16))
            put(g_o, pos_r, 1, tn(h_r[...], du_r[...]).astype(bf16))
            for i in range(cuts):
                rows = slice(i * cut, (i + 1) * cut)
                dh = nt(du_r[rows, :], u_r[...])
                dh_o[rows, :] = dh if first else dh_r[rows, :] + dh
            store_a.wait()

        return call(
            kernel,
            [PLACES[f % 2], h2, dy, row(up_bias[cols])] + ([] if first else [mlp.dh]) + [up_weight, down_weight],
            [((R, D), bf16), ((2 * D, D), bf16), ((1, D), f32), ((R, D), f32)],
            2 * R * D * D * 5,
            scratch=[
                pltpu.VMEM((D, D), bf16), pltpu.VMEM((D, D), bf16), pltpu.VMEM((R, D), bf16),
                pltpu.VMEM((R, D), bf16), pltpu.SemaphoreType.DMA((3,)),
            ],
            smem=1,
            far=2,
            far_out=1,
            after=after,
            aliases={} if first else {4: 3},
        )

    def second_back(after):
        def kernel(x1_r, dy_r, dh_r, g2_r, wo_r, ol_r, og_r, dx_o, do_o, wg_o, sm_o, acc):
            for k in range(3):
                acc[k] = jnp.zeros((8, D), f32)
            for i in range(cuts):
                rows = slice(i * cut, (i + 1) * cut)
                dh = dh_r[rows, :]
                n, r = normal(x1_r[rows, :])
                dx = dy_r[rows, :].astype(f32) + norm_back(n, r, dh, g2_r[...])
                dx_o[rows, :] = dx
                g = dx.astype(bf16)
                do_o[rows, :] = g
                acc[0] += fold(dh * n)
                acc[1] += fold(dh)
                acc[2] += fold(g.astype(f32))
            wg = tn(ol_r[...], do_o[0:LR, :]) + tn(og_r[...], do_o[LR:R, :])
            wg_o[...] = wg.astype(bf16)
            do_o[...] = nt(do_o[...], wo_r[...]).astype(bf16)
            for k in range(3):
                sm_o[k : k + 1, :] = jnp.sum(acc[k], axis=0, keepdims=True)

        return call(
            kernel,
            [x1, dy, mlp.dh, row(second_gain), out_weight, o_l, o_g],
            [((R, D), f32), ((R, D), bf16), ((D, D), bf16), ((8, D), f32)],
            2 * R * D * D * 2,
            scratch=[pltpu.VMEM((3, 8, D), f32)],
            after=after,
        )

    def global_back(q_r, kx_r, p_r, d_r, dq_o, own_o, other_o):
        masks = head_masks()
        for t in range(quads):
            a = 256 * t
            k = jnp.concatenate([q_r[:, D + a : D + a + 256], kx_r[:, a : a + 256]], axis=0)
            v = jnp.concatenate([q_r[:, 2 * D + a : 2 * D + a + 256], kx_r[:, D + a : D + a + 256]], axis=0)
            dq, dk, dv = attend_back(q_r[:, a : a + 256], k, v, p_r[t], d_r[LR:R, a : a + 256], masks, gpad)
            dq_o[:, a : a + 256] = dq.astype(bf16)
            own_o[:, a : a + 256] = dk[0:gpad]
            own_o[:, D + a : D + a + 256] = dv[0:gpad]
            other_o[:, a : a + 256] = dk[gpad:].astype(bf16)
            other_o[:, D + a : D + a + 256] = dv[gpad:].astype(bf16)

    def local_back(q_r, p_r, d_r, o_r):
        masks = head_masks()

        def attn_step(i, carry):
            rows = pl.ds(pl.multiple_of(i * pair, pair), pair)
            for t in range(quads):
                a = 256 * t
                dq, dk, dv = attend_back(
                    q_r[rows, a : a + 256],
                    q_r[rows, D + a : D + a + 256],
                    q_r[rows, 2 * D + a : 2 * D + a + 256],
                    p_r[i * quads + t],
                    d_r[rows, a : a + 256],
                    masks,
                    pair,
                )
                o_r[rows, a : a + 256] = dq.astype(bf16)
                o_r[rows, D + a : D + a + 256] = dk.astype(bf16)
                o_r[rows, 2 * D + a : 2 * D + a + 256] = dv.astype(bf16)
            return carry

        lax.fori_loop(0, slots // 2, attn_step, 0)

    def qkv_back(pa_r, pb_r, hl_r, hg_r, dl_r, dq_r, own_r, got_r, gout_r, ga_o, gb_o, dg_o, sm_o):
        dg_o[:, 0:D] = dq_r[...]
        dg_o[:, D:] = (own_r[...] + got_r[...].astype(f32)).astype(bf16)
        put(ga_o, pa_r, 0, gout_r[...])
        for k, (g_o, p_r, half) in enumerate(((ga_o, pa_r, 1), (gb_o, pb_r, 0), (gb_o, pb_r, 1))):
            cols = slice(k * D, (k + 1) * D)
            w = tn(hl_r[...], dl_r[:, cols]) + tn(hg_r[...], dg_o[:, cols])
            put(g_o, p_r, half, w.astype(bf16))
            if k != 1:
                s = fold(dl_r[:, cols].astype(f32)) + fold(dg_o[:, cols].astype(f32))
                sm_o[k : k + 1, :] = jnp.sum(s, axis=0, keepdims=True)

    def first_back(x_r, xg_r, g_r, w_r, dl_r, dg_r, dx_r, lo_o, go_o, sm_o, xs, gs, dh_s, acc):
        gs[...] = jnp.zeros_like(gs)
        gs[0:glen, :] = xg_r[...].astype(f32)
        n, r = normal(gs[...])
        dh = nt(dg_r[...], w_r[...])
        t = dx_r[LR:R, :] + norm_back(n, r, dh, g_r[...])
        go_o[...] = t[0:glen].astype(bf16)
        acc[0] = fold(dh * n)
        acc[1] = fold(dh)
        dh_s[...] = nt(dl_r[...], w_r[...])
        xs[...] = jnp.zeros_like(xs)

        def rows_step(i, carry):
            rows = pl.ds(pl.multiple_of(i * SR, SR), SR)
            n, r = normal(pad_slots(x_r, xs, i))
            dh = dh_s[rows, :]
            t = dx_r[rows, :] + norm_back(n, r, dh, g_r[...])
            for j in range(step):
                lo_o[step * i + j] = t[j * lpad : j * lpad + llen].astype(bf16)
            acc[0] += fold(dh * n)
            acc[1] += fold(dh)
            return carry

        lax.fori_loop(0, slots // step, rows_step, 0)
        for k in range(2):
            sm_o[k : k + 1, :] = jnp.sum(acc[k], axis=0, keepdims=True)

    def output(n_r, x1_r, b_r, w_r, *rest):
        a_rs, (lo_o, go_o, ys) = rest[:nf], rest[nf:]
        for i in range(cuts):
            rows = slice(i * cut, (i + 1) * cut)
            y = x1_r[rows, :] + b_r[...]
            for f in range(nf):
                y = y + nn(a_rs[f][rows, :], w_r[f * D : (f + 1) * D, :])
            ys[rows, :] = y
        go_o[...] = ys[LR : LR + glen, :].astype(bf16)

        def slot_step(i, carry):
            for j in range(step):
                s = step * i + j
                live = jnp.where(s < n_r[0], 1.0, 0.0)
                lo_o[s] = (ys[pl.ds(pl.multiple_of(s * lpad, 8), llen), :] * live).astype(bf16)
            return carry

        lax.fori_loop(0, slots // step, slot_step, 0)

    def add(a, b):
        return (a.astype(f32) + b.astype(f32)).astype(bf16)

    class Flow:
        def __init__(self, steps):
            self.steps = steps
            self.sends = next(steps)

        def launch(self):
            self.got = [swap(v, b) for v, b in self.sends]

        def land(self):
            try:
                self.sends = self.steps.send(self.got)
            except StopIteration as end:
                self.result = end.value

    def halves(v):
        h = v.shape[0] // 2
        return v[:h], v[h:]

    def join(*parts):
        return jnp.concatenate(parts, axis=0)

    def sum_two(a, b, small=None):
        for bits in (("c", "c"), ("x", "y"), ("y", "x")):
            (a, sa), (b, sb) = halves(a), halves(b)
            ga, gb = yield [(sa, bits[0]), (sb, bits[1])]
            a, b = add(a, ga), add(b, gb)
        for bit in ("z0", "z1"):
            (a, sa), (b, sb) = halves(a), halves(b)
            (got,) = yield [(join(sa, sb), bit)]
            ga, gb = halves(got)
            a, b = add(a, ga), add(b, gb)
        m = 16
        while m < ndp:
            v = join(a, b)
            (got,) = yield [(v, m)]
            a, b = halves(add(v, got))
            m *= 2
        extra = []
        if small is not None:
            total = small()
            m = 16
            while m < ndp:
                total = total.astype(bf16)
                (got,) = yield [(total, m)]
                total = total.astype(f32) + got.astype(f32)
                m *= 2
        rows = 0 if small is None else total.shape[0]
        for bit in ("z1", "z0"):
            if rows:
                total = total.astype(bf16)
                extra = [total]
            (got,) = yield [(join(a, b, *extra), bit)]
            h = a.shape[0]
            a, b = join(a, got[:h]), join(b, got[h : 2 * h])
            if rows:
                total = total.astype(f32) + got[2 * h :].astype(f32)
        for bits in (("y", "x"), ("x", "y"), ("c", "c")):
            if rows:
                total = total.astype(bf16)
                extra = [total]
            ga, gb = yield [(join(a, *extra) if rows else a, bits[0]), (b, bits[1])]
            if rows:
                h = a.shape[0]
                total = total.astype(f32) + ga[h:].astype(f32)
                ga = ga[:h]
            if bits[0] != "c":
                a, b = join(a, ga), join(b, gb)
        sums = [a, ga, b, gb]
        return sums if small is None else (sums, total)

    def place(pos_r, own_r, got_r, half, out):
        rows = own_r.shape[0]
        for j in range(16):
            p = pos_r[half * 16 + j]
            mine = p < rows
            q = pl.multiple_of(jnp.where(mine, p, p - rows), 16)
            value = jnp.where(mine, own_r[pl.ds(q, CHUNK), :], got_r[pl.ds(q, CHUNK), :])
            out[j * CHUNK : (j + 1) * CHUNK, :] = value.astype(f32)

    def place_mlp(pa_r, pb_r, *rest):
        ins, (up_o, down_o) = rest[: 2 * nf], rest[2 * nf :]
        for f in range(nf):
            p_r = (pa_r, pb_r)[f % 2]
            cols = slice(f * D, (f + 1) * D)
            place(p_r, ins[2 * f], ins[2 * f + 1], 0, down_o.at[cols, :])
            place(p_r, ins[2 * f], ins[2 * f + 1], 1, up_o.at[:, cols])

    def place_attn(pa_r, pb_r, a0, a1, b0, b1, out_o, qkv_o):
        place(pa_r, a0, a1, 0, out_o)
        place(pa_r, a0, a1, 1, qkv_o.at[:, 0:D])
        place(pb_r, b0, b1, 0, qkv_o.at[:, D : 2 * D])
        place(pb_r, b0, b1, 1, qkv_o.at[:, 2 * D :])

    arrived = ()

    def run(kernel, *flows):
        nonlocal arrived
        for flow in flows:
            flow.launch()
        out = kernel(arrived) if kernel else None
        if kernel and flows:
            out, got = lax.optimization_barrier((out, [flow.got for flow in flows]))
            for flow, t in zip(flows, got):
                flow.got = t
        if flows:
            arrived = tuple(t for flow in flows for t in flow.got)
        for flow in flows:
            flow.land()
        return out

    acts, up_parts, blocks = [], [], []

    def take(result):
        a, g, ub, mlp.dh = result
        acts.append(a)
        blocks.append(g)
        up_parts.append(ub)

    take(run(lambda t: mlp(0, t)))
    take(run(lambda t: mlp(1, t)))
    one = Flow(sum_two(blocks[0], blocks[1]))
    take(run(lambda t: mlp(2, t), one))
    take(run(lambda t: mlp(3, t), one))
    two = Flow(sum_two(blocks[2], blocks[3]))
    dx1, do, g_out, sums2 = run(second_back, one, two)
    dq_g, kv_own, kv_other = run(
        lambda t: call(
            global_back,
            [qkv_g, kv_x, p_g, do],
            [((gpad, D), bf16), ((gpad, 2 * D), f32), ((gpad, 2 * D), bf16)],
            2 * 4 * gpad * 2 * gpad * D * 6,
            after=t,
        )
    )
    kv_back = swap(kv_other, "y")
    (dqkv_l,) = run(
        lambda t: call(
            local_back, [qkv_l, p_l, do], [((LR, 3 * D), bf16)], 2 * LR * 4 * pair * D * 6, after=t
        ),
        one,
        two,
    )
    g_a, g_b, dqkv_g, sums_qkv = run(
        lambda t: call(
            qkv_back,
            [PLACES[0], PLACES[1], h_l, h_g, dqkv_l, dq_g, kv_own, kv_back, g_out],
            [((2 * D, D), bf16), ((2 * D, D), bf16), ((gpad, 3 * D), bf16), ((8, D), f32)],
            2 * R * D * D * 3,
            smem=2,
            after=t,
        ),
        one,
        two,
    )

    def small():
        return join(
            sums1[0:2], sums_qkv[0:1], sums_qkv[2:3], sums2[2:3], sums2[0:2], d_down_bias, *up_parts,
            jnp.zeros((-(8 + nf) % 16, D), f32),
        )

    three = Flow(sum_two(g_a, g_b, small))
    local_grad, global_grad, sums1 = run(
        lambda t: call(
            first_back,
            [local_tokens, xg, row(first_gain), qkv_weight, dqkv_l, dqkv_g, dx1],
            [((slots, llen, D), bf16), ((glen, D), bf16), ((8, D), f32)],
            2 * R * D * D * 3,
            scratch=[
                pltpu.VMEM((SR, D), f32), pltpu.VMEM((gpad, D), f32), pltpu.VMEM((LR, D), f32),
                pltpu.VMEM((2, 8, D), f32),
            ],
            after=t,
        ),
        one,
        two,
        three,
    )
    local_out, global_out = run(
        lambda t: call(
            output,
            [local_count, x1, row(mlp_down_bias), down_weight, *acts],
            [((slots, llen, D), bf16), ((glen, D), bf16)],
            2 * R * D * D * nf,
            scratch=[pltpu.VMEM((R, D), f32)],
            vmem=56,
            smem=1,
            after=t,
        ),
        one,
        two,
        three,
    )
    while not hasattr(one, "result") or not hasattr(two, "result"):
        run(None, *[t for t in (one, two, three) if not hasattr(t, "result")])
    up_grad, down_grad = run(
        lambda t: call(
            place_mlp,
            PLACES + one.result + two.result,
            [((D, F), f32), ((F, D), f32)],
            0,
            smem=2,
            after=t,
        ),
        three,
    )
    while not hasattr(three, "result"):
        run(None, three)
    attn_sums, total = three.result
    out_grad, qkv_grad = call(place_attn, PLACES + attn_sums, [((D, D), f32), ((D, 3 * D), f32)], 0, smem=2)

    return (
        global_out.reshape(1, glen, D),
        local_out,
        global_grad.reshape(1, glen, D),
        local_grad,
        total[0],
        total[1],
        qkv_grad,
        total[2],
        total[3],
        out_grad,
        total[4],
        total[5],
        total[6],
        up_grad,
        total[8 : 8 + nf].reshape(-1),
        down_grad,
        total[7],
    )


def solution(mesh):
    tokens = (P("dp", "blk", None), P(("blk", "dp"), None, None))
    return jax.shard_map(
        per_device,
        mesh=mesh,
        in_specs=(*tokens, P(("blk", "dp")), *([P()] * 13), *tokens),
        out_specs=(*tokens, *tokens, *([P()] * 13)),
        check_vma=False,
    )
```

```python
import math

import jax
import jax.numpy as jnp
import numpy as np
from jax import lax
from jax.experimental import pallas as pl
from jax.experimental.pallas import tpu as pltpu
from jax.sharding import PartitionSpec as P

HEADS = 12
EPS = 1e-06
bf16 = jnp.bfloat16
f32 = jnp.float32
CHUNK = 48
BLANK = -1e30


def nn(a, b):
    return lax.dot_general(a, b, (((1,), (0,)), ((), ())), preferred_element_type=f32)


def nt(a, b):
    return lax.dot_general(a, b, (((1,), (1,)), ((), ())), preferred_element_type=f32)


def tn(a, b):
    return lax.dot_general(a, b, (((0,), (0,)), ((), ())), preferred_element_type=f32)


def normal(x):
    center = x - jnp.mean(x, axis=-1, keepdims=True)
    r = lax.rsqrt(jnp.mean(center * center, axis=-1, keepdims=True) + EPS)
    return center * r, r


def norm_back(n, r, dh, gain):
    e = dh * gain
    return r * (e - jnp.mean(e, axis=-1, keepdims=True) - n * jnp.mean(e * n, axis=-1, keepdims=True))


def fold(x):
    return jnp.sum(x.reshape(x.shape[0] // 8, 8, x.shape[1]), axis=0)


def head_masks():
    lane = lax.broadcasted_iota(jnp.int32, (1, 128), 1)
    return [(lane < 64).astype(f32).astype(bf16), (lane >= 64).astype(f32).astype(bf16)]


def stack_heads(t, masks):
    return jnp.concatenate([t * m for m in masks], axis=0)


def pick_heads(t):
    n = t.shape[0] // 2
    low = lax.broadcasted_iota(jnp.int32, (n, 128), 1) < 64
    return jnp.where(low, t[:n], t[n:])


def attend(loads, mask, masks):
    scores = [nt(k(), stack_heads(q(), masks)) + mask for q, k, _ in loads]
    chances = []
    for s in scores:
        p = jnp.exp(s - jnp.max(s, axis=0, keepdims=True))
        chances.append((p * (1.0 / jnp.sum(p, axis=0, keepdims=True))).astype(bf16))
    return [(p, pick_heads(tn(p, v()))) for p, (_, _, v) in zip(chances, loads)]


def attend_back(loads, store, masks):
    outer = [stack_heads(do(), masks) for _, _, _, _, do in loads]
    dps = [nt(v(), d) for d, (_, _, v, _, _) in zip(outer, loads)]
    dvs = [nn(p(), d).astype(bf16) for d, (_, _, _, p, _) in zip(outer, loads)]
    dss = []
    for dp, (_, _, _, p, _) in zip(dps, loads):
        pf = p().astype(f32)
        dss.append((pf * (dp - jnp.sum(pf * dp, axis=0, keepdims=True))).astype(bf16))
    for i, (ds, dv, (q, k, _, _, _)) in enumerate(zip(dss, dvs, loads)):
        dk = nn(ds, stack_heads(q(), masks))
        dq = pick_heads(tn(ds, k())) * 0.125
        store(i, dq.astype(bf16), dk, dv)


def call(kernel, ins, outs, flops, scratch=(), vmem=16, smem=0, far=0, far_out=0, aliases=None, wait=()):
    ins = list(ins)
    if wait:
        ins, _ = lax.optimization_barrier((ins, list(wait)))
    whole = pl.BlockSpec(memory_space=pltpu.VMEM)
    scalars = pl.BlockSpec(memory_space=pltpu.SMEM)
    lying = pl.BlockSpec(memory_space=pltpu.HBM)
    near = len(ins) - far

    def nbytes(s, d):
        return math.prod(s) * jnp.dtype(d).itemsize

    def pinned(i, t):
        if i >= near:
            return pltpu.with_memory_space_constraint(t, pltpu.HBM)
        if i >= smem and nbytes(t.shape, t.dtype) > 2**16:
            return pltpu.with_memory_space_constraint(t, pltpu.VMEM)
        return t

    def result(i, s, d):
        if i < far_out:
            return pltpu.HBM(s, d)
        if nbytes(s, d) > 2**16:
            return pltpu.VMEM(s, d)
        return jax.ShapeDtypeStruct(s, d)

    size = sum(nbytes(t.shape, t.dtype) for t in ins) + sum(nbytes(s, d) for s, d in outs)
    return pl.pallas_call(
        kernel,
        in_specs=[scalars] * smem + [whole] * (near - smem) + [lying] * far,
        out_specs=[lying] * far_out + [whole] * (len(outs) - far_out),
        out_shape=[result(i, s, d) for i, (s, d) in enumerate(outs)],
        scratch_shapes=list(scratch),
        input_output_aliases=aliases or {},
        compiler_params=pltpu.CompilerParams(vmem_limit_bytes=vmem * 2**20),
        cost_estimate=pl.CostEstimate(flops=1, bytes_accessed=1, transcendentals=0),
    )(*[pinned(i, t) for i, t in enumerate(ins)])


def per_device(
    global_tokens,
    local_tokens,
    local_count,
    first_gain,
    first_shift,
    qkv_weight,
    query_bias,
    value_bias,
    out_weight,
    out_bias,
    second_gain,
    second_shift,
    up_weight,
    up_bias,
    down_weight,
    mlp_down_bias,
    global_cotan,
    local_cotan,
):
    crops, glen, D = global_tokens.shape
    slots, llen, _ = local_tokens.shape
    F = up_weight.shape[1]
    nf = F // D
    lpad = -(-llen // 8) * 8
    gpad = -(-glen // 16) * 16
    assert crops == 1 and D == 768 and lpad * 2 % 16 == 0 and nf % 2 == 0
    LR = slots * lpad
    R = LR + gpad
    pair = 2 * lpad
    pairs = D // 128
    units = 4
    laps = slots // 2 // units
    assert laps * units * 2 == slots
    nblk, ndp = lax.axis_size("blk"), lax.axis_size("dp")
    blk, dp = lax.axis_index("blk"), lax.axis_index("dp")
    assert nblk == 2 and ndp % 16 == 0
    SR = 4 * lpad
    cuts = 3 if R % 48 == 0 else 1
    row_cuts = [slice(i * (R // cuts), (i + 1) * (R // cuts)) for i in range(cuts)]
    half_at = R // 32 * 16
    row_halves = [slice(0, half_at), slice(half_at, R)]

    bit_of = {"c": 0, "x": 1, "z0": 2, "z1": 3, "y": 4}

    def swap(v, b):
        if b == "y":
            return lax.ppermute(v, "blk", [(0, 1), (1, 0)])
        m = b if isinstance(b, int) else 1 << bit_of[b]
        return lax.ppermute(v, "dp", [(i, i ^ m) for i in range(ndp)])

    me = (dp & 15) + 16 * blk
    relative = jnp.arange(32, dtype=jnp.int32) ^ me.astype(jnp.int32)

    def places(order):
        pos = jnp.zeros_like(relative)
        for b in order:
            pos = 2 * pos + ((relative >> bit_of[b]) & 1)
        return pos * CHUNK

    ORDERS = (("c", "x", "y", "z0", "z1"), ("c", "y", "x", "z0", "z1"))
    PLACES = [places(o) for o in ORDERS]

    def copies(*triples):
        return [pltpu.make_async_copy(src, dst, sem) for src, dst, sem in triples]

    def start(moves):
        for t in moves:
            t.start()

    def finish(moves):
        for t in moves:
            t.wait()

    xg = global_tokens.reshape(glen, D)
    xg_other = swap(xg, "y")
    live = (jnp.arange(slots, dtype=jnp.int32) < local_count[0])[:, None, None]

    def pad(t):
        t = jnp.pad(t.transpose(1, 0, 2), ((0, lpad - llen), (0, 0), (0, 0)))
        return t.transpose(1, 0, 2).reshape(LR, D)

    def unpad(t):
        return t[:LR].reshape(slots, lpad, D)[:, :llen]

    x_l = lax.optimization_barrier(pad(local_tokens))
    dy_l = lax.optimization_barrier(pad(jnp.where(live, local_cotan, 0)))
    vectors = jnp.stack(
        [first_gain, first_shift, query_bias, value_bias, out_bias, second_gain, second_shift, mlp_down_bias]
    )
    vectors = jnp.concatenate([vectors, up_bias.reshape(nf, D)], axis=0)
    G1, C1, QB, VB, OB, G2, C2, DB, UB = range(9)

    assert 8 + nf <= 16
    lmask = np.full((pair, 2 * pair), BLANK, np.float32)
    for r in range(2 * pair):
        t = (r % pair) // lpad * lpad
        lmask[t : t + llen, r] = 0.0
    gmask = np.full((2 * gpad, 2 * gpad), BLANK, np.float32)
    gmask[:glen] = 0.0
    gmask[gpad : gpad + glen] = 0.0
    lmask = jnp.asarray(lmask)
    gmask = jnp.asarray(gmask)

    def front(
        v_r, m_r, x_r, dyl_r, xg_h, xo_h, dg_h, gm_h, w_h, wo_h, u_h, d_h,
        h_h, qkv_h, p_h, qkvg_o, pg_o, o_o, x1_o, h2_o, dy_o, led_o, wo_o, u_o, d_o,
        h_o, qkv_o, p_o, w, hx, gs, ds, xg_r, xo_r, dg_r, gm_r, acc, sems,
    ):
        def vec(i):
            return v_r[i : i + 1, :]

        cols = [slice(k * D, (k + 1) * D) for k in range(3)]
        loads_w = copies(*[(w_h.at[:, c], w.at[:, c], sems.at[k]) for k, c in enumerate(cols)])
        loads_g = copies(
            (xg_h, xg_r, sems.at[3]), (xo_h, xo_r, sems.at[4]), (dg_h, dg_r, sems.at[5]), (gm_h, gm_r, sems.at[6])
        )
        loads_next = copies(
            (wo_h, wo_o, sems.at[7]), (u_h.at[:, 0:D], u_o, sems.at[8]), (d_h.at[0:D, :], d_o, sems.at[9])
        )
        start(loads_w + loads_g + loads_next)

        def out_part(i):
            n = units * pair
            rows = pl.ds(pl.multiple_of(i * n, n), n)
            these = pl.ds(i * units * pairs, units * pairs)
            return copies(
                (qkv_o.at[rows], qkv_h.at[rows], sems.at[13 + 2 * i]),
                (p_o.at[these], p_h.at[these], sems.at[14 + 2 * i]),
            )


        def norm_step(i, carry):
            rows = pl.ds(pl.multiple_of(i * SR, SR), SR)
            n, _ = normal(x_r[rows, :].astype(f32))
            h_o[rows, :] = (n * vec(G1) + vec(C1)).astype(bf16)
            return carry

        lax.fori_loop(0, LR // SR, norm_step, 0)
        finish(loads_g + loads_w + loads_next)
        ds[...] = jnp.zeros_like(ds)
        ds[0:glen, :] = dg_r[...].astype(f32)
        dy_o[LR:R, :] = ds[...].astype(bf16)
        gs[...] = jnp.zeros_like(gs)
        gs[0:glen, :] = xg_r[...].astype(f32)
        gs[gpad : gpad + glen, :] = xo_r[...].astype(f32)
        n, _ = normal(gs[...])
        hg = (n * vec(G1) + vec(C1)).astype(bf16)
        h_o[LR:R, :] = hg[0:gpad]
        hx[...] = hg[gpad:]
        out_h = copies((h_o, h_h, sems.at[12]))
        start(out_h)
        for k, c in enumerate(cols):
            t = nn(h_o[...], w[:, c])
            tx = nn(hx[...], w[:, c])
            if k != 1:
                t = t + vec(QB if k == 0 else VB)
                tx = tx + vec(QB if k == 0 else VB)
            t, tx = t.astype(bf16), tx.astype(bf16)
            if k == 0:
                t = t * jnp.asarray(0.125, bf16)
            qkv_o[:, c] = t[0:LR]
            qkvg_o[0:gpad, c] = t[LR:R]
            qkvg_o[gpad:, c] = tx
        masks = head_masks()

        def attn_step(i, carry):
            where, loads = [], []
            for u in range(units):
                g = i * units + u
                rows = pl.ds(pl.multiple_of(g * pair, pair), pair)
                for t in range(pairs):
                    a = 128 * t
                    where.append((g * pairs + t, rows, slice(a, a + 128)))
                    loads.append([lambda rows=rows, b=k * D + a: qkv_o[rows, b : b + 128] for k in range(3)])
            for (at, rows, lanes), (pt, o) in zip(where, attend(loads, m_r[...], masks)):
                p_o[at] = pt
                o_o[rows, lanes] = o.astype(bf16)
            start(out_part(i))
            return carry

        lax.fori_loop(0, laps, attn_step, 0)
        loads = []
        for t in range(pairs):
            a, b, c = (slice(k * D + 128 * t, k * D + 128 * t + 128) for k in range(3))
            loads.append(
                [lambda a=a: qkvg_o[0:gpad, a], lambda b=b: qkvg_o[:, b], lambda c=c: qkvg_o[:, c]]
            )
        for t, (p, o) in enumerate(attend(loads, gm_r[...], masks)):
            pg_o[t] = p
            o_o[LR:R, 128 * t : 128 * t + 128] = o.astype(bf16)
        finish(out_h)
        for i in range(laps):
            finish(out_part(i))
        acc[...] = jnp.zeros_like(acc)
        x1_o[0:LR, :] = x_r[...].astype(f32)
        x1_o[LR:R, :] = gs[0:gpad, :]
        dy_o[0:LR, :] = dyl_r[...]
        for r in row_cuts:
            x1 = nn(o_o[r, :], wo_o[...]) + vec(OB) + x1_o[r, :]
            x1_o[r, :] = x1
            n2, _ = normal(x1)
            h2_o[r, :] = (n2 * vec(G2) + vec(C2)).astype(bf16)
            acc[...] += fold(dy_o[r, :].astype(f32))
        led_o[...] = jnp.zeros_like(led_o)
        led_o[7:8, :] = jnp.sum(acc[...], axis=0, keepdims=True)

    attn_kept = [((R, D), bf16), ((LR, 3 * D), bf16), ((slots // 2 * pairs, pair, 2 * pair), bf16)]
    h, qkv_l, p_l, qkv_g, p_g, o, x1, h2, dy, ledger, wo, wu, wd = call(
        front,
        [
            vectors, lmask, x_l, dy_l, xg, xg_other, global_cotan.reshape(glen, D), gmask,
            qkv_weight, out_weight, up_weight, down_weight,
        ],
        attn_kept
        + [
            ((2 * gpad, 3 * D), bf16), ((pairs, 2 * gpad, 2 * gpad), bf16), ((R, D), bf16),
            ((R, D), f32), ((R, D), bf16), ((R, D), bf16), ((16, D), f32),
            ((D, D), bf16), ((D, D), bf16), ((D, D), bf16),
        ],
        0,
        scratch=[pltpu.VMEM(s, d) for s, d in attn_kept]
        + [
            pltpu.VMEM((D, 3 * D), bf16), pltpu.VMEM((gpad, D), bf16), pltpu.VMEM((2 * gpad, D), f32),
            pltpu.VMEM((gpad, D), f32),
            pltpu.VMEM((glen, D), bf16), pltpu.VMEM((glen, D), bf16), pltpu.VMEM((glen, D), bf16),
            pltpu.VMEM((2 * gpad, 2 * gpad), f32), pltpu.VMEM((8, D), f32), pltpu.SemaphoreType.DMA((13 + 2 * laps,)),
        ],
        far=8,
        far_out=3,
        vmem=26,
    )

    def place_of(pos_r, i):
        at = pos_r[i]
        mine = at < 16 * CHUNK
        return mine, pl.ds(pl.multiple_of(jnp.where(mine, at, at - 16 * CHUNK), 16), CHUNK)

    def put(keep_o, send_o, pos_r, half, value):
        for j in range(0, 16, 2):
            mine, here = place_of(pos_r, half * 16 + j)
            x, y = (value[(j + k) * CHUNK : (j + k + 1) * CHUNK, :] for k in range(2))
            keep_o[here, :] = jnp.where(mine, x, y)
            send_o[here, :] = jnp.where(mine, y, x)

    def mlp(f, state, wait):
        first, last = f == 0, f == nf - 1
        there = slice((f + 1) * D, (f + 2) * D)

        def kernel(pos_r, h_r, d_r, v_r, u_r, w_r, side_r, led_r, u_h, w_h, a_h, *rest):
            if first:
                side_h, *rest = rest
            keep_o, send_o, led_o, dh_o, *rest = rest
            if not last:
                u_o, w_o, *rest = rest
            a_o, du_r, sems = rest
            moves = []
            if not last:
                moves = copies((u_h.at[:, there], u_o, sems.at[0]), (w_h.at[there, :], w_o, sems.at[1]))
            if first:
                moves += copies((side_r, side_h, sems.at[2]))
            (store,) = copies((a_o, a_h, sems.at[3]))
            start(moves)
            acc = jnp.zeros((8, D), f32)
            for i, rows in enumerate(row_cuts):
                u = nn(h_r[rows, :], u_r[...]) + v_r[UB + f : UB + f + 1, :]
                da = nt(d_r[rows, :], w_r[...])
                cdf = 0.5 + 0.5 * lax.erf(u * math.sqrt(0.5))
                a_o[rows, :] = (u * cdf).astype(bf16)
                slope = cdf + u * (jnp.exp(u * u * -0.5) * (1.0 / math.sqrt(2 * math.pi)))
                du = (da * slope).astype(bf16)
                du_r[rows, :] = du
                acc = acc + fold(du.astype(f32))
                if i == cuts - 2:
                    finish(moves)
            store.start()
            led_o[...] = led_r[...]
            led_o[8 + f : 9 + f, :] = jnp.sum(acc, axis=0, keepdims=True)
            put(keep_o, send_o, pos_r, 0, tn(a_o[...], d_r[...]).astype(bf16))
            put(keep_o, send_o, pos_r, 1, tn(h_r[...], du_r[...]).astype(bf16))
            for rows in row_cuts:
                dh = nt(du_r[rows, :], u_r[...])
                dh_o[rows, :] = dh if first else side_r[rows, :] + dh
            store.wait()

        u_w, d_w, side = state
        nonlocal ledger
        a, *out = call(
            kernel,
            [PLACES[f % 2], h2, dy, vectors, u_w, d_w, side, ledger, up_weight, down_weight],
            [((R, D), bf16)]
            + ([((R, D), f32)] if first else [])
            + [((D, D), bf16), ((D, D), bf16), ((16, D), f32), ((R, D), f32)]
            + ([] if last else [((D, D), bf16), ((D, D), bf16)]),
            0,
            scratch=[pltpu.VMEM((R, D), bf16), pltpu.VMEM((R, D), bf16), pltpu.SemaphoreType.DMA((4,))],
            far_out=2 if first else 1,
            smem=1,
            far=2,
            aliases={} if first else {6: 4},
            vmem=10,
            wait=wait,
        )
        if first:
            kept.append(out.pop(0))
        keep, send, ledger, dh, *state = out
        acts.append(a)
        return (keep, send), (*state, dh)

    def second_back(wait):
        def kernel(
            dy_r, dh_r, v_r, o_r, wo_r, q_r, p_r, led_r, x1_h, dx_h, do_o, wg_o, led_o, dq_o, own_o, other_o, acc, x1_r, dx_o, sems
        ):
            loads = copies(*[(x1_h.at[r], x1_r.at[r], sems.at[i]) for i, r in enumerate(row_cuts)])
            stores = copies((dx_o, dx_h, sems.at[cuts]))
            start(loads)
            for k in range(3):
                acc[k] = jnp.zeros((8, D), f32)
            for t, r in zip(loads, row_cuts):
                t.wait()
                dh = dh_r[r, :]
                n, rs = normal(x1_r[r, :])
                dx = dy_r[r, :].astype(f32) + norm_back(n, rs, dh, v_r[G2 : G2 + 1, :])
                dx_o[r, :] = dx
                g = dx.astype(bf16)
                do_o[r, :] = g
                acc[0] += fold(dh * n)
                acc[1] += fold(dh)
                acc[2] += fold(g.astype(f32))
            start(stores)
            wg_o[...] = tn(o_r[...], do_o[...]).astype(bf16)
            do_o[...] = nt(do_o[...], wo_r[...]).astype(bf16)
            led_o[...] = led_r[...]
            for k, i in enumerate((5, 6, 4)):
                led_o[i : i + 1, :] = jnp.sum(acc[k], axis=0, keepdims=True)
            loads = []
            for t in range(pairs):
                a, b, c = (slice(k * D + 128 * t, k * D + 128 * t + 128) for k in range(3))
                loads.append(
                    [
                        lambda a=a: q_r[0:gpad, a],
                        lambda b=b: q_r[:, b],
                        lambda c=c: q_r[:, c],
                        lambda t=t: p_r[t],
                        lambda a=a: do_o[LR:R, a],
                    ]
                )

            def store(t, dq, dk, dv):
                a, b = (slice(k * D + 128 * t, k * D + 128 * t + 128) for k in range(2))
                dq_o[:, a] = dq
                own_o[:, a] = dk[0:gpad].astype(bf16)
                own_o[:, b] = dv[0:gpad]
                other_o[:, a] = dk[gpad:].astype(bf16)
                other_o[:, b] = dv[gpad:]

            finish(stores)
            attend_back(loads, store, head_masks())

        return call(
            kernel,
            [dy, dh2, vectors, o, wo, qkv_g, p_g, ledger, x1],
            [
                ((R, D), f32), ((R, D), bf16), ((D, D), bf16), ((16, D), f32),
                ((gpad, D), bf16), ((gpad, 2 * D), bf16), ((gpad, 2 * D), bf16),
            ],
            0,
            scratch=[
                pltpu.VMEM((3, 8, D), f32), pltpu.VMEM((R, D), f32), pltpu.VMEM((R, D), f32),
                pltpu.SemaphoreType.DMA((cuts + 1,)),
            ],
            far=1,
            far_out=1,
            vmem=16,
            wait=wait,
        )

    def local_back(wait):
        def kernel(d_r, q_h, p_h, w_h, h_h, o_r, w_o, h_o, q_s, p_s, sems):
            def load(i):
                n = units * pair
                rows = pl.ds(pl.multiple_of(i * n, n), n)
                these = pl.ds(i * units * pairs, units * pairs)
                return copies(
                    (q_h.at[rows], q_s.at[rows], sems.at[2 * i]), (p_h.at[these], p_s.at[these], sems.at[2 * i + 1])
                )

            more = copies((w_h, w_o, sems.at[2 * laps]), (h_h, h_o, sems.at[2 * laps + 1]))
            for i in range(laps):
                start(load(i))
            start(more)
            masks = head_masks()

            def attn_step(i, carry):
                finish(load(i))
                where, loads = [], []
                for u in range(units):
                    g = i * units + u
                    rows = pl.ds(pl.multiple_of(g * pair, pair), pair)
                    for t in range(pairs):
                        a, b, c = (slice(k * D + 128 * t, k * D + 128 * t + 128) for k in range(3))
                        where.append((rows, a, b, c))
                        loads.append(
                            [lambda rows=rows, x=x: q_s[rows, x] for x in (a, b, c)]
                            + [lambda at=g * pairs + t: p_s[at], lambda rows=rows, a=a: d_r[rows, a]]
                        )

                def store(n, dq, dk, dv):
                    rows, a, b, c = where[n]
                    o_r[rows, a] = dq
                    o_r[rows, b] = dk.astype(bf16)
                    o_r[rows, c] = dv

                attend_back(loads, store, masks)
                return carry

            lax.fori_loop(0, laps - 1, attn_step, 0)
            finish(more)
            attn_step(laps - 1, 0)

        return call(
            kernel,
            [do, qkv_l, p_l, qkv_weight, h],
            [((R, 3 * D), bf16), ((D, 3 * D), bf16), ((R, D), bf16)],
            0,
            scratch=[
                pltpu.VMEM((LR, 3 * D), bf16), pltpu.VMEM((slots // 2 * pairs, pair, 2 * pair), bf16),
                pltpu.SemaphoreType.DMA((2 * laps + 2,)),
            ],
            far=4,
            vmem=15,
            wait=wait,
        )

    def qkv_back(wait):
        def kernel(pa_r, pb_r, dqkv_r, h_r, dq_r, own_r, got_r, gout_r, led_r, dqkv_o, ka_o, sa_o, kb_o, sb_o, led_o):
            led_o[...] = led_r[...]
            dqkv_o[LR:R, 0:D] = dq_r[...]
            dqkv_o[LR:R, D:] = (own_r[...].astype(f32) + got_r[...].astype(f32)).astype(bf16)
            put(ka_o, sa_o, pa_r, 0, gout_r[...])
            for k, at in enumerate(((ka_o, sa_o, pa_r, 1), (kb_o, sb_o, pb_r, 0), (kb_o, sb_o, pb_r, 1))):
                cols = slice(k * D, (k + 1) * D)
                put(*at, tn(h_r[...], dqkv_o[:, cols]).astype(bf16))
                if k != 1:
                    s = fold(dqkv_o[:, cols].astype(f32))
                    i = 2 + k // 2
                    led_o[i : i + 1, :] = jnp.sum(s, axis=0, keepdims=True)

        return call(
            kernel,
            [PLACES[0], PLACES[1], dqkv, h_back, dq_g, kv_own, kv_back, g_out, ledger],
            [((R, 3 * D), bf16)] + [((D, D), bf16)] * 4 + [((16, D), f32)],
            0,
            smem=2,
            vmem=5,
            aliases={2: 0},
            wait=wait,
        )

    def first_back(part, so_far, wait):
        rows = row_halves[part]
        n_rows = rows.stop - rows.start
        stop = min(rows.stop, LR)

        def kernel(v_r, w_r, dqkv_r, led_r, *rest):
            if part:
                _, *rest = rest
            x_h, xg_h, dx_h, wd_h, t_o, led_o, *rest = rest
            if not part:
                wd_o, *rest = rest
            dh_s, x_s, acc, xg_s, gs, dx_r, sems = rest
            moves = copies(
                (x_h.at[rows.start : stop], x_s.at[0 : stop - rows.start], sems.at[0]), (dx_h.at[rows], dx_r, sems.at[2])
            )
            if part:
                moves += copies((xg_h, xg_s, sems.at[1]))
            else:
                moves += copies((wd_h, wd_o, sems.at[1]))
            start(moves)
            dh_s[...] = nt(dqkv_r[rows, :], w_r[...])
            acc[...] = jnp.zeros_like(acc)
            finish(moves)
            if part:
                gs[...] = jnp.zeros_like(gs)
                gs[0:glen, :] = xg_s[...].astype(f32)
                x_s[stop - rows.start :, :] = gs[...].astype(bf16)

            def step(i, carry):
                here = pl.ds(pl.multiple_of(i * 16, 16), 16)
                there = pl.ds(pl.multiple_of(rows.start + i * 16, 16), 16)
                n, r = normal(x_s[here, :].astype(f32))
                dh = dh_s[here, :]
                t = dx_r[here, :] + norm_back(n, r, dh, v_r[G1 : G1 + 1, :])
                t_o[there, :] = t.astype(bf16)
                acc[0] += fold(dh * n)
                acc[1] += fold(dh)
                return carry

            lax.fori_loop(0, n_rows // 16, step, 0, unroll=8)
            led_o[...] = led_r[...]
            for k in range(2):
                led_o[k : k + 1, :] = led_r[k : k + 1, :] + jnp.sum(acc[k], axis=0, keepdims=True)

        return call(
            kernel,
            [vectors, wqkv, dqkv, ledger] + ([so_far] if part else []) + [x_l, xg, dx1, down_weight],
            [((R, D), bf16), ((16, D), f32)] + ([] if part else [((F, D), bf16)]),
            0,
            scratch=[
                pltpu.VMEM((n_rows, D), f32), pltpu.VMEM((n_rows, D), bf16), pltpu.VMEM((2, 8, D), f32),
                pltpu.VMEM((glen, D), bf16), pltpu.VMEM((gpad, D), f32), pltpu.VMEM((n_rows, D), f32),
                pltpu.SemaphoreType.DMA((3,)),
            ],
            far=4,
            vmem=11,
            aliases={4: 0} if part else {},
            wait=wait,
        )

    def output(part, so_far, wait):
        rows = row_halves[part]
        n_rows = rows.stop - rows.start

        def kernel(v_r, w_r, *rest):
            if part:
                _, *rest = rest
            x1_h, *rest = rest
            a_hs, (y_o, a_r, x1_r, sems) = rest[:nf], rest[nf:]
            loads = copies(
                *[(a_hs[f].at[rows], a_r.at[f], sems.at[f]) for f in range(nf)], (x1_h.at[rows], x1_r, sems.at[nf])
            )
            start(loads)
            loads[0].wait()
            y = nn(a_r[0], w_r[0:D, :])
            finish(loads[1:])
            y = y + x1_r[...] + v_r[DB : DB + 1, :]
            for f in range(1, nf):
                y = y + nn(a_r[f], w_r[f * D : (f + 1) * D, :])
            y_o[rows, :] = y.astype(bf16)

        return call(
            kernel,
            [vectors, wd_all] + ([so_far] if part else []) + [x1, *acts],
            [((R, D), bf16)],
            0,
            scratch=[
                pltpu.VMEM((nf, n_rows, D), bf16), pltpu.VMEM((n_rows, D), f32), pltpu.SemaphoreType.DMA((nf + 1,)),
            ],
            far=1 + nf,
            vmem=14,
            aliases={2: 0} if part else {},
            wait=wait,
        )[0]

    def add(a, b):
        return (a.astype(f32) + b.astype(f32)).astype(bf16)

    class Flow:
        def __init__(self, steps):
            self.steps = steps
            self.sends = next(steps)
            self.result = None

        def launch(self):
            self.got = [swap(v, b) for v, b in self.sends]

        def land(self):
            try:
                self.sends = self.steps.send(self.got)
            except StopIteration as end:
                self.result = end.value

    def halves(v):
        h = v.shape[0] // 2
        return v[:h], v[h:]

    def join(*parts):
        return jnp.concatenate(parts, axis=0)

    def sum_two(a, b, small=None):
        for bits in (("c", "c"), ("x", "y"), ("y", "x")):
            if bits[0] == "c":
                (a, sa), (b, sb) = a, b
            else:
                (a, sa), (b, sb) = halves(a), halves(b)
            ga, gb = yield [(sa, bits[0]), (sb, bits[1])]
            a, b = add(a, ga), add(b, gb)
        for bit in ("z0", "z1"):
            (a, sa), (b, sb) = halves(a), halves(b)
            (got,) = yield [(join(sa, sb), bit)]
            ga, gb = halves(got)
            a, b = add(a, ga), add(b, gb)
        m = 16
        while m < ndp:
            v = join(a, b)
            (got,) = yield [(v, m)]
            a, b = halves(add(v, got))
            m *= 2
        extra = []
        if small is not None:
            total = small()
            m = 16
            while m < ndp:
                total = total.astype(bf16)
                (got,) = yield [(total, m)]
                total = total.astype(f32) + got.astype(f32)
                m *= 2
        rows = 0 if small is None else total.shape[0]
        for bit in ("z1", "z0"):
            if rows:
                total = total.astype(bf16)
                extra = [total]
            (got,) = yield [(join(a, b, *extra), bit)]
            h = a.shape[0]
            a, b = join(a, got[:h]), join(b, got[h : 2 * h])
            if rows:
                total = total.astype(f32) + got[2 * h :].astype(f32)
        for bits in (("y", "x"), ("x", "y"), ("c", "c")):
            if rows:
                total = total.astype(bf16)
                extra = [total]
            ga, gb = yield [(join(a, *extra) if rows else a, bits[0]), (b, bits[1])]
            if rows:
                h = a.shape[0]
                total = total.astype(f32) + ga[h:].astype(f32)
                ga = ga[:h]
            if bits[0] != "c":
                a, b = join(a, ga), join(b, gb)
        sums = [a, ga, b, gb]
        return sums if small is None else (sums, total)

    def place(blocks, places, sums, outs, wait=()):
        made = [not isinstance(t, tuple) for t in outs]
        shapes = [t.shape if m else t for t, m in zip(outs, made)]

        def kernel(*refs):
            pos_rs, refs = refs[: len(places)], refs[len(places) :]
            sums_r, refs = refs[: len(sums)], refs[len(sums) + sum(made) :]
            outs_h, (work, sems) = refs[: len(outs)], refs[len(outs) :]
            moves = []
            for n, (which, where, side, half) in enumerate(blocks):
                pos_r, own_r, got_r = pos_rs[side], sums_r[2 * side], sums_r[2 * side + 1]
                if n >= 2:
                    moves[n - 2].wait()
                for j in range(0, 16, 2):
                    mine, here = place_of(pos_r, half * 16 + j)
                    x, y = own_r[here, :].astype(f32), got_r[here, :].astype(f32)
                    work[n % 2, j * CHUNK : (j + 1) * CHUNK, :] = jnp.where(mine, x, y)
                    work[n % 2, (j + 1) * CHUNK : (j + 2) * CHUNK, :] = jnp.where(mine, y, x)
                r, c = (slice(i * D, (i + 1) * D) for i in where)
                moves += copies((work.at[n % 2], outs_h[which].at[r, c], sems.at[n]))
                moves[n].start()
            for t in moves[-2:]:
                t.wait()

        before = [t for t, m in zip(outs, made) if m]
        return call(
            kernel,
            places + sums + before,
            [(s, f32) for s in shapes],
            0,
            scratch=[pltpu.VMEM((2, D, D), f32), pltpu.SemaphoreType.DMA((len(blocks),))],
            vmem=12,
            smem=len(places),
            far=len(before),
            far_out=len(outs),
            aliases={len(places + sums) + i: j for i, j in enumerate(j for j, m in enumerate(made) if m)},
            wait=wait,
        )

    waits = []

    def run(kernel, *flows):
        flows = [flow for flow in flows if flow.result is None]
        for flow in flows:
            flow.launch()
        sends = [v for flow in flows for v, _ in flow.sends]
        out = kernel(waits + sends) if kernel else None
        if kernel and flows:
            out, got = lax.optimization_barrier((out, [flow.got for flow in flows]))
            for flow, t in zip(flows, got):
                flow.got = t
        waits[:] = [t for flow in flows for t in flow.got]
        for flow in flows:
            flow.land()
        return out

    acts, blocks, kept = [], [], []
    state = (wu, wd, x1)

    def hidden(f, *flows):
        nonlocal state
        block, state = run(lambda wait: mlp(f, state, wait), *flows)
        blocks.append(block)

    hidden(0)
    (x1,) = kept
    hidden(1)
    one = Flow(sum_two(*blocks[0:2]))
    hidden(2, one)
    hidden(3, one)
    (dh2,) = state
    two = Flow(sum_two(*blocks[2:4]))
    dx1, do, g_out, ledger, dq_g, kv_own, kv_other = run(second_back, one, two)
    kv_back = swap(kv_other, "y")
    dqkv, wqkv, h_back = run(local_back, one, two)
    dqkv, ka, sa, kb, sb, ledger = run(qkv_back, one, two)

    three = Flow(sum_two((ka, sa), (kb, sb), lambda: ledger))
    grad, ledger, wd_all = run(lambda wait: first_back(0, None, wait), three, one, two)
    grad, ledger = run(lambda wait: first_back(1, grad, wait), three, one, two)
    y = run(lambda wait: output(0, None, wait), three, two)
    y = run(lambda wait: output(1, y, wait), three, one, two)

    def place_pair(k, flow, outs, wait):
        blocks = [(i, (0, f) if i == 0 else (f, 0), f % 2, 1 - i) for f in (2 * k, 2 * k + 1) for i in (1, 0)]
        return place(blocks, PLACES, flow.result, outs, wait)

    ends = lambda wait: lax.optimization_barrier((unpad(grad), jnp.where(live, unpad(y), 0)))
    nothing = lambda wait: ()
    local_grad, local_out = run(ends, three, one)
    run(nothing, three, two)
    run(nothing, three, one, two)
    while one.result is None:
        run(nothing, three, one, two)
    up_down = run(lambda wait: place_pair(0, one, [(D, F), (F, D)], wait), three, two)
    while two.result is None:
        run(nothing, three, two)
    up_grad, down_grad = run(lambda wait: place_pair(1, two, up_down, wait), three)
    while three.result is None:
        run(None, three)
    attn_sums, total = three.result
    out_grad, qkv_grad = place(
        [(0, (0, 0), 0, 0), (1, (0, 0), 0, 1), (1, (0, 1), 1, 0), (1, (0, 2), 1, 1)],
        PLACES,
        attn_sums,
        [(D, D), (D, 3 * D)],
    )

    return (
        y[LR : LR + glen].reshape(1, glen, D),
        local_out,
        grad[LR : LR + glen].reshape(1, glen, D),
        local_grad,
        total[0],
        total[1],
        qkv_grad,
        total[2],
        total[3],
        out_grad,
        total[4],
        total[5],
        total[6],
        up_grad,
        total[8 : 8 + nf].reshape(-1),
        down_grad,
        total[7],
    )


def solution(mesh):
    tokens = (P("dp", "blk", None), P(("blk", "dp"), None, None))
    return jax.shard_map(
        per_device,
        mesh=mesh,
        in_specs=(*tokens, P(("blk", "dp")), *([P()] * 13), *tokens),
        out_specs=(*tokens, *tokens, *([P()] * 13)),
        check_vma=False,
    )
```

```python
import math

import jax
import jax.numpy as jnp
import numpy as np
from jax import lax
from jax.experimental import pallas as pl
from jax.experimental.pallas import tpu as pltpu
from jax.sharding import PartitionSpec as P

HEADS = 12
EPS = 1e-06
bf16 = jnp.bfloat16
f32 = jnp.float32
CHUNK = 48
BLANK = -1e30


def nn(a, b):
    return lax.dot_general(a, b, (((1,), (0,)), ((), ())), preferred_element_type=f32)


def nt(a, b):
    return lax.dot_general(a, b, (((1,), (1,)), ((), ())), preferred_element_type=f32)


def tn(a, b):
    return lax.dot_general(a, b, (((0,), (0,)), ((), ())), preferred_element_type=f32)


def normal(x):
    center = x - jnp.mean(x, axis=-1, keepdims=True)
    r = lax.rsqrt(jnp.mean(center * center, axis=-1, keepdims=True) + EPS)
    return center * r, r


def norm_back(n, r, dh, gain):
    e = dh * gain
    return r * (e - jnp.mean(e, axis=-1, keepdims=True) - n * jnp.mean(e * n, axis=-1, keepdims=True))


def fold(x):
    return jnp.sum(x.reshape(x.shape[0] // 8, 8, x.shape[1]), axis=0)


def head_masks():
    lane = lax.broadcasted_iota(jnp.int32, (1, 128), 1)
    return [(lane < 64).astype(f32).astype(bf16), (lane >= 64).astype(f32).astype(bf16)]


def stack_heads(t, masks):
    return jnp.concatenate([t * m for m in masks], axis=0)


def pick_heads(t):
    n = t.shape[0] // 2
    low = lax.broadcasted_iota(jnp.int32, (n, 128), 1) < 64
    return jnp.where(low, t[:n], t[n:])


def attend(loads, mask, masks):
    scores = [nt(k(), stack_heads(q(), masks)) + mask for q, k, _ in loads]
    chances = []
    for s in scores:
        p = jnp.exp(s - jnp.max(s, axis=0, keepdims=True))
        chances.append((p * (1.0 / jnp.sum(p, axis=0, keepdims=True))).astype(bf16))
    return [(p, pick_heads(tn(p, v()))) for p, (_, _, v) in zip(chances, loads)]


def attend_back(loads, store, masks):
    outer = [stack_heads(do(), masks) for _, _, _, _, do in loads]
    dps = [nt(v(), d) for d, (_, _, v, _, _) in zip(outer, loads)]
    dvs = [nn(p(), d).astype(bf16) for d, (_, _, _, p, _) in zip(outer, loads)]
    dss = []
    for dp, (_, _, _, p, _) in zip(dps, loads):
        pf = p().astype(f32)
        dss.append((pf * (dp - jnp.sum(pf * dp, axis=0, keepdims=True))).astype(bf16))
    for i, (ds, dv, (q, k, _, _, _)) in enumerate(zip(dss, dvs, loads)):
        dk = nn(ds, stack_heads(q(), masks))
        dq = pick_heads(tn(ds, k())) * 0.125
        store(i, dq.astype(bf16), dk, dv)


def call(kernel, ins, outs, flops, scratch=(), vmem=16, smem=0, far=0, far_out=0, aliases=None, wait=()):
    ins = list(ins)
    if wait:
        ins, _ = lax.optimization_barrier((ins, list(wait)))
    whole = pl.BlockSpec(memory_space=pltpu.VMEM)
    scalars = pl.BlockSpec(memory_space=pltpu.SMEM)
    lying = pl.BlockSpec(memory_space=pltpu.HBM)
    near = len(ins) - far

    def nbytes(s, d):
        return math.prod(s) * jnp.dtype(d).itemsize

    def pinned(i, t):
        if i >= near:
            return pltpu.with_memory_space_constraint(t, pltpu.HBM)
        if i >= smem and nbytes(t.shape, t.dtype) > 2**16:
            return pltpu.with_memory_space_constraint(t, pltpu.VMEM)
        return t

    def result(i, s, d):
        if i < far_out:
            return pltpu.HBM(s, d)
        if nbytes(s, d) > 2**16:
            return pltpu.VMEM(s, d)
        return jax.ShapeDtypeStruct(s, d)

    size = sum(nbytes(t.shape, t.dtype) for t in ins) + sum(nbytes(s, d) for s, d in outs)
    return pl.pallas_call(
        kernel,
        in_specs=[scalars] * smem + [whole] * (near - smem) + [lying] * far,
        out_specs=[lying] * far_out + [whole] * (len(outs) - far_out),
        out_shape=[result(i, s, d) for i, (s, d) in enumerate(outs)],
        scratch_shapes=list(scratch),
        input_output_aliases=aliases or {},
        compiler_params=pltpu.CompilerParams(vmem_limit_bytes=vmem * 2**20),
        cost_estimate=pl.CostEstimate(flops=1, bytes_accessed=1, transcendentals=0),
    )(*[pinned(i, t) for i, t in enumerate(ins)])


def per_device(
    global_tokens,
    local_tokens,
    local_count,
    first_gain,
    first_shift,
    qkv_weight,
    query_bias,
    value_bias,
    out_weight,
    out_bias,
    second_gain,
    second_shift,
    up_weight,
    up_bias,
    down_weight,
    mlp_down_bias,
    global_cotan,
    local_cotan,
):
    crops, glen, D = global_tokens.shape
    slots, llen, _ = local_tokens.shape
    F = up_weight.shape[1]
    nf = F // D
    lpad = -(-llen // 8) * 8
    gpad = -(-glen // 16) * 16
    assert crops == 1 and D == 768 and lpad * 2 % 16 == 0 and nf % 2 == 0
    LR = slots * lpad
    R = LR + gpad
    pair = 2 * lpad
    pairs = D // 128
    units = 4
    laps = slots // 2 // units
    assert laps * units * 2 == slots
    nblk, ndp = lax.axis_size("blk"), lax.axis_size("dp")
    blk, dp = lax.axis_index("blk"), lax.axis_index("dp")
    assert nblk == 2 and ndp % 16 == 0
    SR = 4 * lpad
    cuts = 3 if R % 48 == 0 else 1
    row_cuts = [slice(i * (R // cuts), (i + 1) * (R // cuts)) for i in range(cuts)]
    half_at = R // 96 * 48
    assert R % 48 == 0
    row_halves = [slice(0, half_at), slice(half_at, R)]

    bit_of = {"c": 0, "x": 1, "z0": 2, "z1": 3, "y": 4}

    def swap(v, b):
        if b == "y":
            return lax.ppermute(v, "blk", [(0, 1), (1, 0)])
        m = b if isinstance(b, int) else 1 << bit_of[b]
        return lax.ppermute(v, "dp", [(i, i ^ m) for i in range(ndp)])

    me = (dp & 15) + 16 * blk
    relative = jnp.arange(32, dtype=jnp.int32) ^ me.astype(jnp.int32)

    def places(order):
        pos = jnp.zeros_like(relative)
        for b in order:
            pos = 2 * pos + ((relative >> bit_of[b]) & 1)
        return pos * CHUNK

    ORDERS = (("c", "x", "y", "z0", "z1"), ("c", "y", "x", "z0", "z1"))
    PLACES = [places(o) for o in ORDERS]

    def copies(*triples):
        return [pltpu.make_async_copy(src, dst, sem) for src, dst, sem in triples]

    def start(moves):
        for t in moves:
            t.start()

    def finish(moves):
        for t in moves:
            t.wait()

    xg = global_tokens.reshape(glen, D)
    xg_other = swap(xg, "y")
    live = (jnp.arange(slots, dtype=jnp.int32) < local_count[0])[:, None, None]

    def unpad(t):
        return t[:LR].reshape(slots, lpad, D)[:, :llen]

    singles = [first_gain, first_shift, query_bias, value_bias, out_bias, second_gain, second_shift, mlp_down_bias, up_bias]
    *singles, xg_other = lax.optimization_barrier((*singles, xg_other))
    vectors = jnp.concatenate([t.reshape(-1, D) for t in singles], axis=0)
    G1, C1, QB, VB, OB, G2, C2, DB, UB = range(9)

    assert 8 + nf <= 16
    lmask = np.full((pair, 2 * pair), BLANK, np.float32)
    for r in range(2 * pair):
        t = (r % pair) // lpad * lpad
        lmask[t : t + llen, r] = 0.0
    gmask = np.full((2 * gpad, 2 * gpad), BLANK, np.float32)
    gmask[:glen] = 0.0
    gmask[gpad : gpad + glen] = 0.0
    lmask = jnp.asarray(lmask)
    gmask = jnp.asarray(gmask)

    def front(
        n_r, v_r, m_r, x_r, dyl_h, xg_h, xo_h, dg_h, gm_h, w_h, wo_h, u_h, d_h,
        x_h, h_h, qkv_h, p_h, qkvg_o, pg_o, o_o, x1_o, h2_o, dy_o, led_o, wo_o, u_o, d_o,
        x_s, dyl_r, h_o, qkv_o, p_o, w, xs, gs, ds, xg_r, xo_r, dg_r, gm_r, acc, sems,
    ):
        def vec(i):
            return v_r[i : i + 1, :]

        cols = [slice(k * D, (k + 1) * D) for k in range(3)]
        loads_w = copies(*[(w_h.at[:, c], w.at[:, c], sems.at[k]) for k, c in enumerate(cols)])
        loads_g = copies(
            (xg_h, xg_r, sems.at[3]), (xo_h, xo_r, sems.at[4]), (dg_h, dg_r, sems.at[5]), (gm_h, gm_r, sems.at[6])
        )
        loads_next = copies(
            (wo_h, wo_o, sems.at[7]), (u_h.at[:, 0:D], u_o, sems.at[8]), (d_h.at[0:D, :], d_o, sems.at[9])
        )
        out_x = copies((x_s, x_h, sems.at[10]))
        load_dy = copies((dyl_h, dyl_r, sems.at[11]))
        start(load_dy + loads_w + loads_g + loads_next)
        xs[...] = jnp.zeros_like(xs)
        acc[...] = jnp.zeros_like(acc)

        def padded(ref, i):
            for j in range(4):
                xs[j * lpad : j * lpad + llen, :] = ref[4 * i + j].astype(f32)
            return xs[...]

        def out_part(i):
            n = units * pair
            rows = pl.ds(pl.multiple_of(i * n, n), n)
            these = pl.ds(i * units * pairs, units * pairs)
            return copies(
                (qkv_o.at[rows], qkv_h.at[rows], sems.at[13 + 2 * i]),
                (p_o.at[these], p_h.at[these], sems.at[14 + 2 * i]),
            )


        def norm_step(i, carry):
            rows = pl.ds(pl.multiple_of(i * SR, SR), SR)
            x = padded(x_r, i)
            x_s[rows, :] = x.astype(bf16)
            n, _ = normal(x)
            h_o[rows, :] = (n * vec(G1) + vec(C1)).astype(bf16)
            return carry

        def dy_step(i, carry):
            rows = pl.ds(pl.multiple_of(i * SR, SR), SR)
            at = i * SR + lax.broadcasted_iota(jnp.int32, (SR, 1), 0)
            dy = jnp.where(at < n_r[0] * lpad, padded(dyl_r, i), 0.0)
            dy_o[rows, :] = dy.astype(bf16)
            acc[...] += fold(dy)
            return carry

        lax.fori_loop(0, LR // SR, norm_step, 0)
        start(out_x)
        finish(load_dy)
        lax.fori_loop(0, LR // SR, dy_step, 0)
        finish(loads_g + loads_w + loads_next)
        ds[...] = jnp.zeros_like(ds)
        ds[0:glen, :] = dg_r[...].astype(f32)
        dy_o[LR:R, :] = ds[...].astype(bf16)
        acc[...] += fold(ds[...])
        gs[...] = jnp.zeros_like(gs)
        gs[0:glen, :] = xg_r[...].astype(f32)
        gs[gpad : gpad + glen, :] = xo_r[...].astype(f32)
        n, _ = normal(gs[...])
        hg = (n * vec(G1) + vec(C1)).astype(bf16)
        h_o[LR:, :] = hg
        out_h = copies((h_o, h_h, sems.at[12]))
        start(out_h)
        for k, c in enumerate(cols):
            t = nn(h_o[...], w[:, c])
            if k != 1:
                t = t + vec(QB if k == 0 else VB)
            t = t.astype(bf16)
            if k == 0:
                t = t * jnp.asarray(0.125, bf16)
            qkv_o[:, c] = t[0:LR]
            qkvg_o[:, c] = t[LR:]
        masks = head_masks()

        def attn_step(i, carry):
            where, loads = [], []
            for u in range(units):
                g = i * units + u
                rows = pl.ds(pl.multiple_of(g * pair, pair), pair)
                for t in range(pairs):
                    a = 128 * t
                    where.append((g * pairs + t, rows, slice(a, a + 128)))
                    loads.append([lambda rows=rows, b=k * D + a: qkv_o[rows, b : b + 128] for k in range(3)])
            for (at, rows, lanes), (pt, o) in zip(where, attend(loads, m_r[...], masks)):
                p_o[at] = pt
                o_o[rows, lanes] = o.astype(bf16)
            start(out_part(i))
            return carry

        lax.fori_loop(0, laps, attn_step, 0)
        loads = []
        for t in range(pairs):
            a, b, c = (slice(k * D + 128 * t, k * D + 128 * t + 128) for k in range(3))
            loads.append(
                [lambda a=a: qkvg_o[0:gpad, a], lambda b=b: qkvg_o[:, b], lambda c=c: qkvg_o[:, c]]
            )
        for t, (p, o) in enumerate(attend(loads, gm_r[...], masks)):
            pg_o[t] = p
            o_o[LR:R, 128 * t : 128 * t + 128] = o.astype(bf16)
        finish(out_h + out_x)
        for i in range(laps):
            finish(out_part(i))
        x1_o[0:LR, :] = x_s[...].astype(f32)
        x1_o[LR:R, :] = gs[0:gpad, :]
        for r in row_cuts:
            x1 = nn(o_o[r, :], wo_o[...]) + vec(OB) + x1_o[r, :]
            x1_o[r, :] = x1
            n2, _ = normal(x1)
            h2_o[r, :] = (n2 * vec(G2) + vec(C2)).astype(bf16)
        led_o[...] = jnp.zeros_like(led_o)
        led_o[7:8, :] = jnp.sum(acc[...], axis=0, keepdims=True)

    RX = R + gpad
    attn_kept = [((RX, D), bf16), ((LR, 3 * D), bf16), ((slots // 2 * pairs, pair, 2 * pair), bf16)]
    x_far, h, qkv_l, p_l, qkv_g, p_g, o, x1, h2, dy, ledger, wo, wu, wd = call(
        front,
        [
            local_count, vectors, lmask, local_tokens, local_cotan, xg, xg_other, global_cotan.reshape(glen, D), gmask,
            qkv_weight, out_weight, up_weight, down_weight,
        ],
        [((LR, D), bf16)]
        + attn_kept
        + [
            ((2 * gpad, 3 * D), bf16), ((pairs, 2 * gpad, 2 * gpad), bf16), ((R, D), bf16),
            ((R, D), f32), ((R, D), bf16), ((R, D), bf16), ((16, D), f32),
            ((D, D), bf16), ((D, D), bf16), ((D, D), bf16),
        ],
        0,
        scratch=[pltpu.VMEM((LR, D), bf16), pltpu.VMEM((slots, llen, D), bf16), pltpu.VMEM((RX, D), bf16)]
        + [pltpu.VMEM(s, d) for s, d in attn_kept[1:]]
        + [
            pltpu.VMEM((D, 3 * D), bf16), pltpu.VMEM((SR, D), f32), pltpu.VMEM((2 * gpad, D), f32),
            pltpu.VMEM((gpad, D), f32),
            pltpu.VMEM((glen, D), bf16), pltpu.VMEM((glen, D), bf16), pltpu.VMEM((glen, D), bf16),
            pltpu.VMEM((2 * gpad, 2 * gpad), f32), pltpu.VMEM((8, D), f32), pltpu.SemaphoreType.DMA((13 + 2 * laps,)),
        ],
        smem=1,
        far=9,
        far_out=4,
        vmem=27,
    )

    def place_of(pos_r, i):
        at = pos_r[i]
        mine = at < 16 * CHUNK
        return mine, pl.ds(pl.multiple_of(jnp.where(mine, at, at - 16 * CHUNK), 16), CHUNK)

    def put(keep_o, send_o, pos_r, half, value):
        for j in range(0, 16, 2):
            mine, here = place_of(pos_r, half * 16 + j)
            x, y = (value[(j + k) * CHUNK : (j + k + 1) * CHUNK, :] for k in range(2))
            keep_o[here, :] = jnp.where(mine, x, y)
            send_o[here, :] = jnp.where(mine, y, x)

    def mlp(f, state, wait):
        first, last = f == 0, f == nf - 1
        there = slice((f + 1) * D, (f + 2) * D)

        def kernel(pos_r, h_r, d_r, v_r, u_r, w_r, side_r, led_r, u_h, w_h, a_h, *rest):
            if first:
                side_h, *rest = rest
            keep_o, send_o, led_o, dh_o, *rest = rest
            if not last:
                u_o, w_o, *rest = rest
            a_o, du_r, sems = rest
            moves = []
            if not last:
                moves = copies((u_h.at[:, there], u_o, sems.at[0]), (w_h.at[there, :], w_o, sems.at[1]))
            if first:
                moves += copies((side_r, side_h, sems.at[2]))
            (store,) = copies((a_o, a_h, sems.at[3]))
            start(moves)
            acc = jnp.zeros((8, D), f32)
            for i, rows in enumerate(row_cuts):
                u = nn(h_r[rows, :], u_r[...]) + v_r[UB + f : UB + f + 1, :]
                da = nt(d_r[rows, :], w_r[...])
                cdf = 0.5 + 0.5 * lax.erf(u * math.sqrt(0.5))
                a_o[rows, :] = (u * cdf).astype(bf16)
                slope = cdf + u * (jnp.exp(u * u * -0.5) * (1.0 / math.sqrt(2 * math.pi)))
                du = (da * slope).astype(bf16)
                du_r[rows, :] = du
                acc = acc + fold(du.astype(f32))
                if i == cuts - 2:
                    finish(moves)
            store.start()
            led_o[...] = led_r[...]
            led_o[8 + f : 9 + f, :] = jnp.sum(acc, axis=0, keepdims=True)
            put(keep_o, send_o, pos_r, 0, tn(a_o[...], d_r[...]).astype(bf16))
            put(keep_o, send_o, pos_r, 1, tn(h_r[...], du_r[...]).astype(bf16))
            for rows in row_cuts:
                dh = nt(du_r[rows, :], u_r[...])
                dh_o[rows, :] = dh if first else side_r[rows, :] + dh
            store.wait()

        u_w, d_w, side = state
        nonlocal ledger
        a, *out = call(
            kernel,
            [PLACES[f % 2], h2, dy, vectors, u_w, d_w, side, ledger, up_weight, down_weight],
            [((R, D), bf16)]
            + ([((R, D), f32)] if first else [])
            + [((D, D), bf16), ((D, D), bf16), ((16, D), f32), ((R, D), f32)]
            + ([] if last else [((D, D), bf16), ((D, D), bf16)]),
            0,
            scratch=[pltpu.VMEM((R, D), bf16), pltpu.VMEM((R, D), bf16), pltpu.SemaphoreType.DMA((4,))],
            far_out=2 if first else 1,
            smem=1,
            far=2,
            aliases={} if first else {6: 4},
            vmem=9,
            wait=wait,
        )
        if first:
            kept.append(out.pop(0))
        keep, send, ledger, dh, *state = out
        acts.append(a)
        return (keep, send), (*state, dh)

    def second_back(wait):
        def kernel(
            dy_r, dh_r, v_r, o_r, wo_r, q_r, p_r, led_r, x1_h, dx_h, do_o, wg_o, led_o, dq_o, own_o, other_o, acc, x1_r, dx_o, sems
        ):
            loads = copies(*[(x1_h.at[r], x1_r.at[r], sems.at[i]) for i, r in enumerate(row_cuts)])
            stores = copies((dx_o, dx_h, sems.at[cuts]))
            start(loads)
            for k in range(3):
                acc[k] = jnp.zeros((8, D), f32)
            for t, r in zip(loads, row_cuts):
                t.wait()
                dh = dh_r[r, :]
                n, rs = normal(x1_r[r, :])
                dx = dy_r[r, :].astype(f32) + norm_back(n, rs, dh, v_r[G2 : G2 + 1, :])
                dx_o[r, :] = dx
                g = dx.astype(bf16)
                do_o[r, :] = g
                acc[0] += fold(dh * n)
                acc[1] += fold(dh)
                acc[2] += fold(g.astype(f32))
            start(stores)
            wg_o[...] = tn(o_r[...], do_o[...]).astype(bf16)
            do_o[...] = nt(do_o[...], wo_r[...]).astype(bf16)
            led_o[...] = led_r[...]
            for k, i in enumerate((5, 6, 4)):
                led_o[i : i + 1, :] = jnp.sum(acc[k], axis=0, keepdims=True)
            loads = []
            for t in range(pairs):
                a, b, c = (slice(k * D + 128 * t, k * D + 128 * t + 128) for k in range(3))
                loads.append(
                    [
                        lambda a=a: q_r[0:gpad, a],
                        lambda b=b: q_r[:, b],
                        lambda c=c: q_r[:, c],
                        lambda t=t: p_r[t],
                        lambda a=a: do_o[LR:R, a],
                    ]
                )

            def store(t, dq, dk, dv):
                a, b = (slice(k * D + 128 * t, k * D + 128 * t + 128) for k in range(2))
                dq_o[:, a] = dq
                own_o[:, a] = dk[0:gpad].astype(bf16)
                own_o[:, b] = dv[0:gpad]
                other_o[:, a] = dk[gpad:].astype(bf16)
                other_o[:, b] = dv[gpad:]

            finish(stores)
            attend_back(loads, store, head_masks())

        return call(
            kernel,
            [dy, dh2, vectors, o, wo, qkv_g, p_g, ledger, x1],
            [
                ((R, D), f32), ((R, D), bf16), ((D, D), bf16), ((16, D), f32),
                ((gpad, D), bf16), ((gpad, 2 * D), bf16), ((gpad, 2 * D), bf16),
            ],
            0,
            scratch=[
                pltpu.VMEM((3, 8, D), f32), pltpu.VMEM((R, D), f32), pltpu.VMEM((R, D), f32),
                pltpu.SemaphoreType.DMA((cuts + 1,)),
            ],
            far=1,
            far_out=1,
            vmem=14,
            wait=wait,
        )

    def local_back(wait):
        def kernel(d_r, q_h, p_h, w_h, h_h, o_r, w_o, h_o, q_s, p_s, sems):
            def load(i):
                n = units * pair
                rows = pl.ds(pl.multiple_of(i * n, n), n)
                these = pl.ds(i * units * pairs, units * pairs)
                return copies(
                    (q_h.at[rows], q_s.at[rows], sems.at[2 * i]), (p_h.at[these], p_s.at[these], sems.at[2 * i + 1])
                )

            more = copies((w_h, w_o, sems.at[2 * laps]), (h_h, h_o, sems.at[2 * laps + 1]))
            for i in range(laps):
                start(load(i))
            start(more)
            masks = head_masks()

            def attn_step(i, carry):
                finish(load(i))
                where, loads = [], []
                for u in range(units):
                    g = i * units + u
                    rows = pl.ds(pl.multiple_of(g * pair, pair), pair)
                    for t in range(pairs):
                        a, b, c = (slice(k * D + 128 * t, k * D + 128 * t + 128) for k in range(3))
                        where.append((rows, a, b, c))
                        loads.append(
                            [lambda rows=rows, x=x: q_s[rows, x] for x in (a, b, c)]
                            + [lambda at=g * pairs + t: p_s[at], lambda rows=rows, a=a: d_r[rows, a]]
                        )

                def store(n, dq, dk, dv):
                    rows, a, b, c = where[n]
                    o_r[rows, a] = dq
                    o_r[rows, b] = dk.astype(bf16)
                    o_r[rows, c] = dv

                attend_back(loads, store, masks)
                return carry

            lax.fori_loop(0, laps - 1, attn_step, 0)
            finish(more)
            attn_step(laps - 1, 0)

        return call(
            kernel,
            [do, qkv_l, p_l, qkv_weight, h],
            [((RX, 3 * D), bf16), ((D, 3 * D), bf16), ((RX, D), bf16)],
            0,
            scratch=[
                pltpu.VMEM((LR, 3 * D), bf16), pltpu.VMEM((slots // 2 * pairs, pair, 2 * pair), bf16),
                pltpu.SemaphoreType.DMA((2 * laps + 2,)),
            ],
            far=4,
            vmem=15,
            wait=wait,
        )

    def qkv_back(wait):
        def kernel(pa_r, pb_r, dqkv_r, h_r, dq_r, own_r, other_r, gout_r, led_r, dqkv_o, ka_o, sa_o, kb_o, sb_o, led_o):
            led_o[...] = led_r[...]
            dqkv_o[LR:R, 0:D] = dq_r[...]
            dqkv_o[LR:R, D:] = own_r[...]
            dqkv_o[R:, 0:D] = jnp.zeros((gpad, D), bf16)
            dqkv_o[R:, D:] = other_r[...]
            put(ka_o, sa_o, pa_r, 0, gout_r[...])
            for k, at in enumerate(((ka_o, sa_o, pa_r, 1), (kb_o, sb_o, pb_r, 0), (kb_o, sb_o, pb_r, 1))):
                cols = slice(k * D, (k + 1) * D)
                put(*at, tn(h_r[...], dqkv_o[:, cols]).astype(bf16))
                if k != 1:
                    s = fold(dqkv_o[:, cols].astype(f32))
                    i = 2 + k // 2
                    led_o[i : i + 1, :] = jnp.sum(s, axis=0, keepdims=True)

        return call(
            kernel,
            [PLACES[0], PLACES[1], dqkv, h_back, dq_g, kv_own, kv_other, g_out, ledger],
            [((RX, 3 * D), bf16)] + [((D, D), bf16)] * 4 + [((16, D), f32)],
            0,
            smem=2,
            vmem=4,
            aliases={2: 0},
            wait=wait,
        )

    def first_back(part, so_far, wait):
        rows = row_halves[part]
        n_rows = rows.stop - rows.start
        stop = min(rows.stop, LR)

        def kernel(v_r, w_r, dqkv_r, led_r, *rest):
            if part:
                kv_r, _, *rest = rest
            x_h, xg_h, dx_h, wd_h, t_o, led_o, *rest = rest
            if not part:
                wd_o, *rest = rest
            dh_s, x_s, acc, xg_s, gs, dx_r, own_s, sems = rest
            moves = copies(
                (x_h.at[rows.start : stop], x_s.at[0 : stop - rows.start], sems.at[0]), (dx_h.at[rows], dx_r, sems.at[2])
            )
            if part:
                moves += copies((xg_h, xg_s, sems.at[1]))
            else:
                moves += copies((wd_h, wd_o, sems.at[1]))
            start(moves)
            dh_s[0 : stop - rows.start, :] = nt(dqkv_r[rows.start : stop, :], w_r[...])
            if part:
                own_s[:, 0:D] = dqkv_r[LR:R, 0:D]
                own_s[:, D:] = (dqkv_r[LR:R, D:].astype(f32) + kv_r[...].astype(f32)).astype(bf16)
                dh_s[stop - rows.start :, :] = nt(own_s[...], w_r[...])
            acc[...] = jnp.zeros_like(acc)
            finish(moves)
            if part:
                gs[...] = jnp.zeros_like(gs)
                gs[0:glen, :] = xg_s[...].astype(f32)
                x_s[stop - rows.start :, :] = gs[...].astype(bf16)

            def step(i, carry):
                here = pl.ds(pl.multiple_of(i * 48, 16), 48)
                there = pl.ds(pl.multiple_of(rows.start + i * 48, 16), 48)
                n, r = normal(x_s[here, :].astype(f32))
                dh = dh_s[here, :]
                t = dx_r[here, :] + norm_back(n, r, dh, v_r[G1 : G1 + 1, :])
                t_o[there, :] = t.astype(bf16)
                acc[0] += fold(dh * n)
                acc[1] += fold(dh)
                return carry

            lax.fori_loop(0, n_rows // 48, step, 0, unroll=True)
            led_o[...] = led_r[...]
            for k in range(2):
                led_o[k : k + 1, :] = led_r[k : k + 1, :] + jnp.sum(acc[k], axis=0, keepdims=True)

        return call(
            kernel,
            [vectors, wqkv, dqkv, ledger] + ([kv_back, so_far] if part else []) + [x_far, xg, dx1, down_weight],
            [((R, D), bf16), ((16, D), f32)] + ([] if part else [((F, D), bf16)]),
            0,
            scratch=[
                pltpu.VMEM((n_rows, D), f32), pltpu.VMEM((n_rows, D), bf16), pltpu.VMEM((2, 8, D), f32),
                pltpu.VMEM((glen, D), bf16), pltpu.VMEM((gpad, D), f32), pltpu.VMEM((n_rows, D), f32),
                pltpu.VMEM((gpad, 3 * D), bf16), pltpu.SemaphoreType.DMA((3,)),
            ],
            far=4,
            vmem=10,
            aliases={5: 0} if part else {},
            wait=wait,
        )

    def output(part, so_far, wait):
        rows = row_halves[part]
        n_rows = rows.stop - rows.start

        def kernel(v_r, w_r, *rest):
            if part:
                _, *rest = rest
            x1_h, *rest = rest
            a_hs, (y_o, a_r, x1_r, sems) = rest[:nf], rest[nf:]
            loads = copies(
                *[(a_hs[f].at[rows], a_r.at[f], sems.at[f]) for f in range(nf)], (x1_h.at[rows], x1_r, sems.at[nf])
            )
            start(loads)
            loads[0].wait()
            y = nn(a_r[0], w_r[0:D, :])
            finish(loads[1:])
            y = y + x1_r[...] + v_r[DB : DB + 1, :]
            for f in range(1, nf):
                y = y + nn(a_r[f], w_r[f * D : (f + 1) * D, :])
            y_o[rows, :] = y.astype(bf16)

        return call(
            kernel,
            [vectors, wd_all] + ([so_far] if part else []) + [x1, *acts],
            [((R, D), bf16)],
            0,
            scratch=[
                pltpu.VMEM((nf, n_rows, D), bf16), pltpu.VMEM((n_rows, D), f32), pltpu.SemaphoreType.DMA((nf + 1,)),
            ],
            far=1 + nf,
            vmem=11,
            aliases={2: 0} if part else {},
            wait=wait,
        )[0]

    def add(a, b):
        return (a.astype(f32) + b.astype(f32)).astype(bf16)

    class Flow:
        def __init__(self, steps):
            self.steps = steps
            self.sends = next(steps)
            self.result = self.got = None

        def launch(self):
            self.got = [swap(v, b) for v, b in self.sends]

        def land(self):
            got, self.got = self.got, None
            try:
                self.sends = self.steps.send(got)
            except StopIteration as end:
                self.result = end.value

    def halves(v):
        h = v.shape[0] // 2
        return v[:h], v[h:]

    def join(*parts):
        return jnp.concatenate(parts, axis=0)

    def sum_two(a, b):
        for bits in (("c", "c"), ("x", "y"), ("y", "x")):
            if bits[0] == "c":
                (a, sa), (b, sb) = a, b
            else:
                (a, sa), (b, sb) = halves(a), halves(b)
            ga, gb = yield [(sa, bits[0]), (sb, bits[1])]
            a, b = add(a, ga), add(b, gb)
        for bit in ("z0", "z1"):
            (a, sa), (b, sb) = halves(a), halves(b)
            (got,) = yield [(join(sa, sb), bit)]
            ga, gb = halves(got)
            a, b = add(a, ga), add(b, gb)
        m = 16
        while m < ndp:
            v = join(a, b)
            (got,) = yield [(v, m)]
            a, b = halves(add(v, got))
            m *= 2
        for bit in ("z1", "z0"):
            (got,) = yield [(join(a, b), bit)]
            ga, gb = halves(got)
            a, b = join(a, ga), join(b, gb)
        for bits in (("y", "x"), ("x", "y"), ("c", "c")):
            ga, gb = yield [(a, bits[0]), (b, bits[1])]
            if bits[0] != "c":
                a, b = join(a, ga), join(b, gb)
        return [a, ga, b, gb]

    def send_once(v, bit):
        (got,) = yield [(v, bit)]
        return got

    def sum_small(v):
        more, m = [], 16
        while m < ndp:
            more.append(m)
            m *= 2
        for bit in (*more, "z1", "c", "z0", "y", "x"):
            v = v.astype(bf16)
            (got,) = yield [(v, bit)]
            v = v.astype(f32) + got.astype(f32)
        return v

    def place(blocks, places, sums, outs, wait=()):
        made = [not isinstance(t, tuple) for t in outs]
        shapes = [t.shape if m else t for t, m in zip(outs, made)]

        def kernel(*refs):
            pos_rs, refs = refs[: len(places)], refs[len(places) :]
            sums_r, refs = refs[: len(sums)], refs[len(sums) + sum(made) :]
            outs_h, (work, sems) = refs[: len(outs)], refs[len(outs) :]
            moves = []
            for n, (which, where, side, half) in enumerate(blocks):
                pos_r, own_r, got_r = pos_rs[side], sums_r[2 * side], sums_r[2 * side + 1]
                if n >= 2:
                    moves[n - 2].wait()
                for j in range(0, 16, 2):
                    mine, here = place_of(pos_r, half * 16 + j)
                    x, y = own_r[here, :].astype(f32), got_r[here, :].astype(f32)
                    work[n % 2, j * CHUNK : (j + 1) * CHUNK, :] = jnp.where(mine, x, y)
                    work[n % 2, (j + 1) * CHUNK : (j + 2) * CHUNK, :] = jnp.where(mine, y, x)
                r, c = (slice(i * D, (i + 1) * D) for i in where)
                moves += copies((work.at[n % 2], outs_h[which].at[r, c], sems.at[n]))
                moves[n].start()
            for t in moves[-2:]:
                t.wait()

        before = [t for t, m in zip(outs, made) if m]
        return call(
            kernel,
            places + sums + before,
            [(s, f32) for s in shapes],
            0,
            scratch=[pltpu.VMEM((2, D, D), f32), pltpu.SemaphoreType.DMA((len(blocks),))],
            vmem=7,
            smem=len(places),
            far=len(before),
            far_out=len(outs),
            aliases={len(places + sums) + i: j for i, j in enumerate(j for j, m in enumerate(made) if m)},
            wait=wait,
        )

    waits = []

    def run(kernel, *flows, hold=()):
        flows = [flow for flow in flows if flow.result is None]
        for flow in (*flows, *hold):
            if flow.got is None:
                flow.launch()
        sends = [v for flow in flows for v, _ in flow.sends]
        out = kernel(waits + sends) if kernel else None
        if kernel and flows:
            out, got = lax.optimization_barrier((out, [flow.got for flow in flows]))
            for flow, t in zip(flows, got):
                flow.got = t
        waits[:] = [t for flow in flows for t in flow.got]
        for flow in flows:
            flow.land()
        return out

    acts, blocks, kept = [], [], []
    state = (wu, wd, x1)

    def hidden(f, *flows):
        nonlocal state
        block, state = run(lambda wait: mlp(f, state, wait), *flows)
        blocks.append(block)

    hidden(0)
    (x1,) = kept
    hidden(1)
    one = Flow(sum_two(*blocks[0:2]))
    hidden(2, one)
    hidden(3, one)
    (dh2,) = state
    two = Flow(sum_two(*blocks[2:4]))
    dx1, do, g_out, ledger, dq_g, kv_own, kv_other = run(second_back, one, two)
    dqkv, wqkv, h_back = run(local_back, one, two)
    dqkv, ka, sa, kb, sb, ledger = run(qkv_back, one, two)

    three = Flow(sum_two((ka, sa), (kb, sb)))
    nothing = lambda wait: ()

    def place_pair(k, flow, outs, wait):
        blocks = [(i, (0, f) if i == 0 else (f, 0), f % 2, 1 - i) for f in (2 * k, 2 * k + 1) for i in (1, 0)]
        return place(blocks, PLACES, flow.result, outs, wait)

    run(nothing, three)
    grad, ledger, wd_all = run(lambda wait: first_back(0, None, wait), three, one, two)
    kv = Flow(send_once(lax.optimization_barrier((kv_other, three.sends[0][0]))[0], "y"))
    run(nothing, three, one, two, kv)
    kv_back = kv.result
    grad, ledger = run(lambda wait: first_back(1, grad, wait), three, one, two)
    four = Flow(sum_small(ledger))
    run(nothing, three, one, two, four)
    y = run(lambda wait: output(0, None, wait), three, two, four)
    y = run(lambda wait: output(1, y, wait), three, one, two, four)
    local_grad = run(lambda wait: lax.optimization_barrier(unpad(grad)), three, two, four)
    while one.result is None:
        run(nothing, three, one, two, four)
    local_out, up_down = run(
        lambda wait: (
            lax.optimization_barrier(jnp.where(live, unpad(y), 0)),
            place_pair(0, one, [(D, F), (F, D)], wait),
        ),
        three,
        four,
    )
    while four.result is None or two.result is None:
        run(nothing, three, two, four)
    total = four.result

    def last_rows(wait):
        pieces = [t[LR : LR + glen].reshape(1, glen, D) for t in (y, grad)]
        pieces += [total[i] for i in range(8)] + [total[8 : 8 + nf].reshape(-1)]
        return lax.optimization_barrier(tuple(pieces)), place_pair(1, two, up_down, wait)

    pieces, (up_grad, down_grad) = run(last_rows, three)
    global_out, global_grad, *total = pieces
    while three.result is None:
        run(None, three)
    attn_sums = three.result
    out_grad, qkv_grad = place(
        [(0, (0, 0), 0, 0), (1, (0, 0), 0, 1), (1, (0, 1), 1, 0), (1, (0, 2), 1, 1)],
        PLACES,
        attn_sums,
        [(D, D), (D, 3 * D)],
    )

    return (
        global_out,
        local_out,
        global_grad,
        local_grad,
        total[0],
        total[1],
        qkv_grad,
        total[2],
        total[3],
        out_grad,
        total[4],
        total[5],
        total[6],
        up_grad,
        total[8],
        down_grad,
        total[7],
    )


def solution(mesh):
    tokens = (P("dp", "blk", None), P(("blk", "dp"), None, None))
    return jax.shard_map(
        per_device,
        mesh=mesh,
        in_specs=(*tokens, P(("blk", "dp")), *([P()] * 13), *tokens),
        out_specs=(*tokens, *tokens, *([P()] * 13)),
        check_vma=False,
    )
```

```python
import math

import jax
import jax.numpy as jnp
import numpy as np
from jax import lax
from jax.experimental import pallas as pl
from jax.experimental.pallas import tpu as pltpu
from jax.sharding import PartitionSpec as P

HEADS = 12
EPS = 1e-06
bf16 = jnp.bfloat16
f32 = jnp.float32
CHUNK = 48
BLANK = -1e30


def nn(a, b):
    return lax.dot_general(a, b, (((1,), (0,)), ((), ())), preferred_element_type=f32)


def nt(a, b):
    return lax.dot_general(a, b, (((1,), (1,)), ((), ())), preferred_element_type=f32)


def tn(a, b):
    return lax.dot_general(a, b, (((0,), (0,)), ((), ())), preferred_element_type=f32)


def normal(x):
    center = x - jnp.mean(x, axis=-1, keepdims=True)
    r = lax.rsqrt(jnp.mean(center * center, axis=-1, keepdims=True) + EPS)
    return center * r, r


def norm_back(n, r, dh, gain):
    e = dh * gain
    return r * (e - jnp.mean(e, axis=-1, keepdims=True) - n * jnp.mean(e * n, axis=-1, keepdims=True))


def fold(x):
    return jnp.sum(x.reshape(x.shape[0] // 8, 8, x.shape[1]), axis=0)


def head_masks():
    lane = lax.broadcasted_iota(jnp.int32, (1, 128), 1)
    return [(lane < 64).astype(f32).astype(bf16), (lane >= 64).astype(f32).astype(bf16)]


def stack_heads(t, masks):
    return jnp.concatenate([t * m for m in masks], axis=0)


def pick_heads(t):
    n = t.shape[0] // 2
    low = lax.broadcasted_iota(jnp.int32, (n, 128), 1) < 64
    return jnp.where(low, t[:n], t[n:])


def attend(loads, mask, masks):
    scores = [nt(k(), stack_heads(q(), masks)) + mask for q, k, _ in loads]
    chances = []
    for s in scores:
        p = jnp.exp(s - jnp.max(s, axis=0, keepdims=True))
        chances.append((p * (1.0 / jnp.sum(p, axis=0, keepdims=True))).astype(bf16))
    return [(p, pick_heads(tn(p, v()))) for p, (_, _, v) in zip(chances, loads)]


def attend_back(loads, store, masks):
    outer = [stack_heads(do(), masks) for _, _, _, _, do in loads]
    dps = [nt(v(), d) for d, (_, _, v, _, _) in zip(outer, loads)]
    dvs = [nn(p(), d).astype(bf16) for d, (_, _, _, p, _) in zip(outer, loads)]
    dss = []
    for dp, (_, _, _, p, _) in zip(dps, loads):
        pf = p().astype(f32)
        dss.append((pf * (dp - jnp.sum(pf * dp, axis=0, keepdims=True))).astype(bf16))
    for i, (ds, dv, (q, k, _, _, _)) in enumerate(zip(dss, dvs, loads)):
        dk = nn(ds, stack_heads(q(), masks))
        dq = pick_heads(tn(ds, k())) * 0.125
        store(i, dq.astype(bf16), dk, dv)


def call(kernel, ins, outs, flops, scratch=(), vmem=16, smem=0, far=0, far_out=0, aliases=None, wait=()):
    ins = list(ins)
    if wait:
        ins, _ = lax.optimization_barrier((ins, list(wait)))
    whole = pl.BlockSpec(memory_space=pltpu.VMEM)
    scalars = pl.BlockSpec(memory_space=pltpu.SMEM)
    lying = pl.BlockSpec(memory_space=pltpu.HBM)
    near = len(ins) - far

    def nbytes(s, d):
        return math.prod(s) * jnp.dtype(d).itemsize

    def pinned(i, t):
        if i >= near:
            return pltpu.with_memory_space_constraint(t, pltpu.HBM)
        if i >= smem and nbytes(t.shape, t.dtype) > 2**16:
            return pltpu.with_memory_space_constraint(t, pltpu.VMEM)
        return t

    def result(i, s, d):
        if i < far_out:
            return pltpu.HBM(s, d)
        if nbytes(s, d) > 2**16:
            return pltpu.VMEM(s, d)
        return jax.ShapeDtypeStruct(s, d)

    size = sum(nbytes(t.shape, t.dtype) for t in ins) + sum(nbytes(s, d) for s, d in outs)
    return pl.pallas_call(
        kernel,
        in_specs=[scalars] * smem + [whole] * (near - smem) + [lying] * far,
        out_specs=[lying] * far_out + [whole] * (len(outs) - far_out),
        out_shape=[result(i, s, d) for i, (s, d) in enumerate(outs)],
        scratch_shapes=list(scratch),
        input_output_aliases=aliases or {},
        compiler_params=pltpu.CompilerParams(vmem_limit_bytes=vmem * 2**20),
        cost_estimate=pl.CostEstimate(flops=1, bytes_accessed=1, transcendentals=0),
    )(*[pinned(i, t) for i, t in enumerate(ins)])


def per_device(
    global_tokens,
    local_tokens,
    local_count,
    first_gain,
    first_shift,
    qkv_weight,
    query_bias,
    value_bias,
    out_weight,
    out_bias,
    second_gain,
    second_shift,
    up_weight,
    up_bias,
    down_weight,
    mlp_down_bias,
    global_cotan,
    local_cotan,
):
    crops, glen, D = global_tokens.shape
    slots, llen, _ = local_tokens.shape
    F = up_weight.shape[1]
    nf = F // D
    lpad = -(-llen // 8) * 8
    gpad = -(-glen // 16) * 16
    assert crops == 1 and D == 768 and lpad * 2 % 16 == 0 and nf % 2 == 0
    LR = slots * lpad
    R = LR + gpad
    pair = 2 * lpad
    pairs = D // 128
    units = 4
    laps = slots // 2 // units
    assert laps * units * 2 == slots and slots % 8 == 0
    nblk, ndp = lax.axis_size("blk"), lax.axis_size("dp")
    blk, dp = lax.axis_index("blk"), lax.axis_index("dp")
    assert nblk == 2 and ndp % 16 == 0
    per_step = 8
    SR = per_step * lpad
    cuts = 3 if R % 48 == 0 else 1
    row_cuts = [slice(i * (R // cuts), (i + 1) * (R // cuts)) for i in range(cuts)]
    half_at = R // 96 * 48
    assert R % 48 == 0
    row_halves = [slice(0, half_at), slice(half_at, R)]

    bit_of = {"c": 0, "x": 1, "z0": 2, "z1": 3, "y": 4}

    def swap(v, b):
        if b == "y":
            return lax.ppermute(v, "blk", [(0, 1), (1, 0)])
        m = b if isinstance(b, int) else 1 << bit_of[b]
        return lax.ppermute(v, "dp", [(i, i ^ m) for i in range(ndp)])

    me = (dp & 15) + 16 * blk
    relative = jnp.arange(32, dtype=jnp.int32) ^ me.astype(jnp.int32)

    def places(order):
        pos = jnp.zeros_like(relative)
        for b in order:
            pos = 2 * pos + ((relative >> bit_of[b]) & 1)
        return pos * CHUNK

    ORDERS = (("c", "x", "y", "z0", "z1"), ("c", "y", "x", "z0", "z1"))
    PLACES = [places(o) for o in ORDERS]

    def copies(*triples):
        return [pltpu.make_async_copy(src, dst, sem) for src, dst, sem in triples]

    def start(moves):
        for t in moves:
            t.start()

    def finish(moves):
        for t in moves:
            t.wait()

    xg = global_tokens.reshape(glen, D)
    xg_other = swap(xg, "y")
    live = (jnp.arange(slots, dtype=jnp.int32) < local_count[0])[:, None, None]

    def unpad(t):
        return t[:LR].reshape(slots, lpad, D)[:, :llen]

    singles = [first_gain, first_shift, query_bias, value_bias, out_bias, second_gain, second_shift, mlp_down_bias, up_bias]
    *singles, xg_other = lax.optimization_barrier((*singles, xg_other))
    vectors = jnp.concatenate([t.reshape(-1, D) for t in singles], axis=0)
    G1, C1, QB, VB, OB, G2, C2, DB, UB = range(9)

    assert 8 + nf <= 16
    lmask = np.full((pair, 2 * pair), BLANK, np.float32)
    for r in range(2 * pair):
        t = (r % pair) // lpad * lpad
        lmask[t : t + llen, r] = 0.0
    gmask = np.full((2 * gpad, 2 * gpad), BLANK, np.float32)
    gmask[:glen] = 0.0
    gmask[gpad : gpad + glen] = 0.0
    lmask = jnp.asarray(lmask)
    gmask = jnp.asarray(gmask)

    def front(
        n_r, v_r, m_r, x_r, dyl_h, xg_h, xo_h, dg_h, gm_h, w_h, wo_h, u_h, d_h,
        x_h, h_h, qkv_h, p_h, qkvg_o, pg_o, o_o, x1_o, h2_o, dy_o, led_o, wo_o, u_o, d_o,
        x_s, dyl_r, h_o, qkv_o, p_o, w, xs, gs, ds, xg_r, xo_r, dg_r, gm_r, acc, sems,
    ):
        def vec(i):
            return v_r[i : i + 1, :]

        cols = [slice(k * D, (k + 1) * D) for k in range(3)]
        loads_w = copies(*[(w_h.at[:, c], w.at[:, c], sems.at[k]) for k, c in enumerate(cols)])
        loads_g = copies(
            (xg_h, xg_r, sems.at[3]), (xo_h, xo_r, sems.at[4]), (dg_h, dg_r, sems.at[5]), (gm_h, gm_r, sems.at[6])
        )
        loads_next = copies(
            (wo_h, wo_o, sems.at[7]), (u_h.at[:, 0:D], u_o, sems.at[8]), (d_h.at[0:D, :], d_o, sems.at[9])
        )
        out_x = copies((x_s, x_h, sems.at[10]))
        load_dy = copies((dyl_h, dyl_r, sems.at[11]))
        start(load_dy + loads_w + loads_g + loads_next)
        xs[...] = jnp.zeros_like(xs)
        acc[...] = jnp.zeros_like(acc)

        def padded(ref, i):
            for j in range(per_step):
                xs[j * lpad : j * lpad + llen, :] = ref[per_step * i + j].astype(f32)
            return xs[...]

        def out_part(i):
            n = units * pair
            rows = pl.ds(pl.multiple_of(i * n, n), n)
            these = pl.ds(i * units * pairs, units * pairs)
            return copies(
                (qkv_o.at[rows], qkv_h.at[rows], sems.at[13 + 2 * i]),
                (p_o.at[these], p_h.at[these], sems.at[14 + 2 * i]),
            )


        def norm_step(i, carry):
            rows = pl.ds(pl.multiple_of(i * SR, SR), SR)
            x = padded(x_r, i)
            x_s[rows, :] = x.astype(bf16)
            n, _ = normal(x)
            h_o[rows, :] = (n * vec(G1) + vec(C1)).astype(bf16)
            return carry

        def dy_step(i, carry):
            rows = pl.ds(pl.multiple_of(i * SR, SR), SR)
            at = i * SR + lax.broadcasted_iota(jnp.int32, (SR, 1), 0)
            dy = jnp.where(at < n_r[0] * lpad, padded(dyl_r, i), 0.0)
            dy_o[rows, :] = dy.astype(bf16)
            acc[...] += fold(dy)
            return carry

        lax.fori_loop(0, LR // SR, norm_step, 0)
        start(out_x)
        finish(load_dy)
        lax.fori_loop(0, LR // SR, dy_step, 0)
        finish(loads_g + loads_w + loads_next)
        ds[...] = jnp.zeros_like(ds)
        ds[0:glen, :] = dg_r[...].astype(f32)
        dy_o[LR:R, :] = ds[...].astype(bf16)
        acc[...] += fold(ds[...])
        gs[...] = jnp.zeros_like(gs)
        gs[0:glen, :] = xg_r[...].astype(f32)
        gs[gpad : gpad + glen, :] = xo_r[...].astype(f32)
        n, _ = normal(gs[...])
        hg = (n * vec(G1) + vec(C1)).astype(bf16)
        h_o[LR:, :] = hg
        out_h = copies((h_o, h_h, sems.at[12]))
        start(out_h)
        for k, c in enumerate(cols):
            t = nn(h_o[...], w[:, c])
            if k != 1:
                t = t + vec(QB if k == 0 else VB)
            t = t.astype(bf16)
            if k == 0:
                t = t * jnp.asarray(0.125, bf16)
            qkv_o[:, c] = t[0:LR]
            qkvg_o[:, c] = t[LR:]
        masks = head_masks()

        def attn_step(i, carry):
            where, loads = [], []
            for u in range(units):
                g = i * units + u
                rows = pl.ds(pl.multiple_of(g * pair, pair), pair)
                for t in range(pairs):
                    a = 128 * t
                    where.append((g * pairs + t, rows, slice(a, a + 128)))
                    loads.append([lambda rows=rows, b=k * D + a: qkv_o[rows, b : b + 128] for k in range(3)])
            for (at, rows, lanes), (pt, o) in zip(where, attend(loads, m_r[...], masks)):
                p_o[at] = pt
                o_o[rows, lanes] = o.astype(bf16)
            start(out_part(i))
            return carry

        lax.fori_loop(0, laps, attn_step, 0)
        loads = []
        for t in range(pairs):
            a, b, c = (slice(k * D + 128 * t, k * D + 128 * t + 128) for k in range(3))
            loads.append(
                [lambda a=a: qkvg_o[0:gpad, a], lambda b=b: qkvg_o[:, b], lambda c=c: qkvg_o[:, c]]
            )
        for t, (p, o) in enumerate(attend(loads, gm_r[...], masks)):
            pg_o[t] = p
            o_o[LR:R, 128 * t : 128 * t + 128] = o.astype(bf16)
        finish(out_h + out_x)
        for i in range(laps):
            finish(out_part(i))
        x1_o[0:LR, :] = x_s[...].astype(f32)
        x1_o[LR:R, :] = gs[0:gpad, :]
        for r in row_cuts:
            x1 = nn(o_o[r, :], wo_o[...]) + vec(OB) + x1_o[r, :]
            x1_o[r, :] = x1
            n2, _ = normal(x1)
            h2_o[r, :] = (n2 * vec(G2) + vec(C2)).astype(bf16)
        led_o[...] = jnp.zeros_like(led_o)
        led_o[7:8, :] = jnp.sum(acc[...], axis=0, keepdims=True)

    RX = R + gpad
    attn_kept = [((RX, D), bf16), ((LR, 3 * D), bf16), ((slots // 2 * pairs, pair, 2 * pair), bf16)]
    x_far, h, qkv_l, p_l, qkv_g, p_g, o, x1, h2, dy, ledger, wo, wu, wd = call(
        front,
        [
            local_count, vectors, lmask, local_tokens, local_cotan, xg, xg_other, global_cotan.reshape(glen, D), gmask,
            qkv_weight, out_weight, up_weight, down_weight,
        ],
        [((LR, D), bf16)]
        + attn_kept
        + [
            ((2 * gpad, 3 * D), bf16), ((pairs, 2 * gpad, 2 * gpad), bf16), ((R, D), bf16),
            ((R, D), f32), ((R, D), bf16), ((R, D), bf16), ((16, D), f32),
            ((D, D), bf16), ((D, D), bf16), ((D, D), bf16),
        ],
        0,
        scratch=[pltpu.VMEM((LR, D), bf16), pltpu.VMEM((slots, llen, D), bf16), pltpu.VMEM((RX, D), bf16)]
        + [pltpu.VMEM(s, d) for s, d in attn_kept[1:]]
        + [
            pltpu.VMEM((D, 3 * D), bf16), pltpu.VMEM((SR, D), f32), pltpu.VMEM((2 * gpad, D), f32),
            pltpu.VMEM((gpad, D), f32),
            pltpu.VMEM((glen, D), bf16), pltpu.VMEM((glen, D), bf16), pltpu.VMEM((glen, D), bf16),
            pltpu.VMEM((2 * gpad, 2 * gpad), f32), pltpu.VMEM((8, D), f32), pltpu.SemaphoreType.DMA((13 + 2 * laps,)),
        ],
        smem=1,
        far=9,
        far_out=4,
        vmem=27,
    )

    def place_of(pos_r, i):
        at = pos_r[i]
        mine = at < 16 * CHUNK
        return mine, pl.ds(pl.multiple_of(jnp.where(mine, at, at - 16 * CHUNK), 16), CHUNK)

    def put(keep_o, send_o, pos_r, half, value):
        for j in range(0, 16, 2):
            mine, here = place_of(pos_r, half * 16 + j)
            x, y = (value[(j + k) * CHUNK : (j + k + 1) * CHUNK, :] for k in range(2))
            keep_o[here, :] = jnp.where(mine, x, y)
            send_o[here, :] = jnp.where(mine, y, x)

    def mlp(f, state, wait):
        first, last = f == 0, f == nf - 1
        there = slice((f + 1) * D, (f + 2) * D)

        def kernel(pos_r, h_r, d_r, v_r, u_r, w_r, side_r, led_r, u_h, w_h, *rest):
            if last:
                x1_h, *rest = rest
            a_h, *rest = rest
            if first:
                side_h, *rest = rest
            keep_o, send_o, led_o, dh_o, *rest = rest
            if last:
                x1_o, *rest = rest
            else:
                u_o, w_o, *rest = rest
            a_o, du_r, sems = rest
            moves = []
            if not last:
                moves = copies((u_h.at[:, there], u_o, sems.at[0]), (w_h.at[there, :], w_o, sems.at[1]))
            if first:
                moves += copies((side_r, side_h, sems.at[2]))
            if last:
                moves += copies((x1_h, x1_o, sems.at[0]))
            (store,) = copies((a_o, a_h, sems.at[3]))
            start(moves)
            acc = jnp.zeros((8, D), f32)
            for i, rows in enumerate(row_cuts):
                u = nn(h_r[rows, :], u_r[...]) + v_r[UB + f : UB + f + 1, :]
                da = nt(d_r[rows, :], w_r[...])
                cdf = 0.5 + 0.5 * lax.erf(u * math.sqrt(0.5))
                a_o[rows, :] = (u * cdf).astype(bf16)
                slope = cdf + u * (jnp.exp(u * u * -0.5) * (1.0 / math.sqrt(2 * math.pi)))
                du = (da * slope).astype(bf16)
                du_r[rows, :] = du
                acc = acc + fold(du.astype(f32))
                if i == cuts - 2:
                    finish(moves)
            store.start()
            led_o[...] = led_r[...]
            led_o[8 + f : 9 + f, :] = jnp.sum(acc, axis=0, keepdims=True)
            put(keep_o, send_o, pos_r, 0, tn(a_o[...], d_r[...]).astype(bf16))
            put(keep_o, send_o, pos_r, 1, tn(h_r[...], du_r[...]).astype(bf16))
            for rows in row_cuts:
                dh = nt(du_r[rows, :], u_r[...])
                dh_o[rows, :] = dh if first else side_r[rows, :] + dh
            store.wait()

        u_w, d_w, side = state
        nonlocal ledger
        a, *out = call(
            kernel,
            [PLACES[f % 2], h2, dy, vectors, u_w, d_w, side, ledger, up_weight, down_weight] + ([x1] if last else []),
            [((R, D), bf16)]
            + ([((R, D), f32)] if first else [])
            + [((D, D), bf16), ((D, D), bf16), ((16, D), f32), ((R, D), f32)]
            + ([((R, D), f32)] if last else [((D, D), bf16), ((D, D), bf16)]),
            0,
            scratch=[pltpu.VMEM((R, D), bf16), pltpu.VMEM((R, D), bf16), pltpu.SemaphoreType.DMA((4,))],
            far_out=2 if first else 1,
            smem=1,
            far=3 if last else 2,
            aliases={} if first else {6: 4},
            vmem=9,
            wait=wait,
        )
        if first:
            kept.append(out.pop(0))
        keep, send, ledger, dh, *state = out
        acts.append(a)
        return (keep, send), (*state, dh)

    def second_back(wait):
        def kernel(dy_r, dh_r, v_r, x1_r, wo_r, led_r, q_h, p_h, dx_o, do_o, g_o, led_o, q_o, p_o, acc, sems):
            first_lap = copies(
                (q_h.at[0 : units * pair], q_o, sems.at[0]), (p_h.at[0 : units * pairs], p_o, sems.at[1])
            )
            start(first_lap)
            for k in range(3):
                acc[k] = jnp.zeros((8, D), f32)
            for r in row_cuts:
                dh = dh_r[r, :]
                n, rs = normal(x1_r[r, :])
                dx = dy_r[r, :].astype(f32) + norm_back(n, rs, dh, v_r[G2 : G2 + 1, :])
                dx_o[r, :] = dx
                g = dx.astype(bf16)
                g_o[r, :] = g
                acc[0] += fold(dh * n)
                acc[1] += fold(dh)
                acc[2] += fold(g.astype(f32))
            finish(first_lap)
            led_o[...] = led_r[...]
            for k, i in enumerate((5, 6, 4)):
                led_o[i : i + 1, :] = jnp.sum(acc[k], axis=0, keepdims=True)
            do_o[...] = nt(g_o[...], wo_r[...]).astype(bf16)

        return call(
            kernel,
            [dy, dh2, vectors, x1_near, wo, ledger, qkv_l, p_l],
            [
                ((R, D), f32), ((R, D), bf16), ((R, D), bf16), ((16, D), f32),
                ((units * pair, 3 * D), bf16), ((units * pairs, pair, 2 * pair), bf16),
            ],
            0,
            scratch=[pltpu.VMEM((3, 8, D), f32), pltpu.SemaphoreType.DMA((2,))],
            far=2,
            vmem=6,
            wait=wait,
        )

    def global_back(wait):
        def kernel(d_r, g_r, o_r, q_r, p_r, wg_o, dq_o, own_o, other_o):
            wg_o[...] = tn(o_r[...], g_r[...]).astype(bf16)
            loads = []
            for t in range(pairs):
                a, b, c = (slice(k * D + 128 * t, k * D + 128 * t + 128) for k in range(3))
                loads.append(
                    [
                        lambda a=a: q_r[0:gpad, a],
                        lambda b=b: q_r[:, b],
                        lambda c=c: q_r[:, c],
                        lambda t=t: p_r[t],
                        lambda a=a: d_r[LR:R, a],
                    ]
                )

            def store(t, dq, dk, dv):
                a, b = (slice(k * D + 128 * t, k * D + 128 * t + 128) for k in range(2))
                dq_o[:, a] = dq
                own_o[:, a] = dk[0:gpad].astype(bf16)
                own_o[:, b] = dv[0:gpad]
                other_o[:, a] = dk[gpad:].astype(bf16)
                other_o[:, b] = dv[gpad:]

            attend_back(loads, store, head_masks())

        return call(
            kernel,
            [do, g_mid, o, qkv_g, p_g],
            [((D, D), bf16), ((gpad, D), bf16), ((gpad, 2 * D), bf16), ((gpad, 2 * D), bf16)],
            0,
            vmem=8,
            wait=wait,
        )

    def local_back(wait):
        def kernel(d_r, q0_r, p0_r, dx_r, q_h, p_h, w_h, h_h, dx_h, o_r, w_o, h_o, q_s, p_s, sems):
            n, np_ = units * pair, units * pairs

            def load(i):
                rows = pl.ds(pl.multiple_of(i * n, n), n)
                here = pl.ds(pl.multiple_of((i - 1) * n, n), n)
                these, there = pl.ds(i * np_, np_), pl.ds((i - 1) * np_, np_)
                return copies(
                    (q_h.at[rows], q_s.at[here], sems.at[2 * i]), (p_h.at[these], p_s.at[there], sems.at[2 * i + 1])
                )

            more = copies((w_h, w_o, sems.at[0]), (h_h, h_o, sems.at[1]), (dx_r, dx_h, sems.at[2 * laps]))
            for i in range(1, laps):
                start(load(i))
            start(more)
            masks = head_masks()

            def lap(i, q_r, p_r, at):
                where, loads = [], []
                for u in range(units):
                    rows = pl.ds(pl.multiple_of(i * n + u * pair, pair), pair)
                    here = pl.ds(pl.multiple_of(at * n + u * pair, pair), pair)
                    for t in range(pairs):
                        a, b, c = (slice(k * D + 128 * t, k * D + 128 * t + 128) for k in range(3))
                        where.append((rows, a, b, c))
                        loads.append(
                            [lambda here=here, x=x: q_r[here, x] for x in (a, b, c)]
                            + [lambda m=at * np_ + u * pairs + t: p_r[m], lambda rows=rows, a=a: d_r[rows, a]]
                        )

                def store(m, dq, dk, dv):
                    rows, a, b, c = where[m]
                    o_r[rows, a] = dq
                    o_r[rows, b] = dk.astype(bf16)
                    o_r[rows, c] = dv

                attend_back(loads, store, masks)

            def attn_step(i, carry):
                finish(load(i))
                lap(i, q_s, p_s, i - 1)
                return carry

            lap(0, q0_r, p0_r, 0)
            lax.fori_loop(1, laps - 1, attn_step, 0)
            finish(more)
            attn_step(laps - 1, 0)

        out = call(
            kernel,
            [do, q_first, p_first, dx1, qkv_l, p_l, qkv_weight, h],
            [((R, D), f32), ((RX, 3 * D), bf16), ((D, 3 * D), bf16), ((RX, D), bf16)],
            0,
            scratch=[
                pltpu.VMEM((LR - units * pair, 3 * D), bf16),
                pltpu.VMEM((slots // 2 * pairs - units * pairs, pair, 2 * pair), bf16),
                pltpu.SemaphoreType.DMA((2 * laps + 1,)),
            ],
            far=4,
            far_out=1,
            vmem=12,
            wait=wait,
        )
        return out[1:], out[0]

    def qkv_back(wait):
        def kernel(pa_r, pb_r, dqkv_r, h_r, dq_r, own_r, other_r, gout_r, led_r, dqkv_o, ka_o, sa_o, kb_o, sb_o, led_o):
            led_o[...] = led_r[...]
            dqkv_o[LR:R, 0:D] = dq_r[...]
            dqkv_o[LR:R, D:] = own_r[...]
            dqkv_o[R:, 0:D] = jnp.zeros((gpad, D), bf16)
            dqkv_o[R:, D:] = other_r[...]
            put(ka_o, sa_o, pa_r, 0, gout_r[...])
            for k, at in enumerate(((ka_o, sa_o, pa_r, 1), (kb_o, sb_o, pb_r, 0), (kb_o, sb_o, pb_r, 1))):
                cols = slice(k * D, (k + 1) * D)
                put(*at, tn(h_r[...], dqkv_o[:, cols]).astype(bf16))
                if k != 1:
                    s = fold(dqkv_o[:, cols].astype(f32))
                    i = 2 + k // 2
                    led_o[i : i + 1, :] = jnp.sum(s, axis=0, keepdims=True)

        return call(
            kernel,
            [PLACES[0], PLACES[1], dqkv, h_back, dq_g, kv_own, kv_other, g_out, ledger],
            [((RX, 3 * D), bf16)] + [((D, D), bf16)] * 4 + [((16, D), f32)],
            0,
            smem=2,
            vmem=4,
            aliases={2: 0},
            wait=wait,
        )

    def first_back(part, so_far, wait):
        rows = row_halves[part]
        n_rows = rows.stop - rows.start
        stop = min(rows.stop, LR)

        def kernel(v_r, w_r, dqkv_r, led_r, *rest):
            if part:
                kv_r, _, *rest = rest
            x_h, xg_h, dx_h, wd_h, t_o, led_o, *rest = rest
            if not part:
                wd_o, *rest = rest
            dh_s, x_s, acc, xg_s, gs, dx_r, own_s, sems = rest
            moves = copies(
                (x_h.at[rows.start : stop], x_s.at[0 : stop - rows.start], sems.at[0]), (dx_h.at[rows], dx_r, sems.at[2])
            )
            if part:
                moves += copies((xg_h, xg_s, sems.at[1]))
            else:
                moves += copies((wd_h, wd_o, sems.at[1]))
            start(moves)
            dh_s[0 : stop - rows.start, :] = nt(dqkv_r[rows.start : stop, :], w_r[...])
            if part:
                own_s[:, 0:D] = dqkv_r[LR:R, 0:D]
                own_s[:, D:] = (dqkv_r[LR:R, D:].astype(f32) + kv_r[...].astype(f32)).astype(bf16)
                dh_s[stop - rows.start :, :] = nt(own_s[...], w_r[...])
            acc[...] = jnp.zeros_like(acc)
            finish(moves)
            if part:
                gs[...] = jnp.zeros_like(gs)
                gs[0:glen, :] = xg_s[...].astype(f32)
                x_s[stop - rows.start :, :] = gs[...].astype(bf16)

            def step(i, carry):
                here = pl.ds(pl.multiple_of(i * 48, 16), 48)
                there = pl.ds(pl.multiple_of(rows.start + i * 48, 16), 48)
                n, r = normal(x_s[here, :].astype(f32))
                dh = dh_s[here, :]
                t = dx_r[here, :] + norm_back(n, r, dh, v_r[G1 : G1 + 1, :])
                t_o[there, :] = t.astype(bf16)
                acc[0] += fold(dh * n)
                acc[1] += fold(dh)
                return carry

            lax.fori_loop(0, n_rows // 48, step, 0, unroll=True)
            led_o[...] = led_r[...]
            for k in range(2):
                led_o[k : k + 1, :] = led_r[k : k + 1, :] + jnp.sum(acc[k], axis=0, keepdims=True)

        return call(
            kernel,
            [vectors, wqkv, dqkv, ledger] + ([kv_back, so_far] if part else []) + [x_far, xg, dx1, down_weight],
            [((R, D), bf16), ((16, D), f32)] + ([] if part else [((F, D), bf16)]),
            0,
            scratch=[
                pltpu.VMEM((n_rows, D), f32), pltpu.VMEM((n_rows, D), bf16), pltpu.VMEM((2, 8, D), f32),
                pltpu.VMEM((glen, D), bf16), pltpu.VMEM((gpad, D), f32), pltpu.VMEM((n_rows, D), f32),
                pltpu.VMEM((gpad, 3 * D), bf16), pltpu.SemaphoreType.DMA((3,)),
            ],
            far=4,
            vmem=10,
            aliases={5: 0} if part else {},
            wait=wait,
        )

    def output(part, so_far, wait):
        rows = row_halves[part]
        n_rows = rows.stop - rows.start

        def kernel(v_r, w_r, *rest):
            if part:
                _, *rest = rest
            x1_h, *rest = rest
            a_hs, (y_o, a_r, x1_r, sems) = rest[:nf], rest[nf:]
            loads = copies(
                *[(a_hs[f].at[rows], a_r.at[f], sems.at[f]) for f in range(nf)], (x1_h.at[rows], x1_r, sems.at[nf])
            )
            start(loads)
            loads[0].wait()
            y = nn(a_r[0], w_r[0:D, :])
            finish(loads[1:])
            y = y + x1_r[...] + v_r[DB : DB + 1, :]
            for f in range(1, nf):
                y = y + nn(a_r[f], w_r[f * D : (f + 1) * D, :])
            y_o[rows, :] = y.astype(bf16)

        return call(
            kernel,
            [vectors, wd_all] + ([so_far] if part else []) + [x1, *acts],
            [((R, D), bf16)],
            0,
            scratch=[
                pltpu.VMEM((nf, n_rows, D), bf16), pltpu.VMEM((n_rows, D), f32), pltpu.SemaphoreType.DMA((nf + 1,)),
            ],
            far=1 + nf,
            vmem=11,
            aliases={2: 0} if part else {},
            wait=wait,
        )[0]

    def add(a, b):
        return (a.astype(f32) + b.astype(f32)).astype(bf16)

    class Flow:
        def __init__(self, steps):
            self.steps = steps
            self.sends = next(steps)
            self.result = self.got = None

        def launch(self):
            self.got = [swap(v, b) for v, b in self.sends]

        def land(self):
            got, self.got = self.got, None
            try:
                self.sends = self.steps.send(got)
            except StopIteration as end:
                self.result = end.value

    def halves(v):
        h = v.shape[0] // 2
        return v[:h], v[h:]

    def join(*parts):
        return jnp.concatenate(parts, axis=0)

    def sum_two(a, b):
        for bits in (("c", "c"), ("x", "y"), ("y", "x")):
            if bits[0] == "c":
                (a, sa), (b, sb) = a, b
            else:
                (a, sa), (b, sb) = halves(a), halves(b)
            ga, gb = yield [(sa, bits[0]), (sb, bits[1])]
            a, b = add(a, ga), add(b, gb)
        for bit in ("z0", "z1"):
            (a, sa), (b, sb) = halves(a), halves(b)
            (got,) = yield [(join(sa, sb), bit)]
            ga, gb = halves(got)
            a, b = add(a, ga), add(b, gb)
        m = 16
        while m < ndp:
            v = join(a, b)
            (got,) = yield [(v, m)]
            a, b = halves(add(v, got))
            m *= 2
        for bit in ("z1", "z0"):
            (got,) = yield [(join(a, b), bit)]
            ga, gb = halves(got)
            a, b = join(a, ga), join(b, gb)
        for bits in (("y", "x"), ("x", "y"), ("c", "c")):
            ga, gb = yield [(a, bits[0]), (b, bits[1])]
            if bits[0] != "c":
                a, b = join(a, ga), join(b, gb)
        return [a, ga, b, gb]

    def send_once(v, bit):
        (got,) = yield [(v, bit)]
        return got

    def sum_small(v):
        more, m = [], 16
        while m < ndp:
            more.append(m)
            m *= 2
        for bit in (*more, "z1", "c", "z0", "y", "x"):
            v = v.astype(bf16)
            (got,) = yield [(v, bit)]
            v = v.astype(f32) + got.astype(f32)
        return v

    def place(blocks, places, sums, outs, wait=()):
        made = [not isinstance(t, tuple) for t in outs]
        shapes = [t.shape if m else t for t, m in zip(outs, made)]

        def kernel(*refs):
            pos_rs, refs = refs[: len(places)], refs[len(places) :]
            sums_r, refs = refs[: len(sums)], refs[len(sums) + sum(made) :]
            outs_h, (work, sems) = refs[: len(outs)], refs[len(outs) :]
            moves = []
            for n, (which, where, side, half) in enumerate(blocks):
                pos_r, own_r, got_r = pos_rs[side], sums_r[2 * side], sums_r[2 * side + 1]
                if n >= 2:
                    moves[n - 2].wait()
                for j in range(0, 16, 2):
                    mine, here = place_of(pos_r, half * 16 + j)
                    x, y = own_r[here, :].astype(f32), got_r[here, :].astype(f32)
                    work[n % 2, j * CHUNK : (j + 1) * CHUNK, :] = jnp.where(mine, x, y)
                    work[n % 2, (j + 1) * CHUNK : (j + 2) * CHUNK, :] = jnp.where(mine, y, x)
                r, c = (slice(i * D, (i + 1) * D) for i in where)
                moves += copies((work.at[n % 2], outs_h[which].at[r, c], sems.at[n]))
                moves[n].start()
            for t in moves[-2:]:
                t.wait()

        before = [t for t, m in zip(outs, made) if m]
        return call(
            kernel,
            places + sums + before,
            [(s, f32) for s in shapes],
            0,
            scratch=[pltpu.VMEM((2, D, D), f32), pltpu.SemaphoreType.DMA((len(blocks),))],
            vmem=7,
            smem=len(places),
            far=len(before),
            far_out=len(outs),
            aliases={len(places + sums) + i: j for i, j in enumerate(j for j, m in enumerate(made) if m)},
            wait=wait,
        )

    waits = []

    def run(kernel, *flows, hold=()):
        flows = [flow for flow in flows if flow.result is None]
        for flow in (*flows, *hold):
            if flow.got is None:
                flow.launch()
        sends = [v for flow in flows for v, _ in flow.sends]
        out = kernel(waits + sends) if kernel else None
        if kernel and flows:
            out, got = lax.optimization_barrier((out, [flow.got for flow in flows]))
            for flow, t in zip(flows, got):
                flow.got = t
        waits[:] = [t for flow in flows for t in flow.got]
        for flow in flows:
            flow.land()
        return out

    acts, blocks, kept = [], [], []
    state = (wu, wd, x1)

    def hidden(f, *flows):
        nonlocal state
        block, state = run(lambda wait: mlp(f, state, wait), *flows)
        blocks.append(block)

    hidden(0)
    (x1,) = kept
    hidden(1)
    one = Flow(sum_two(*blocks[0:2]))
    hidden(2, one)
    hidden(3, one)
    x1_near, dh2 = state
    two = Flow(sum_two(*blocks[2:4]))
    dx1, do, g_mid, ledger, q_first, p_first = run(second_back, one, two)
    (g_out, dq_g, kv_own, kv_other), ((dqkv, wqkv, h_back), dx1) = run(
        lambda wait: (global_back(wait), local_back(wait)), one, two
    )
    kv = Flow(send_once(kv_other, "y"))
    dqkv, ka, sa, kb, sb, ledger = run(qkv_back, one, two, kv)
    kv_back = kv.result

    three = Flow(sum_two((ka, sa), (kb, sb)))
    nothing = lambda wait: ()

    def place_half(pick, blocks, sums, outs, wait=()):
        made = [not isinstance(t, tuple) for t in outs]
        shapes = [t.shape if m else t for t, m in zip(outs, made)]

        def kernel(pa_r, pb_r, *refs):
            sums_r, refs = refs[:2], refs[2 + sum(made) :]
            outs_h, (work, sems) = refs[: len(outs)], refs[len(outs) :]
            moves = []
            for n, (which, where, side, half) in enumerate(blocks):
                for k in range(8):
                    mine, here = place_of((pa_r, pb_r)[side], half * 16 + 2 * k)
                    j = 2 * k + jnp.where(mine, pick, 1 - pick)
                    work[n, k] = sums_r[side][here, :].astype(f32)
                    rows = pl.ds(pl.multiple_of(where[0] * D + j * CHUNK, 16), CHUNK)
                    cols = slice(where[1] * D, (where[1] + 1) * D)
                    moves += copies((work.at[n, k], outs_h[which].at[rows, cols], sems.at[8 * n + k]))
                    moves[-1].start()
            finish(moves)

        before = [t for t, m in zip(outs, made) if m]
        return call(
            kernel,
            PLACES + sums + before,
            [(s, f32) for s in shapes],
            0,
            scratch=[pltpu.VMEM((len(blocks), 8, CHUNK, D), f32), pltpu.SemaphoreType.DMA((8 * len(blocks),))],
            vmem=7,
            smem=2,
            far=len(before),
            far_out=len(outs),
            aliases={4 + i: i for i in range(len(before))},
            wait=wait,
        )

    def place_pair(k, flow, outs, wait):
        blocks = [(i, (0, f) if i == 0 else (f, 0), f % 2, 1 - i) for f in (2 * k, 2 * k + 1) for i in (1, 0)]
        return place(blocks, PLACES, flow.result, outs, wait)

    run(nothing, three)
    grad, ledger, wd_all = run(lambda wait: first_back(0, None, wait), three, one, two)
    run(nothing, three, one, two)
    grad, ledger = run(lambda wait: first_back(1, grad, wait), three, one, two)
    four = Flow(sum_small(ledger))
    run(nothing, three, one, two, four)
    y = run(lambda wait: output(0, None, wait), three, two, four)
    y = run(lambda wait: output(1, y, wait), three, one, two, four)
    local_grad = run(lambda wait: lax.optimization_barrier(unpad(grad)), three, two, four)
    while one.result is None or two.result is None:
        run(nothing, three, one, two, four)

    def places_mlp(wait):
        made = place_pair(0, one, [(D, F), (F, D)], wait)
        return lax.optimization_barrier(jnp.where(live, unpad(y), 0)), place_pair(1, two, made, wait)

    local_out, (up_grad, down_grad) = run(places_mlp, three, four)
    while four.result is None or len(three.sends) != 2 or three.sends[0][1] != "c":
        run(nothing, three, four)
    total = four.result
    blocks = [(0, (0, 0), 0, 0), (1, (0, 0), 0, 1), (1, (0, 1), 1, 0), (1, (0, 2), 1, 1)]

    def last_rows(wait):
        pieces = [t[LR : LR + glen].reshape(1, glen, D) for t in (y, grad)]
        pieces += [total[i] for i in range(8)] + [total[8 : 8 + nf].reshape(-1)]
        own = [v for v, _ in three.sends]
        return lax.optimization_barrier(tuple(pieces)), place_half(0, blocks, own, [(D, D), (D, 3 * D)], wait)

    pieces, made = run(last_rows, three)
    global_out, global_grad, *total = pieces
    out_grad, qkv_grad = place_half(1, blocks, three.result[1::2], made)

    return (
        global_out,
        local_out,
        global_grad,
        local_grad,
        total[0],
        total[1],
        qkv_grad,
        total[2],
        total[3],
        out_grad,
        total[4],
        total[5],
        total[6],
        up_grad,
        total[8],
        down_grad,
        total[7],
    )


def solution(mesh):
    tokens = (P("dp", "blk", None), P(("blk", "dp"), None, None))
    return jax.shard_map(
        per_device,
        mesh=mesh,
        in_specs=(*tokens, P(("blk", "dp")), *([P()] * 13), *tokens),
        out_specs=(*tokens, *tokens, *([P()] * 13)),
        check_vma=False,
    )
```

```python
import math

import jax
import jax.numpy as jnp
import numpy as np
from jax import lax
from jax.experimental import pallas as pl
from jax.experimental.pallas import tpu as pltpu
from jax.sharding import PartitionSpec as P

HEADS = 12
EPS = 1e-06
bf16 = jnp.bfloat16
f32 = jnp.float32
CHUNK = 48
BLANK = -1e30


def nn(a, b):
    return lax.dot_general(a, b, (((1,), (0,)), ((), ())), preferred_element_type=f32)


def nt(a, b):
    return lax.dot_general(a, b, (((1,), (1,)), ((), ())), preferred_element_type=f32)


def tn(a, b):
    return lax.dot_general(a, b, (((0,), (0,)), ((), ())), preferred_element_type=f32)


def normal(x):
    center = x - jnp.mean(x, axis=-1, keepdims=True)
    r = lax.rsqrt(jnp.mean(center * center, axis=-1, keepdims=True) + EPS)
    return center * r, r


def norm_back(n, r, dh, gain):
    e = dh * gain
    return r * (e - jnp.mean(e, axis=-1, keepdims=True) - n * jnp.mean(e * n, axis=-1, keepdims=True))


def fold(x):
    return jnp.sum(x.reshape(x.shape[0] // 8, 8, x.shape[1]), axis=0)


def head_masks():
    lane = lax.broadcasted_iota(jnp.int32, (1, 128), 1)
    return [(lane < 64).astype(f32).astype(bf16), (lane >= 64).astype(f32).astype(bf16)]


def stack_heads(t, masks):
    return jnp.concatenate([t * m for m in masks], axis=0)


def pick_heads(t):
    n = t.shape[0] // 2
    low = lax.broadcasted_iota(jnp.int32, (n, 128), 1) < 64
    return jnp.where(low, t[:n], t[n:])


def attend(loads, mask, masks):
    scores = [nt(k(), stack_heads(q(), masks)) + mask for q, k, _ in loads]
    chances = []
    for s in scores:
        p = jnp.exp(s - jnp.max(s, axis=0, keepdims=True))
        chances.append((p * (1.0 / jnp.sum(p, axis=0, keepdims=True))).astype(bf16))
    return [(p, pick_heads(tn(p, v()))) for p, (_, _, v) in zip(chances, loads)]


def attend_back(loads, store, masks):
    outer = [stack_heads(do(), masks) for _, _, _, _, do in loads]
    dps = [nt(v(), d) for d, (_, _, v, _, _) in zip(outer, loads)]
    dvs = [nn(p(), d).astype(bf16) for d, (_, _, _, p, _) in zip(outer, loads)]
    dss = []
    for dp, (_, _, _, p, _) in zip(dps, loads):
        pf = p().astype(f32)
        dss.append((pf * (dp - jnp.sum(pf * dp, axis=0, keepdims=True))).astype(bf16))
    for i, (ds, dv, (q, k, _, _, _)) in enumerate(zip(dss, dvs, loads)):
        dk = nn(ds, stack_heads(q(), masks))
        dq = pick_heads(tn(ds, k())) * 0.125
        store(i, dq.astype(bf16), dk, dv)


def call(kernel, ins, outs, flops, scratch=(), vmem=16, smem=0, far=0, far_out=0, aliases=None, wait=()):
    ins = list(ins)
    if wait:
        ins, _ = lax.optimization_barrier((ins, list(wait)))
    whole = pl.BlockSpec(memory_space=pltpu.VMEM)
    scalars = pl.BlockSpec(memory_space=pltpu.SMEM)
    lying = pl.BlockSpec(memory_space=pltpu.HBM)
    near = len(ins) - far

    def nbytes(s, d):
        return math.prod(s) * jnp.dtype(d).itemsize

    def pinned(i, t):
        if i >= near:
            return pltpu.with_memory_space_constraint(t, pltpu.HBM)
        if i >= smem and nbytes(t.shape, t.dtype) > 2**16:
            return pltpu.with_memory_space_constraint(t, pltpu.VMEM)
        return t

    def result(i, s, d):
        if i < far_out:
            return pltpu.HBM(s, d)
        if nbytes(s, d) > 2**16:
            return pltpu.VMEM(s, d)
        return jax.ShapeDtypeStruct(s, d)

    size = sum(nbytes(t.shape, t.dtype) for t in ins) + sum(nbytes(s, d) for s, d in outs)
    return pl.pallas_call(
        kernel,
        in_specs=[scalars] * smem + [whole] * (near - smem) + [lying] * far,
        out_specs=[lying] * far_out + [whole] * (len(outs) - far_out),
        out_shape=[result(i, s, d) for i, (s, d) in enumerate(outs)],
        scratch_shapes=list(scratch),
        input_output_aliases=aliases or {},
        compiler_params=pltpu.CompilerParams(vmem_limit_bytes=vmem * 2**20),
        cost_estimate=pl.CostEstimate(flops=1, bytes_accessed=1, transcendentals=0),
    )(*[pinned(i, t) for i, t in enumerate(ins)])


def per_device(
    global_tokens,
    local_tokens,
    local_count,
    first_gain,
    first_shift,
    qkv_weight,
    query_bias,
    value_bias,
    out_weight,
    out_bias,
    second_gain,
    second_shift,
    up_weight,
    up_bias,
    down_weight,
    mlp_down_bias,
    global_cotan,
    local_cotan,
):
    crops, glen, D = global_tokens.shape
    slots, llen, _ = local_tokens.shape
    F = up_weight.shape[1]
    nf = F // D
    lpad = -(-llen // 8) * 8
    gpad = -(-glen // 16) * 16
    assert crops == 1 and D == 768 and lpad * 2 % 16 == 0 and nf % 2 == 0
    LR = slots * lpad
    R = LR + gpad
    pair = 2 * lpad
    pairs = D // 128
    units = 4
    laps = slots // 2 // units
    assert laps * units * 2 == slots and slots % 8 == 0
    nblk, ndp = lax.axis_size("blk"), lax.axis_size("dp")
    blk, dp = lax.axis_index("blk"), lax.axis_index("dp")
    assert nblk == 2 and ndp % 16 == 0
    per_step = 8
    SR = per_step * lpad
    cuts = 3 if R % 48 == 0 else 1
    row_cuts = [slice(i * (R // cuts), (i + 1) * (R // cuts)) for i in range(cuts)]
    half_at = R // 96 * 48
    assert R % 48 == 0
    row_halves = [slice(0, half_at), slice(half_at, R)]

    bit_of = {"c": 0, "x": 1, "z0": 2, "z1": 3, "y": 4}

    def swap(v, b):
        if b == "y":
            return lax.ppermute(v, "blk", [(0, 1), (1, 0)])
        m = b if isinstance(b, int) else 1 << bit_of[b]
        return lax.ppermute(v, "dp", [(i, i ^ m) for i in range(ndp)])

    me = (dp & 15) + 16 * blk
    relative = jnp.arange(32, dtype=jnp.int32) ^ me.astype(jnp.int32)

    def places(order):
        pos = jnp.zeros_like(relative)
        for b in order:
            pos = 2 * pos + ((relative >> bit_of[b]) & 1)
        return pos * CHUNK

    ORDERS = (("c", "x", "y", "z0", "z1"), ("c", "y", "x", "z0", "z1"))
    PLACES = [places(o) for o in ORDERS]

    def copies(*triples):
        return [pltpu.make_async_copy(src, dst, sem) for src, dst, sem in triples]

    def start(moves):
        for t in moves:
            t.start()

    def finish(moves):
        for t in moves:
            t.wait()

    xg = global_tokens.reshape(glen, D)
    xg_other = swap(xg, "y")
    live = (jnp.arange(slots, dtype=jnp.int32) < local_count[0])[:, None, None]

    def unpad(t):
        return t[:LR].reshape(slots, lpad, D)[:, :llen]

    singles = [first_gain, first_shift, query_bias, value_bias, out_bias, second_gain, second_shift, mlp_down_bias, up_bias]
    *singles, xg_other = lax.optimization_barrier((*singles, xg_other))
    vectors = jnp.concatenate([t.reshape(-1, D) for t in singles], axis=0)
    G1, C1, QB, VB, OB, G2, C2, DB, UB = range(9)

    assert 8 + nf <= 16
    lmask = np.full((pair, 2 * pair), BLANK, np.float32)
    for r in range(2 * pair):
        t = (r % pair) // lpad * lpad
        lmask[t : t + llen, r] = 0.0
    gmask = np.full((2 * gpad, 2 * gpad), BLANK, np.float32)
    gmask[:glen] = 0.0
    gmask[gpad : gpad + glen] = 0.0
    lmask = jnp.asarray(lmask)
    gmask = jnp.asarray(gmask)

    def front(
        n_r, v_r, m_r, x_r, dyl_h, xg_h, xo_h, dg_h, gm_h, w_h, wo_h, u_h, d_h,
        x_h, h_h, qkv_h, p_h, qkvg_o, pg_o, o_o, x1_o, h2_o, dy_o, led_o, wo_o, u_o, d_o,
        x_s, dyl_r, h_o, qkv_o, p_o, w, xs, ys, gs, ds, xg_r, xo_r, dg_r, gm_r, acc, sems,
    ):
        def vec(i):
            return v_r[i : i + 1, :]

        cols = [slice(k * D, (k + 1) * D) for k in range(3)]
        loads_w = copies(*[(w_h.at[:, c], w.at[:, c], sems.at[k]) for k, c in enumerate(cols)])
        loads_g = copies(
            (xg_h, xg_r, sems.at[3]), (xo_h, xo_r, sems.at[4]), (dg_h, dg_r, sems.at[5]), (gm_h, gm_r, sems.at[6])
        )
        loads_next = copies(
            (wo_h, wo_o, sems.at[7]), (u_h.at[:, 0:D], u_o, sems.at[8]), (d_h.at[0:D, :], d_o, sems.at[9])
        )
        out_x = copies((x_s, x_h, sems.at[10]))
        load_dy = copies((dyl_h, dyl_r, sems.at[11]))
        start(load_dy + loads_w + loads_g + loads_next)
        xs[...] = jnp.zeros_like(xs)
        ys[...] = jnp.zeros_like(ys)
        acc[...] = jnp.zeros_like(acc)

        def padded(ref, i, xs):
            for j in range(per_step):
                xs[j * lpad : j * lpad + llen, :] = ref[per_step * i + j].astype(f32)
            return xs[...]

        def out_part(i):
            n = units * pair
            rows = pl.ds(pl.multiple_of(i * n, n), n)
            these = pl.ds(i * units * pairs, units * pairs)
            return copies(
                (qkv_o.at[rows], qkv_h.at[rows], sems.at[13 + 2 * i]),
                (p_o.at[these], p_h.at[these], sems.at[14 + 2 * i]),
            )


        def norm_step(i, carry):
            rows = pl.ds(pl.multiple_of(i * SR, SR), SR)
            x = padded(x_r, i, xs)
            x_s[rows, :] = x.astype(bf16)
            n, _ = normal(x)
            h_o[rows, :] = (n * vec(G1) + vec(C1)).astype(bf16)
            at = i * SR + lax.broadcasted_iota(jnp.int32, (SR, 1), 0)
            dy = jnp.where(at < n_r[0] * lpad, padded(dyl_r, i, ys), 0.0)
            dy_o[rows, :] = dy.astype(bf16)
            acc[...] += fold(dy)
            return carry

        finish(load_dy)
        lax.fori_loop(0, LR // SR, norm_step, 0)
        start(out_x)
        finish(loads_g + loads_w + loads_next)
        ds[...] = jnp.zeros_like(ds)
        ds[0:glen, :] = dg_r[...].astype(f32)
        dy_o[LR:R, :] = ds[...].astype(bf16)
        acc[...] += fold(ds[...])
        gs[...] = jnp.zeros_like(gs)
        gs[0:glen, :] = xg_r[...].astype(f32)
        gs[gpad : gpad + glen, :] = xo_r[...].astype(f32)
        n, _ = normal(gs[...])
        hg = (n * vec(G1) + vec(C1)).astype(bf16)
        h_o[LR:, :] = hg
        out_h = copies((h_o, h_h, sems.at[12]))
        start(out_h)
        for k, c in enumerate(cols):
            t = nn(h_o[...], w[:, c])
            if k != 1:
                t = t + vec(QB if k == 0 else VB)
            t = t.astype(bf16)
            if k == 0:
                t = t * jnp.asarray(0.125, bf16)
            qkv_o[:, c] = t[0:LR]
            qkvg_o[:, c] = t[LR:]
        masks = head_masks()

        def attn_step(i, carry):
            where, loads = [], []
            for u in range(units):
                g = i * units + u
                rows = pl.ds(pl.multiple_of(g * pair, pair), pair)
                for t in range(pairs):
                    a = 128 * t
                    where.append((g * pairs + t, rows, slice(a, a + 128)))
                    loads.append([lambda rows=rows, b=k * D + a: qkv_o[rows, b : b + 128] for k in range(3)])
            for (at, rows, lanes), (pt, o) in zip(where, attend(loads, m_r[...], masks)):
                p_o[at] = pt
                o_o[rows, lanes] = o.astype(bf16)
            start(out_part(i))
            return carry

        lax.fori_loop(0, laps, attn_step, 0)
        loads = []
        for t in range(pairs):
            a, b, c = (slice(k * D + 128 * t, k * D + 128 * t + 128) for k in range(3))
            loads.append(
                [lambda a=a: qkvg_o[0:gpad, a], lambda b=b: qkvg_o[:, b], lambda c=c: qkvg_o[:, c]]
            )
        for t, (p, o) in enumerate(attend(loads, gm_r[...], masks)):
            pg_o[t] = p
            o_o[LR:R, 128 * t : 128 * t + 128] = o.astype(bf16)
        finish(out_h + out_x)
        for i in range(laps):
            finish(out_part(i))
        x1_o[0:LR, :] = x_s[...].astype(f32)
        x1_o[LR:R, :] = gs[0:gpad, :]
        for r in row_cuts:
            x1 = nn(o_o[r, :], wo_o[...]) + vec(OB) + x1_o[r, :]
            x1_o[r, :] = x1
            n2, _ = normal(x1)
            h2_o[r, :] = (n2 * vec(G2) + vec(C2)).astype(bf16)
        led_o[...] = jnp.zeros_like(led_o)
        led_o[7:8, :] = jnp.sum(acc[...], axis=0, keepdims=True)

    RX = R + gpad
    attn_kept = [((RX, D), bf16), ((LR, 3 * D), bf16), ((slots // 2 * pairs, pair, 2 * pair), bf16)]
    x_far, h, qkv_l, p_l, qkv_g, p_g, o, x1, h2, dy, ledger, wo, wu, wd = call(
        front,
        [
            local_count, vectors, lmask, local_tokens, local_cotan, xg, xg_other, global_cotan.reshape(glen, D), gmask,
            qkv_weight, out_weight, up_weight, down_weight,
        ],
        [((LR, D), bf16)]
        + attn_kept
        + [
            ((2 * gpad, 3 * D), bf16), ((pairs, 2 * gpad, 2 * gpad), bf16), ((R, D), bf16),
            ((R, D), f32), ((R, D), bf16), ((R, D), bf16), ((16, D), f32),
            ((D, D), bf16), ((D, D), bf16), ((D, D), bf16),
        ],
        0,
        scratch=[pltpu.VMEM((LR, D), bf16), pltpu.VMEM((slots, llen, D), bf16), pltpu.VMEM((RX, D), bf16)]
        + [pltpu.VMEM(s, d) for s, d in attn_kept[1:]]
        + [
            pltpu.VMEM((D, 3 * D), bf16), pltpu.VMEM((SR, D), f32), pltpu.VMEM((SR, D), f32), pltpu.VMEM((2 * gpad, D), f32),
            pltpu.VMEM((gpad, D), f32),
            pltpu.VMEM((glen, D), bf16), pltpu.VMEM((glen, D), bf16), pltpu.VMEM((glen, D), bf16),
            pltpu.VMEM((2 * gpad, 2 * gpad), f32), pltpu.VMEM((8, D), f32), pltpu.SemaphoreType.DMA((13 + 2 * laps,)),
        ],
        smem=1,
        far=9,
        far_out=4,
        vmem=27,
    )

    def place_of(pos_r, i):
        at = pos_r[i]
        mine = at < 16 * CHUNK
        return mine, pl.ds(pl.multiple_of(jnp.where(mine, at, at - 16 * CHUNK), 16), CHUNK)

    def put(keep_o, send_o, pos_r, half, value):
        for j in range(0, 16, 2):
            mine, here = place_of(pos_r, half * 16 + j)
            x, y = (value[(j + k) * CHUNK : (j + k + 1) * CHUNK, :] for k in range(2))
            keep_o[here, :] = jnp.where(mine, x, y)
            send_o[here, :] = jnp.where(mine, y, x)

    def mlp(f, state, wait):
        first, last = f == 0, f == nf - 1
        there = slice((f + 1) * D, (f + 2) * D)

        def kernel(pos_r, h_r, d_r, v_r, u_r, w_r, side_r, led_r, u_h, w_h, *rest):
            if last:
                x1_h, *rest = rest
            a_h, *rest = rest
            if first:
                side_h, *rest = rest
            keep_o, send_o, led_o, dh_o, *rest = rest
            if last:
                x1_o, *rest = rest
            else:
                u_o, w_o, *rest = rest
            a_o, du_r, sems = rest
            moves = []
            if not last:
                moves = copies((u_h.at[:, there], u_o, sems.at[0]), (w_h.at[there, :], w_o, sems.at[1]))
            if first:
                moves += copies((side_r, side_h, sems.at[2]))
            if last:
                moves += copies((x1_h, x1_o, sems.at[0]))
            (store,) = copies((a_o, a_h, sems.at[3]))
            start(moves)
            acc = jnp.zeros((8, D), f32)
            for i, rows in enumerate(row_cuts):
                u = nn(h_r[rows, :], u_r[...]) + v_r[UB + f : UB + f + 1, :]
                da = nt(d_r[rows, :], w_r[...])
                cdf = 0.5 + 0.5 * lax.erf(u * math.sqrt(0.5))
                a_o[rows, :] = (u * cdf).astype(bf16)
                slope = cdf + u * (jnp.exp(u * u * -0.5) * (1.0 / math.sqrt(2 * math.pi)))
                du = (da * slope).astype(bf16)
                du_r[rows, :] = du
                acc = acc + fold(du.astype(f32))
                if i == cuts - 2:
                    finish(moves)
            store.start()
            led_o[...] = led_r[...]
            led_o[8 + f : 9 + f, :] = jnp.sum(acc, axis=0, keepdims=True)
            put(keep_o, send_o, pos_r, 0, tn(a_o[...], d_r[...]).astype(bf16))
            put(keep_o, send_o, pos_r, 1, tn(h_r[...], du_r[...]).astype(bf16))
            for rows in row_cuts:
                dh = nt(du_r[rows, :], u_r[...])
                dh_o[rows, :] = dh if first else side_r[rows, :] + dh
            store.wait()

        u_w, d_w, side = state
        nonlocal ledger
        a, *out = call(
            kernel,
            [PLACES[f % 2], h2, dy, vectors, u_w, d_w, side, ledger, up_weight, down_weight] + ([x1] if last else []),
            [((R, D), bf16)]
            + ([((R, D), f32)] if first else [])
            + [((D, D), bf16), ((D, D), bf16), ((16, D), f32), ((R, D), f32)]
            + ([((R, D), f32)] if last else [((D, D), bf16), ((D, D), bf16)]),
            0,
            scratch=[pltpu.VMEM((R, D), bf16), pltpu.VMEM((R, D), bf16), pltpu.SemaphoreType.DMA((4,))],
            far_out=2 if first else 1,
            smem=1,
            far=3 if last else 2,
            aliases={} if first else {6: 4},
            vmem=9,
            wait=wait,
        )
        if first:
            kept.append(out.pop(0))
        keep, send, ledger, dh, *state = out
        acts.append(a)
        return (keep, send), (*state, dh)

    def second_back(wait):
        def kernel(dy_r, dh_r, v_r, x1_r, wo_r, led_r, q_h, p_h, dx_o, do_o, g_o, led_o, q_o, p_o, acc, sems):
            first_lap = copies(
                (q_h.at[0 : units * pair], q_o, sems.at[0]), (p_h.at[0 : units * pairs], p_o, sems.at[1])
            )
            start(first_lap)
            for k in range(3):
                acc[k] = jnp.zeros((8, D), f32)
            for r in row_cuts:
                dh = dh_r[r, :]
                n, rs = normal(x1_r[r, :])
                dx = dy_r[r, :].astype(f32) + norm_back(n, rs, dh, v_r[G2 : G2 + 1, :])
                dx_o[r, :] = dx
                g = dx.astype(bf16)
                g_o[r, :] = g
                acc[0] += fold(dh * n)
                acc[1] += fold(dh)
                acc[2] += fold(g.astype(f32))
            finish(first_lap)
            led_o[...] = led_r[...]
            for k, i in enumerate((5, 6, 4)):
                led_o[i : i + 1, :] = jnp.sum(acc[k], axis=0, keepdims=True)
            do_o[...] = nt(g_o[...], wo_r[...]).astype(bf16)

        return call(
            kernel,
            [dy, dh2, vectors, x1_near, wo, ledger, qkv_l, p_l],
            [
                ((R, D), f32), ((R, D), bf16), ((R, D), bf16), ((16, D), f32),
                ((units * pair, 3 * D), bf16), ((units * pairs, pair, 2 * pair), bf16),
            ],
            0,
            scratch=[pltpu.VMEM((3, 8, D), f32), pltpu.SemaphoreType.DMA((2,))],
            far=2,
            vmem=6,
            wait=wait,
        )

    def global_back(wait):
        def kernel(d_r, g_r, o_r, q_r, p_r, wg_o, dq_o, own_o, other_o):
            wg_o[...] = tn(o_r[...], g_r[...]).astype(bf16)
            loads = []
            for t in range(pairs):
                a, b, c = (slice(k * D + 128 * t, k * D + 128 * t + 128) for k in range(3))
                loads.append(
                    [
                        lambda a=a: q_r[0:gpad, a],
                        lambda b=b: q_r[:, b],
                        lambda c=c: q_r[:, c],
                        lambda t=t: p_r[t],
                        lambda a=a: d_r[LR:R, a],
                    ]
                )

            def store(t, dq, dk, dv):
                a, b = (slice(k * D + 128 * t, k * D + 128 * t + 128) for k in range(2))
                dq_o[:, a] = dq
                own_o[:, a] = dk[0:gpad].astype(bf16)
                own_o[:, b] = dv[0:gpad]
                other_o[:, a] = dk[gpad:].astype(bf16)
                other_o[:, b] = dv[gpad:]

            attend_back(loads, store, head_masks())

        return call(
            kernel,
            [do, g_mid, o, qkv_g, p_g],
            [((D, D), bf16), ((gpad, D), bf16), ((gpad, 2 * D), bf16), ((gpad, 2 * D), bf16)],
            0,
            vmem=8,
            wait=wait,
        )

    def local_back(wait):
        def kernel(d_r, q0_r, p0_r, dx_r, q_h, p_h, w_h, h_h, dx_h, o_r, w_o, h_o, q_s, p_s, sems):
            n, np_ = units * pair, units * pairs

            def load(i):
                rows = pl.ds(pl.multiple_of(i * n, n), n)
                here = pl.ds(pl.multiple_of((i - 1) * n, n), n)
                these, there = pl.ds(i * np_, np_), pl.ds((i - 1) * np_, np_)
                return copies(
                    (q_h.at[rows], q_s.at[here], sems.at[2 * i]), (p_h.at[these], p_s.at[there], sems.at[2 * i + 1])
                )

            more = copies((w_h, w_o, sems.at[0]), (h_h, h_o, sems.at[1]), (dx_r, dx_h, sems.at[2 * laps]))
            for i in range(1, laps):
                start(load(i))
            start(more)
            masks = head_masks()

            def lap(i, q_r, p_r, at):
                where, loads = [], []
                for u in range(units):
                    rows = pl.ds(pl.multiple_of(i * n + u * pair, pair), pair)
                    here = pl.ds(pl.multiple_of(at * n + u * pair, pair), pair)
                    for t in range(pairs):
                        a, b, c = (slice(k * D + 128 * t, k * D + 128 * t + 128) for k in range(3))
                        where.append((rows, a, b, c))
                        loads.append(
                            [lambda here=here, x=x: q_r[here, x] for x in (a, b, c)]
                            + [lambda m=at * np_ + u * pairs + t: p_r[m], lambda rows=rows, a=a: d_r[rows, a]]
                        )

                def store(m, dq, dk, dv):
                    rows, a, b, c = where[m]
                    o_r[rows, a] = dq
                    o_r[rows, b] = dk.astype(bf16)
                    o_r[rows, c] = dv

                attend_back(loads, store, masks)

            def attn_step(i, carry):
                finish(load(i))
                lap(i, q_s, p_s, i - 1)
                return carry

            lap(0, q0_r, p0_r, 0)
            lax.fori_loop(1, laps - 1, attn_step, 0)
            finish(more)
            attn_step(laps - 1, 0)

        out = call(
            kernel,
            [do, q_first, p_first, dx1, qkv_l, p_l, qkv_weight, h],
            [((R, D), f32), ((RX, 3 * D), bf16), ((D, 3 * D), bf16), ((RX, D), bf16)],
            0,
            scratch=[
                pltpu.VMEM((LR - units * pair, 3 * D), bf16),
                pltpu.VMEM((slots // 2 * pairs - units * pairs, pair, 2 * pair), bf16),
                pltpu.SemaphoreType.DMA((2 * laps + 1,)),
            ],
            far=4,
            far_out=1,
            vmem=12,
            wait=wait,
        )
        return out[1:], out[0]

    def qkv_back(wait):
        def kernel(pa_r, pb_r, dqkv_r, h_r, dq_r, own_r, other_r, gout_r, led_r, dqkv_o, ka_o, sa_o, kb_o, sb_o, led_o):
            led_o[...] = led_r[...]
            dqkv_o[LR:R, 0:D] = dq_r[...]
            dqkv_o[LR:R, D:] = own_r[...]
            dqkv_o[R:, 0:D] = jnp.zeros((gpad, D), bf16)
            dqkv_o[R:, D:] = other_r[...]
            put(ka_o, sa_o, pa_r, 0, gout_r[...])
            for k, at in enumerate(((ka_o, sa_o, pa_r, 1), (kb_o, sb_o, pb_r, 0), (kb_o, sb_o, pb_r, 1))):
                cols = slice(k * D, (k + 1) * D)
                put(*at, tn(h_r[...], dqkv_o[:, cols]).astype(bf16))
                if k != 1:
                    s = fold(dqkv_o[:, cols].astype(f32))
                    i = 2 + k // 2
                    led_o[i : i + 1, :] = jnp.sum(s, axis=0, keepdims=True)

        return call(
            kernel,
            [PLACES[0], PLACES[1], dqkv, h_back, dq_g, kv_own, kv_other, g_out, ledger],
            [((RX, 3 * D), bf16)] + [((D, D), bf16)] * 4 + [((16, D), f32)],
            0,
            smem=2,
            vmem=4,
            aliases={2: 0},
            wait=wait,
        )

    def first_back(part, so_far, wait):
        rows = row_halves[part]
        n_rows = rows.stop - rows.start
        stop = min(rows.stop, LR)

        def kernel(v_r, w_r, dqkv_r, led_r, *rest):
            if part:
                kv_r, _, *rest = rest
            x_h, xg_h, dx_h, wd_h, t_o, led_o, *rest = rest
            if not part:
                wd_o, *rest = rest
            dh_s, x_s, acc, xg_s, gs, dx_r, own_s, sems = rest
            moves = copies(
                (x_h.at[rows.start : stop], x_s.at[0 : stop - rows.start], sems.at[0]), (dx_h.at[rows], dx_r, sems.at[2])
            )
            if part:
                moves += copies((xg_h, xg_s, sems.at[1]))
            else:
                moves += copies((wd_h, wd_o, sems.at[1]))
            start(moves)
            dh_s[0 : stop - rows.start, :] = nt(dqkv_r[rows.start : stop, :], w_r[...])
            if part:
                own_s[:, 0:D] = dqkv_r[LR:R, 0:D]
                own_s[:, D:] = (dqkv_r[LR:R, D:].astype(f32) + kv_r[...].astype(f32)).astype(bf16)
                dh_s[stop - rows.start :, :] = nt(own_s[...], w_r[...])
            acc[...] = jnp.zeros_like(acc)
            finish(moves)
            if part:
                gs[...] = jnp.zeros_like(gs)
                gs[0:glen, :] = xg_s[...].astype(f32)
                x_s[stop - rows.start :, :] = gs[...].astype(bf16)

            def step(i, carry):
                here = pl.ds(pl.multiple_of(i * 48, 16), 48)
                there = pl.ds(pl.multiple_of(rows.start + i * 48, 16), 48)
                n, r = normal(x_s[here, :].astype(f32))
                dh = dh_s[here, :]
                t = dx_r[here, :] + norm_back(n, r, dh, v_r[G1 : G1 + 1, :])
                t_o[there, :] = t.astype(bf16)
                acc[0] += fold(dh * n)
                acc[1] += fold(dh)
                return carry

            lax.fori_loop(0, n_rows // 48, step, 0, unroll=True)
            led_o[...] = led_r[...]
            for k in range(2):
                led_o[k : k + 1, :] = led_r[k : k + 1, :] + jnp.sum(acc[k], axis=0, keepdims=True)

        return call(
            kernel,
            [vectors, wqkv, dqkv, ledger] + ([kv_back, so_far] if part else []) + [x_far, xg, dx1, down_weight],
            [((R, D), bf16), ((16, D), f32)] + ([] if part else [((F, D), bf16)]),
            0,
            scratch=[
                pltpu.VMEM((n_rows, D), f32), pltpu.VMEM((n_rows, D), bf16), pltpu.VMEM((2, 8, D), f32),
                pltpu.VMEM((glen, D), bf16), pltpu.VMEM((gpad, D), f32), pltpu.VMEM((n_rows, D), f32),
                pltpu.VMEM((gpad, 3 * D), bf16), pltpu.SemaphoreType.DMA((3,)),
            ],
            far=4,
            vmem=10,
            aliases={5: 0} if part else {},
            wait=wait,
        )

    def output(part, so_far, wait):
        rows = row_halves[part]
        n_rows = rows.stop - rows.start

        def kernel(v_r, w_r, *rest):
            if part:
                _, *rest = rest
            x1_h, *rest = rest
            a_hs, (y_o, a_r, x1_r, sems) = rest[:nf], rest[nf:]
            loads = copies(
                *[(a_hs[f].at[rows], a_r.at[f], sems.at[f]) for f in range(nf)], (x1_h.at[rows], x1_r, sems.at[nf])
            )
            start(loads)
            loads[0].wait()
            y = nn(a_r[0], w_r[0:D, :])
            finish(loads[1:])
            y = y + x1_r[...] + v_r[DB : DB + 1, :]
            for f in range(1, nf):
                y = y + nn(a_r[f], w_r[f * D : (f + 1) * D, :])
            y_o[rows, :] = y.astype(bf16)

        return call(
            kernel,
            [vectors, wd_all] + ([so_far] if part else []) + [x1, *acts],
            [((R, D), bf16)],
            0,
            scratch=[
                pltpu.VMEM((nf, n_rows, D), bf16), pltpu.VMEM((n_rows, D), f32), pltpu.SemaphoreType.DMA((nf + 1,)),
            ],
            far=1 + nf,
            vmem=11,
            aliases={2: 0} if part else {},
            wait=wait,
        )[0]

    def add(a, b):
        return (a.astype(f32) + b.astype(f32)).astype(bf16)

    class Flow:
        def __init__(self, steps):
            self.steps = steps
            self.sends = next(steps)
            self.result = self.got = None

        def launch(self):
            self.got = [swap(v, b) for v, b in self.sends]

        def land(self):
            got, self.got = self.got, None
            try:
                self.sends = self.steps.send(got)
            except StopIteration as end:
                self.result = end.value

    def halves(v):
        h = v.shape[0] // 2
        return v[:h], v[h:]

    def join(*parts):
        return jnp.concatenate(parts, axis=0)

    def sum_two(a, b):
        for bits in (("c", "c"), ("x", "y"), ("y", "x")):
            if bits[0] == "c":
                (a, sa), (b, sb) = a, b
            else:
                (a, sa), (b, sb) = halves(a), halves(b)
            ga, gb = yield [(sa, bits[0]), (sb, bits[1])]
            a, b = add(a, ga), add(b, gb)
        for bit in ("z0", "z1"):
            (a, sa), (b, sb) = halves(a), halves(b)
            (got,) = yield [(join(sa, sb), bit)]
            ga, gb = halves(got)
            a, b = add(a, ga), add(b, gb)
        m = 16
        while m < ndp:
            v = join(a, b)
            (got,) = yield [(v, m)]
            a, b = halves(add(v, got))
            m *= 2
        for bit in ("z1", "z0"):
            (got,) = yield [(join(a, b), bit)]
            ga, gb = halves(got)
            a, b = join(a, ga), join(b, gb)
        for bits in (("y", "x"), ("x", "y"), ("c", "c")):
            ga, gb = yield [(a, bits[0]), (b, bits[1])]
            if bits[0] != "c":
                a, b = join(a, ga), join(b, gb)
        return [a, ga, b, gb]

    def send_once(v, bit):
        (got,) = yield [(v, bit)]
        return got

    def sum_small(v):
        more, m = [], 16
        while m < ndp:
            more.append(m)
            m *= 2
        for bit in (*more, "z1", "c", "z0", "y", "x"):
            v = v.astype(bf16)
            (got,) = yield [(v, bit)]
            v = v.astype(f32) + got.astype(f32)
        return v

    def place(blocks, places, sums, outs, wait=()):
        made = [not isinstance(t, tuple) for t in outs]
        shapes = [t.shape if m else t for t, m in zip(outs, made)]

        def kernel(*refs):
            pos_rs, refs = refs[: len(places)], refs[len(places) :]
            sums_r, refs = refs[: len(sums)], refs[len(sums) + sum(made) :]
            outs_h, (work, sems) = refs[: len(outs)], refs[len(outs) :]
            moves = []
            for n, (which, where, side, half) in enumerate(blocks):
                pos_r, own_r, got_r = pos_rs[side], sums_r[2 * side], sums_r[2 * side + 1]
                if n >= 2:
                    moves[n - 2].wait()
                for j in range(0, 16, 2):
                    mine, here = place_of(pos_r, half * 16 + j)
                    x, y = own_r[here, :].astype(f32), got_r[here, :].astype(f32)
                    work[n % 2, j * CHUNK : (j + 1) * CHUNK, :] = jnp.where(mine, x, y)
                    work[n % 2, (j + 1) * CHUNK : (j + 2) * CHUNK, :] = jnp.where(mine, y, x)
                r, c = (slice(i * D, (i + 1) * D) for i in where)
                moves += copies((work.at[n % 2], outs_h[which].at[r, c], sems.at[n]))
                moves[n].start()
            for t in moves[-2:]:
                t.wait()

        before = [t for t, m in zip(outs, made) if m]
        return call(
            kernel,
            places + sums + before,
            [(s, f32) for s in shapes],
            0,
            scratch=[pltpu.VMEM((2, D, D), f32), pltpu.SemaphoreType.DMA((len(blocks),))],
            vmem=7,
            smem=len(places),
            far=len(before),
            far_out=len(outs),
            aliases={len(places + sums) + i: j for i, j in enumerate(j for j, m in enumerate(made) if m)},
            wait=wait,
        )

    waits = []

    def run(kernel, *flows, hold=()):
        flows = [flow for flow in flows if flow.result is None]
        for flow in (*flows, *hold):
            if flow.got is None:
                flow.launch()
        sends = [v for flow in flows for v, _ in flow.sends]
        out = kernel(waits + sends) if kernel else None
        if kernel and flows:
            out, got = lax.optimization_barrier((out, [flow.got for flow in flows]))
            for flow, t in zip(flows, got):
                flow.got = t
        waits[:] = [t for flow in flows for t in flow.got]
        for flow in flows:
            flow.land()
        return out

    acts, blocks, kept = [], [], []
    state = (wu, wd, x1)

    def hidden(f, *flows):
        nonlocal state
        block, state = run(lambda wait: mlp(f, state, wait), *flows)
        blocks.append(block)

    hidden(0)
    (x1,) = kept
    hidden(1)
    one = Flow(sum_two(*blocks[0:2]))
    hidden(2, one)
    hidden(3, one)
    x1_near, dh2 = state
    two = Flow(sum_two(*blocks[2:4]))
    dx1, do, g_mid, ledger, q_first, p_first = run(second_back, one, two)
    (g_out, dq_g, kv_own, kv_other), ((dqkv, wqkv, h_back), dx1) = run(
        lambda wait: (global_back(wait), local_back(wait)), one, two
    )
    dqkv, ka, sa, kb, sb, ledger = run(qkv_back, one, two)

    three = Flow(sum_two((ka, sa), (kb, sb)))
    nothing = lambda wait: ()

    def place_half(pick, blocks, sums, outs, wait=()):
        made = [not isinstance(t, tuple) for t in outs]
        shapes = [t.shape if m else t for t, m in zip(outs, made)]

        def kernel(pa_r, pb_r, *refs):
            sums_r, refs = refs[:2], refs[2 + sum(made) :]
            outs_h, (work, sems) = refs[: len(outs)], refs[len(outs) :]
            moves = []
            for n, (which, where, side, half) in enumerate(blocks):
                for k in range(8):
                    mine, here = place_of((pa_r, pb_r)[side], half * 16 + 2 * k)
                    j = 2 * k + jnp.where(mine, pick, 1 - pick)
                    work[n, k] = sums_r[side][here, :].astype(f32)
                    rows = pl.ds(pl.multiple_of(where[0] * D + j * CHUNK, 16), CHUNK)
                    cols = slice(where[1] * D, (where[1] + 1) * D)
                    moves += copies((work.at[n, k], outs_h[which].at[rows, cols], sems.at[8 * n + k]))
                    moves[-1].start()
            finish(moves)

        before = [t for t, m in zip(outs, made) if m]
        return call(
            kernel,
            PLACES + sums + before,
            [(s, f32) for s in shapes],
            0,
            scratch=[pltpu.VMEM((len(blocks), 8, CHUNK, D), f32), pltpu.SemaphoreType.DMA((8 * len(blocks),))],
            vmem=7,
            smem=2,
            far=len(before),
            far_out=len(outs),
            aliases={4 + i: i for i in range(len(before))},
            wait=wait,
        )

    def place_pair(k, flow, outs, wait):
        blocks = [(i, (0, f) if i == 0 else (f, 0), f % 2, 1 - i) for f in (2 * k, 2 * k + 1) for i in (1, 0)]
        return place(blocks, PLACES, flow.result, outs, wait)

    run(nothing, three)
    grad, ledger, wd_all = run(lambda wait: first_back(0, None, wait), three, one, two)
    kv = Flow(send_once(lax.optimization_barrier((kv_other, three.sends[0][0]))[0], "y"))
    run(nothing, three, one, two, kv)
    kv_back = kv.result
    grad, ledger = run(lambda wait: first_back(1, grad, wait), three, one, two)
    four = Flow(sum_small(ledger))
    y = run(lambda wait: output(0, None, wait), three, one, two, four)
    local_grad = run(lambda wait: lax.optimization_barrier(unpad(grad)), three, two, four)
    y = run(lambda wait: output(1, y, wait), three, one, two, four)
    local_out = run(lambda wait: lax.optimization_barrier(jnp.where(live, unpad(y), 0)), three, two, four)
    while one.result is None or two.result is None:
        run(nothing, three, one, two, four)

    def places_mlp(wait):
        return place_pair(1, two, place_pair(0, one, [(D, F), (F, D)], wait), wait)

    up_grad, down_grad = run(places_mlp, three, four)
    while four.result is None or len(three.sends) != 2 or three.sends[0][1] != "c":
        run(nothing, three, four)
    total = four.result
    blocks = [(0, (0, 0), 0, 0), (1, (0, 0), 0, 1), (1, (0, 1), 1, 0), (1, (0, 2), 1, 1)]

    def last_rows(wait):
        pieces = [t[LR : LR + glen].reshape(1, glen, D) for t in (y, grad)]
        pieces += [total[i] for i in range(8)] + [total[8 : 8 + nf].reshape(-1)]
        own = [v for v, _ in three.sends]
        return lax.optimization_barrier(tuple(pieces)), place_half(0, blocks, own, [(D, D), (D, 3 * D)], wait)

    pieces, made = run(last_rows, three)
    global_out, global_grad, *total = pieces
    out_grad, qkv_grad = place_half(1, blocks, three.result[1::2], made)

    return (
        global_out,
        local_out,
        global_grad,
        local_grad,
        total[0],
        total[1],
        qkv_grad,
        total[2],
        total[3],
        out_grad,
        total[4],
        total[5],
        total[6],
        up_grad,
        total[8],
        down_grad,
        total[7],
    )


def solution(mesh):
    tokens = (P("dp", "blk", None), P(("blk", "dp"), None, None))
    return jax.shard_map(
        per_device,
        mesh=mesh,
        in_specs=(*tokens, P(("blk", "dp")), *([P()] * 13), *tokens),
        out_specs=(*tokens, *tokens, *([P()] * 13)),
        check_vma=False,
    )
```

```python
import math

import jax
import jax.numpy as jnp
import numpy as np
from jax import lax
from jax.experimental import pallas as pl
from jax.experimental.pallas import tpu as pltpu
from jax.sharding import PartitionSpec as P

HEADS = 12
EPS = 1e-06
bf16 = jnp.bfloat16
f32 = jnp.float32
CHUNK = 48
BLANK = -1e30


def nn(a, b):
    return lax.dot_general(a, b, (((1,), (0,)), ((), ())), preferred_element_type=f32)


def nt(a, b):
    return lax.dot_general(a, b, (((1,), (1,)), ((), ())), preferred_element_type=f32)


def tn(a, b):
    return lax.dot_general(a, b, (((0,), (0,)), ((), ())), preferred_element_type=f32)


def normal(x):
    center = x - jnp.mean(x, axis=-1, keepdims=True)
    r = lax.rsqrt(jnp.mean(center * center, axis=-1, keepdims=True) + EPS)
    return center * r, r


def norm_back(n, r, dh, gain):
    e = dh * gain
    return r * (e - jnp.mean(e, axis=-1, keepdims=True) - n * jnp.mean(e * n, axis=-1, keepdims=True))


def fold(x):
    return jnp.sum(x.reshape(x.shape[0] // 8, 8, x.shape[1]), axis=0)


def head_masks():
    lane = lax.broadcasted_iota(jnp.int32, (1, 128), 1)
    return [(lane < 64).astype(f32).astype(bf16), (lane >= 64).astype(f32).astype(bf16)]


def stack_heads(t, masks):
    return jnp.concatenate([t * m for m in masks], axis=0)


def pick_heads(t):
    n = t.shape[0] // 2
    low = lax.broadcasted_iota(jnp.int32, (n, 128), 1) < 64
    return jnp.where(low, t[:n], t[n:])


def attend(loads, mask, masks):
    scores = [nt(k(), stack_heads(q(), masks)) + mask for q, k, _ in loads]
    chances = []
    for s in scores:
        p = jnp.exp(s - jnp.max(s, axis=0, keepdims=True))
        chances.append((p * (1.0 / jnp.sum(p, axis=0, keepdims=True))).astype(bf16))
    return [(p, pick_heads(tn(p, v()))) for p, (_, _, v) in zip(chances, loads)]


def attend_back(loads, store, masks):
    outer = [stack_heads(do(), masks) for _, _, _, _, do in loads]
    dps = [nt(v(), d) for d, (_, _, v, _, _) in zip(outer, loads)]
    dvs = [nn(p(), d).astype(bf16) for d, (_, _, _, p, _) in zip(outer, loads)]
    dss = []
    for dp, (_, _, _, p, _) in zip(dps, loads):
        pf = p().astype(f32)
        dss.append((pf * (dp - jnp.sum(pf * dp, axis=0, keepdims=True))).astype(bf16))
    for i, (ds, dv, (q, k, _, _, _)) in enumerate(zip(dss, dvs, loads)):
        dk = nn(ds, stack_heads(q(), masks))
        dq = pick_heads(tn(ds, k())) * 0.125
        store(i, dq.astype(bf16), dk, dv)


def call(kernel, ins, outs, flops, scratch=(), vmem=16, smem=0, far=0, far_out=0, aliases=None, wait=()):
    ins = list(ins)
    if wait:
        ins, _ = lax.optimization_barrier((ins, list(wait)))
    whole = pl.BlockSpec(memory_space=pltpu.VMEM)
    scalars = pl.BlockSpec(memory_space=pltpu.SMEM)
    lying = pl.BlockSpec(memory_space=pltpu.HBM)
    near = len(ins) - far

    def nbytes(s, d):
        return math.prod(s) * jnp.dtype(d).itemsize

    def pinned(i, t):
        if i >= near:
            return pltpu.with_memory_space_constraint(t, pltpu.HBM)
        if i >= smem and nbytes(t.shape, t.dtype) > 2**16:
            return pltpu.with_memory_space_constraint(t, pltpu.VMEM)
        return t

    def result(i, s, d):
        if i < far_out:
            return pltpu.HBM(s, d)
        if nbytes(s, d) > 2**16:
            return pltpu.VMEM(s, d)
        return jax.ShapeDtypeStruct(s, d)

    size = sum(nbytes(t.shape, t.dtype) for t in ins) + sum(nbytes(s, d) for s, d in outs)
    return pl.pallas_call(
        kernel,
        in_specs=[scalars] * smem + [whole] * (near - smem) + [lying] * far,
        out_specs=[lying] * far_out + [whole] * (len(outs) - far_out),
        out_shape=[result(i, s, d) for i, (s, d) in enumerate(outs)],
        scratch_shapes=list(scratch),
        input_output_aliases=aliases or {},
        compiler_params=pltpu.CompilerParams(vmem_limit_bytes=vmem * 2**20),
        cost_estimate=pl.CostEstimate(flops=1, bytes_accessed=1, transcendentals=0),
    )(*[pinned(i, t) for i, t in enumerate(ins)])


def per_device(
    global_tokens,
    local_tokens,
    local_count,
    first_gain,
    first_shift,
    qkv_weight,
    query_bias,
    value_bias,
    out_weight,
    out_bias,
    second_gain,
    second_shift,
    up_weight,
    up_bias,
    down_weight,
    mlp_down_bias,
    global_cotan,
    local_cotan,
):
    crops, glen, D = global_tokens.shape
    slots, llen, _ = local_tokens.shape
    F = up_weight.shape[1]
    nf = F // D
    lpad = -(-llen // 8) * 8
    gpad = -(-glen // 16) * 16
    assert crops == 1 and D == 768 and lpad * 2 % 16 == 0 and nf == 4
    LR = slots * lpad
    R = LR + gpad
    pair = 2 * lpad
    pairs = D // 128
    units = 4
    laps = slots // 2 // units
    assert laps * units * 2 == slots and slots % 8 == 0
    nblk, ndp = lax.axis_size("blk"), lax.axis_size("dp")
    blk, dp = lax.axis_index("blk"), lax.axis_index("dp")
    assert nblk == 2 and ndp % 16 == 0
    per_step = 8
    SR = per_step * lpad
    cuts = 3 if R % 48 == 0 else 1
    row_cuts = [slice(i * (R // cuts), (i + 1) * (R // cuts)) for i in range(cuts)]
    half_at = R // 96 * 48
    assert R % 48 == 0
    row_halves = [slice(0, half_at), slice(half_at, R)]

    bit_of = {"c": 0, "x": 1, "z0": 2, "z1": 3, "y": 4}

    def swap(v, b):
        if b == "y":
            return lax.ppermute(v, "blk", [(0, 1), (1, 0)])
        m = b if isinstance(b, int) else 1 << bit_of[b]
        return lax.ppermute(v, "dp", [(i, i ^ m) for i in range(ndp)])

    me = (dp & 15) + 16 * blk
    relative = jnp.arange(32, dtype=jnp.int32) ^ me.astype(jnp.int32)

    def places(order):
        pos = jnp.zeros_like(relative)
        for b in order:
            pos = 2 * pos + ((relative >> bit_of[b]) & 1)
        return pos * CHUNK

    ORDERS = (("c", "x", "y", "z0", "z1"), ("c", "y", "x", "z0", "z1"))
    PLACES = [places(o) for o in ORDERS]

    def copies(*triples):
        return [pltpu.make_async_copy(src, dst, sem) for src, dst, sem in triples]

    def start(moves):
        for t in moves:
            t.start()

    def finish(moves):
        for t in moves:
            t.wait()

    xg = global_tokens.reshape(glen, D)
    xg_other = swap(xg, "y")
    live = (jnp.arange(slots, dtype=jnp.int32) < local_count[0])[:, None, None]

    def unpad(t):
        return t[:LR].reshape(slots, lpad, D)[:, :llen]

    singles = [first_gain, first_shift, query_bias, value_bias, out_bias, second_gain, second_shift, mlp_down_bias, up_bias]
    *singles, xg_other = lax.optimization_barrier((*singles, xg_other))
    vectors = jnp.concatenate([t.reshape(-1, D) for t in singles], axis=0)
    G1, C1, QB, VB, OB, G2, C2, DB, UB = range(9)

    assert 8 + nf <= 16
    lmask = np.full((pair, 2 * pair), BLANK, np.float32)
    for r in range(2 * pair):
        t = (r % pair) // lpad * lpad
        lmask[t : t + llen, r] = 0.0
    gmask = np.full((2 * gpad, 2 * gpad), BLANK, np.float32)
    gmask[:glen] = 0.0
    gmask[gpad : gpad + glen] = 0.0
    lmask = jnp.asarray(lmask)
    gmask = jnp.asarray(gmask)

    def front(
        n_r, v_r, m_r, x_r, dyl_h, xg_h, xo_h, dg_h, gm_h, w_h, wo_h, u_h, d_h,
        x_h, h_h, qkv_h, p_h, qkvg_o, pg_o, o_o, x1_o, h2_o, dy_o, led_o, wo_o, u_o, d_o,
        x_s, dyl_r, h_o, qkv_o, p_o, w, xs, ys, gs, ds, xg_r, xo_r, dg_r, gm_r, acc, sems,
    ):
        def vec(i):
            return v_r[i : i + 1, :]

        cols = [slice(k * D, (k + 1) * D) for k in range(3)]
        loads_w = copies(*[(w_h.at[:, c], w.at[:, c], sems.at[k]) for k, c in enumerate(cols)])
        loads_g = copies(
            (xg_h, xg_r, sems.at[3]), (xo_h, xo_r, sems.at[4]), (dg_h, dg_r, sems.at[5]), (gm_h, gm_r, sems.at[6])
        )
        loads_next = copies(
            (wo_h, wo_o, sems.at[7]), (u_h.at[:, 0:D], u_o, sems.at[8]), (d_h.at[0:D, :], d_o, sems.at[9])
        )
        out_x = copies((x_s, x_h, sems.at[10]))
        load_dy = copies((dyl_h, dyl_r, sems.at[11]))
        start(load_dy + loads_w + loads_g + loads_next)
        xs[...] = jnp.zeros_like(xs)
        ys[...] = jnp.zeros_like(ys)
        acc[...] = jnp.zeros_like(acc)

        def padded(ref, i, xs):
            for j in range(per_step):
                xs[j * lpad : j * lpad + llen, :] = ref[per_step * i + j].astype(f32)
            return xs[...]

        def out_part(i):
            n = units * pair
            rows = pl.ds(pl.multiple_of(i * n, n), n)
            these = pl.ds(i * units * pairs, units * pairs)
            return copies(
                (qkv_o.at[rows], qkv_h.at[rows], sems.at[13 + 2 * i]),
                (p_o.at[these], p_h.at[these], sems.at[14 + 2 * i]),
            )


        def norm_step(i, carry):
            rows = pl.ds(pl.multiple_of(i * SR, SR), SR)
            x = padded(x_r, i, xs)
            x_s[rows, :] = x.astype(bf16)
            n, _ = normal(x)
            h_o[rows, :] = (n * vec(G1) + vec(C1)).astype(bf16)
            at = i * SR + lax.broadcasted_iota(jnp.int32, (SR, 1), 0)
            dy = jnp.where(at < n_r[0] * lpad, padded(dyl_r, i, ys), 0.0)
            dy_o[rows, :] = dy.astype(bf16)
            acc[...] += fold(dy)
            return carry

        finish(load_dy)
        lax.fori_loop(0, LR // SR, norm_step, 0)
        start(out_x)
        finish(loads_g + loads_w + loads_next)
        ds[...] = jnp.zeros_like(ds)
        ds[0:glen, :] = dg_r[...].astype(f32)
        dy_o[LR:R, :] = ds[...].astype(bf16)
        acc[...] += fold(ds[...])
        gs[...] = jnp.zeros_like(gs)
        gs[0:glen, :] = xg_r[...].astype(f32)
        gs[gpad : gpad + glen, :] = xo_r[...].astype(f32)
        n, _ = normal(gs[...])
        hg = (n * vec(G1) + vec(C1)).astype(bf16)
        h_o[LR:, :] = hg
        out_h = copies((h_o, h_h, sems.at[12]))
        start(out_h)
        for k, c in enumerate(cols):
            t = nn(h_o[...], w[:, c])
            if k != 1:
                t = t + vec(QB if k == 0 else VB)
            t = t.astype(bf16)
            if k == 0:
                t = t * jnp.asarray(0.125, bf16)
            qkv_o[:, c] = t[0:LR]
            qkvg_o[:, c] = t[LR:]
        masks = head_masks()

        def attn_step(i, carry):
            where, loads = [], []
            for u in range(units):
                g = i * units + u
                rows = pl.ds(pl.multiple_of(g * pair, pair), pair)
                for t in range(pairs):
                    a = 128 * t
                    where.append((g * pairs + t, rows, slice(a, a + 128)))
                    loads.append([lambda rows=rows, b=k * D + a: qkv_o[rows, b : b + 128] for k in range(3)])
            for (at, rows, lanes), (pt, o) in zip(where, attend(loads, m_r[...], masks)):
                p_o[at] = pt
                o_o[rows, lanes] = o.astype(bf16)
            start(out_part(i))
            return carry

        lax.fori_loop(0, laps, attn_step, 0)
        loads = []
        for t in range(pairs):
            a, b, c = (slice(k * D + 128 * t, k * D + 128 * t + 128) for k in range(3))
            loads.append(
                [lambda a=a: qkvg_o[0:gpad, a], lambda b=b: qkvg_o[:, b], lambda c=c: qkvg_o[:, c]]
            )
        for t, (p, o) in enumerate(attend(loads, gm_r[...], masks)):
            pg_o[t] = p
            o_o[LR:R, 128 * t : 128 * t + 128] = o.astype(bf16)
        finish(out_h + out_x)
        for i in range(laps):
            finish(out_part(i))
        x1_o[0:LR, :] = x_s[...].astype(f32)
        x1_o[LR:R, :] = gs[0:gpad, :]
        for r in row_cuts:
            x1 = nn(o_o[r, :], wo_o[...]) + vec(OB) + x1_o[r, :]
            x1_o[r, :] = x1
            n2, _ = normal(x1)
            h2_o[r, :] = (n2 * vec(G2) + vec(C2)).astype(bf16)
        led_o[...] = jnp.zeros_like(led_o)
        led_o[7:8, :] = jnp.sum(acc[...], axis=0, keepdims=True)

    RX = R + gpad
    attn_kept = [((RX, D), bf16), ((LR, 3 * D), bf16), ((slots // 2 * pairs, pair, 2 * pair), bf16)]
    x_far, h, qkv_l, p_l, qkv_g, p_g, o, x1, h2, dy, ledger, wo, wu, wd = call(
        front,
        [
            local_count, vectors, lmask, local_tokens, local_cotan, xg, xg_other, global_cotan.reshape(glen, D), gmask,
            qkv_weight, out_weight, up_weight, down_weight,
        ],
        [((LR, D), bf16)]
        + attn_kept
        + [
            ((2 * gpad, 3 * D), bf16), ((pairs, 2 * gpad, 2 * gpad), bf16), ((R, D), bf16),
            ((R, D), f32), ((R, D), bf16), ((R, D), bf16), ((16, D), f32),
            ((D, D), bf16), ((D, D), bf16), ((D, D), bf16),
        ],
        0,
        scratch=[pltpu.VMEM((LR, D), bf16), pltpu.VMEM((slots, llen, D), bf16), pltpu.VMEM((RX, D), bf16)]
        + [pltpu.VMEM(s, d) for s, d in attn_kept[1:]]
        + [
            pltpu.VMEM((D, 3 * D), bf16), pltpu.VMEM((SR, D), f32), pltpu.VMEM((SR, D), f32), pltpu.VMEM((2 * gpad, D), f32),
            pltpu.VMEM((gpad, D), f32),
            pltpu.VMEM((glen, D), bf16), pltpu.VMEM((glen, D), bf16), pltpu.VMEM((glen, D), bf16),
            pltpu.VMEM((2 * gpad, 2 * gpad), f32), pltpu.VMEM((8, D), f32), pltpu.SemaphoreType.DMA((13 + 2 * laps,)),
        ],
        smem=1,
        far=9,
        far_out=4,
        vmem=27,
    )

    def place_of(pos_r, i):
        at = pos_r[i]
        mine = at < 16 * CHUNK
        return mine, pl.ds(pl.multiple_of(jnp.where(mine, at, at - 16 * CHUNK), 16), CHUNK)

    def put(keep_o, send_o, pos_r, half, value):
        for j in range(0, 16, 2):
            mine, here = place_of(pos_r, half * 16 + j)
            x, y = (value[(j + k) * CHUNK : (j + k + 1) * CHUNK, :] for k in range(2))
            keep_o[here, :] = jnp.where(mine, x, y)
            send_o[here, :] = jnp.where(mine, y, x)

    def mlp(f, state, wait):
        first, last = f == 0, f == nf - 1
        late = f == nf - 2
        there = slice((f + 1) * D, (f + 2) * D)

        def kernel(pos_r, h_r, d_r, v_r, u_r, w_r, side_r, led_r, *rest):
            if last:
                a_late_r, du_late_r, u_late_r, *rest = rest
            u_h, w_h, *rest = rest
            if last:
                x1_h, *rest = rest
            if not late:
                a_h, *rest = rest
            if last:
                a_late_h, *rest = rest
            if first:
                side_h, *rest = rest
            keep_o, send_o, led_o, *rest = rest
            if late:
                a_o, du_r, *rest = rest
            else:
                dh_o, *rest = rest
            if last:
                x1_o, *rest = rest
            else:
                u_o, w_o, *rest = rest
            if not late:
                a_o, du_r, *rest = rest
            (sems,) = rest
            moves = []
            if not last:
                moves = copies((u_h.at[:, there], u_o, sems.at[0]), (w_h.at[there, :], w_o, sems.at[1]))
            if first:
                moves += copies((side_r, side_h, sems.at[2]))
            if last:
                moves += copies((x1_h, x1_o, sems.at[0]), (a_late_r, a_late_h, sems.at[1]))
            stores = [] if late else copies((a_o, a_h, sems.at[3]))
            start(moves)
            acc = jnp.zeros((8, D), f32)
            for i, rows in enumerate(row_cuts):
                u = nn(h_r[rows, :], u_r[...]) + v_r[UB + f : UB + f + 1, :]
                da = nt(d_r[rows, :], w_r[...])
                cdf = 0.5 + 0.5 * lax.erf(u * math.sqrt(0.5))
                a_o[rows, :] = (u * cdf).astype(bf16)
                slope = cdf + u * (jnp.exp(u * u * -0.5) * (1.0 / math.sqrt(2 * math.pi)))
                du = (da * slope).astype(bf16)
                du_r[rows, :] = du
                acc = acc + fold(du.astype(f32))
                if i == cuts - 2:
                    finish(moves)
            start(stores)
            led_o[...] = led_r[...]
            led_o[8 + f : 9 + f, :] = jnp.sum(acc, axis=0, keepdims=True)
            put(keep_o, send_o, pos_r, 0, tn(a_o[...], d_r[...]).astype(bf16))
            put(keep_o, send_o, pos_r, 1, tn(h_r[...], du_r[...]).astype(bf16))
            for rows in [] if late else row_cuts:
                dh = nt(du_r[rows, :], u_r[...])
                if last:
                    dh = dh + nt(du_late_r[rows, :], u_late_r[...])
                dh_o[rows, :] = dh if first else side_r[rows, :] + dh
            finish(stores)

        nonlocal ledger
        u_w, d_w, side, *before = state
        wide, full = ((R, D), bf16), ((R, D), f32)
        out = call(
            kernel,
            [PLACES[f % 2], h2, dy, vectors, u_w, d_w, side, ledger, *before, up_weight, down_weight] + ([x1] if last else []),
            ([] if late else [wide])
            + ([wide] if last else [])
            + ([full] if first else [])
            + [((D, D), bf16), ((D, D), bf16), ((16, D), f32)]
            + ([wide, wide] if late else [full])
            + ([full] if last else [((D, D), bf16), ((D, D), bf16)]),
            0,
            scratch=([] if late else [pltpu.VMEM((R, D), bf16), pltpu.VMEM((R, D), bf16)])
            + [pltpu.SemaphoreType.DMA((4,))],
            far_out=0 if late else 2 if first or last else 1,
            smem=1,
            far=3 if last else 2,
            aliases={6: 5 if last else 4} if not (first or late) else {},
            vmem=9,
            wait=wait,
        )
        out = list(out)
        if last:
            a, a_late, keep, send, ledger, dh, x1_near = out
            acts.extend([a_late, a])
            return (keep, send), (x1_near, dh)
        if late:
            keep, send, ledger, a, du, *state = out
            return (keep, send), (*state, side, a, du, u_w)
        acts.append(out.pop(0))
        if first:
            kept.append(out.pop(0))
        keep, send, ledger, dh, *state = out
        return (keep, send), (*state, dh)

    def second_back(wait):
        def kernel(dy_r, dh_r, v_r, x1_r, wo_r, led_r, q_h, p_h, dx_o, do_o, g_o, led_o, q_o, p_o, acc, sems):
            first_lap = copies(
                (q_h.at[0 : units * pair], q_o, sems.at[0]), (p_h.at[0 : units * pairs], p_o, sems.at[1])
            )
            start(first_lap)
            for k in range(3):
                acc[k] = jnp.zeros((8, D), f32)
            for r in row_cuts:
                dh = dh_r[r, :]
                n, rs = normal(x1_r[r, :])
                dx = dy_r[r, :].astype(f32) + norm_back(n, rs, dh, v_r[G2 : G2 + 1, :])
                dx_o[r, :] = dx
                g = dx.astype(bf16)
                g_o[r, :] = g
                acc[0] += fold(dh * n)
                acc[1] += fold(dh)
                acc[2] += fold(g.astype(f32))
            finish(first_lap)
            led_o[...] = led_r[...]
            for k, i in enumerate((5, 6, 4)):
                led_o[i : i + 1, :] = jnp.sum(acc[k], axis=0, keepdims=True)
            do_o[...] = nt(g_o[...], wo_r[...]).astype(bf16)

        return call(
            kernel,
            [dy, dh2, vectors, x1_near, wo, ledger, qkv_l, p_l],
            [
                ((R, D), f32), ((R, D), bf16), ((R, D), bf16), ((16, D), f32),
                ((units * pair, 3 * D), bf16), ((units * pairs, pair, 2 * pair), bf16),
            ],
            0,
            scratch=[pltpu.VMEM((3, 8, D), f32), pltpu.SemaphoreType.DMA((2,))],
            far=2,
            vmem=6,
            wait=wait,
        )

    def global_back(wait):
        def kernel(d_r, g_r, o_r, q_r, p_r, wg_o, dq_o, own_o, other_o):
            wg_o[...] = tn(o_r[...], g_r[...]).astype(bf16)
            loads = []
            for t in range(pairs):
                a, b, c = (slice(k * D + 128 * t, k * D + 128 * t + 128) for k in range(3))
                loads.append(
                    [
                        lambda a=a: q_r[0:gpad, a],
                        lambda b=b: q_r[:, b],
                        lambda c=c: q_r[:, c],
                        lambda t=t: p_r[t],
                        lambda a=a: d_r[LR:R, a],
                    ]
                )

            def store(t, dq, dk, dv):
                a, b = (slice(k * D + 128 * t, k * D + 128 * t + 128) for k in range(2))
                dq_o[:, a] = dq
                own_o[:, a] = dk[0:gpad].astype(bf16)
                own_o[:, b] = dv[0:gpad]
                other_o[:, a] = dk[gpad:].astype(bf16)
                other_o[:, b] = dv[gpad:]

            attend_back(loads, store, head_masks())

        return call(
            kernel,
            [do, g_mid, o, qkv_g, p_g],
            [((D, D), bf16), ((gpad, D), bf16), ((gpad, 2 * D), bf16), ((gpad, 2 * D), bf16)],
            0,
            vmem=8,
            wait=wait,
        )

    def local_back(wait):
        def kernel(d_r, q0_r, p0_r, dx_r, q_h, p_h, w_h, h_h, dx_h, o_r, w_o, h_o, q_s, p_s, sems):
            n, np_ = units * pair, units * pairs

            def load(i):
                rows = pl.ds(pl.multiple_of(i * n, n), n)
                here = pl.ds(pl.multiple_of((i - 1) * n, n), n)
                these, there = pl.ds(i * np_, np_), pl.ds((i - 1) * np_, np_)
                return copies(
                    (q_h.at[rows], q_s.at[here], sems.at[2 * i]), (p_h.at[these], p_s.at[there], sems.at[2 * i + 1])
                )

            more = copies((w_h, w_o, sems.at[0]), (h_h, h_o, sems.at[1]), (dx_r, dx_h, sems.at[2 * laps]))
            for i in range(1, laps):
                start(load(i))
            start(more)
            masks = head_masks()

            def lap(i, q_r, p_r, at):
                where, loads = [], []
                for u in range(units):
                    rows = pl.ds(pl.multiple_of(i * n + u * pair, pair), pair)
                    here = pl.ds(pl.multiple_of(at * n + u * pair, pair), pair)
                    for t in range(pairs):
                        a, b, c = (slice(k * D + 128 * t, k * D + 128 * t + 128) for k in range(3))
                        where.append((rows, a, b, c))
                        loads.append(
                            [lambda here=here, x=x: q_r[here, x] for x in (a, b, c)]
                            + [lambda m=at * np_ + u * pairs + t: p_r[m], lambda rows=rows, a=a: d_r[rows, a]]
                        )

                def store(m, dq, dk, dv):
                    rows, a, b, c = where[m]
                    o_r[rows, a] = dq
                    o_r[rows, b] = dk.astype(bf16)
                    o_r[rows, c] = dv

                attend_back(loads, store, masks)

            def attn_step(i, carry):
                finish(load(i))
                lap(i, q_s, p_s, i - 1)
                return carry

            lap(0, q0_r, p0_r, 0)
            lax.fori_loop(1, laps - 1, attn_step, 0)
            finish(more)
            attn_step(laps - 1, 0)

        out = call(
            kernel,
            [do, q_first, p_first, dx1, qkv_l, p_l, qkv_weight, h],
            [((R, D), f32), ((RX, 3 * D), bf16), ((D, 3 * D), bf16), ((RX, D), bf16)],
            0,
            scratch=[
                pltpu.VMEM((LR - units * pair, 3 * D), bf16),
                pltpu.VMEM((slots // 2 * pairs - units * pairs, pair, 2 * pair), bf16),
                pltpu.SemaphoreType.DMA((2 * laps + 1,)),
            ],
            far=4,
            far_out=1,
            vmem=12,
            wait=wait,
        )
        return out[1:], out[0]

    def qkv_back(wait):
        def kernel(pa_r, pb_r, dqkv_r, h_r, dq_r, own_r, other_r, gout_r, led_r, dqkv_o, ka_o, sa_o, kb_o, sb_o, led_o):
            led_o[...] = led_r[...]
            dqkv_o[LR:R, 0:D] = dq_r[...]
            dqkv_o[LR:R, D:] = own_r[...]
            dqkv_o[R:, 0:D] = jnp.zeros((gpad, D), bf16)
            dqkv_o[R:, D:] = other_r[...]
            put(ka_o, sa_o, pa_r, 0, gout_r[...])
            for k, at in enumerate(((ka_o, sa_o, pa_r, 1), (kb_o, sb_o, pb_r, 0), (kb_o, sb_o, pb_r, 1))):
                cols = slice(k * D, (k + 1) * D)
                put(*at, tn(h_r[...], dqkv_o[:, cols]).astype(bf16))
                if k != 1:
                    s = fold(dqkv_o[:, cols].astype(f32))
                    i = 2 + k // 2
                    led_o[i : i + 1, :] = jnp.sum(s, axis=0, keepdims=True)

        return call(
            kernel,
            [PLACES[0], PLACES[1], dqkv, h_back, dq_g, kv_own, kv_other, g_out, ledger],
            [((RX, 3 * D), bf16)] + [((D, D), bf16)] * 4 + [((16, D), f32)],
            0,
            smem=2,
            vmem=4,
            aliases={2: 0},
            wait=wait,
        )

    def first_back(part, so_far, wait):
        rows = row_halves[part]
        n_rows = rows.stop - rows.start
        stop = min(rows.stop, LR)

        def kernel(v_r, w_r, dqkv_r, led_r, *rest):
            if part:
                kv_r, _, *rest = rest
            x_h, xg_h, dx_h, wd_h, t_o, led_o, *rest = rest
            if not part:
                wd_o, *rest = rest
            dh_s, x_s, acc, xg_s, gs, dx_r, own_s, sems = rest
            moves = copies(
                (x_h.at[rows.start : stop], x_s.at[0 : stop - rows.start], sems.at[0]), (dx_h.at[rows], dx_r, sems.at[2])
            )
            if part:
                moves += copies((xg_h, xg_s, sems.at[1]))
            else:
                moves += copies((wd_h, wd_o, sems.at[1]))
            start(moves)
            dh_s[0 : stop - rows.start, :] = nt(dqkv_r[rows.start : stop, :], w_r[...])
            if part:
                own_s[:, 0:D] = dqkv_r[LR:R, 0:D]
                own_s[:, D:] = (dqkv_r[LR:R, D:].astype(f32) + kv_r[...].astype(f32)).astype(bf16)
                dh_s[stop - rows.start :, :] = nt(own_s[...], w_r[...])
            acc[...] = jnp.zeros_like(acc)
            finish(moves)
            if part:
                gs[...] = jnp.zeros_like(gs)
                gs[0:glen, :] = xg_s[...].astype(f32)
                x_s[stop - rows.start :, :] = gs[...].astype(bf16)

            def step(i, carry):
                here = pl.ds(pl.multiple_of(i * 48, 16), 48)
                there = pl.ds(pl.multiple_of(rows.start + i * 48, 16), 48)
                n, r = normal(x_s[here, :].astype(f32))
                dh = dh_s[here, :]
                t = dx_r[here, :] + norm_back(n, r, dh, v_r[G1 : G1 + 1, :])
                t_o[there, :] = t.astype(bf16)
                acc[0] += fold(dh * n)
                acc[1] += fold(dh)
                return carry

            lax.fori_loop(0, n_rows // 48, step, 0, unroll=True)
            led_o[...] = led_r[...]
            for k in range(2):
                led_o[k : k + 1, :] = led_r[k : k + 1, :] + jnp.sum(acc[k], axis=0, keepdims=True)

        return call(
            kernel,
            [vectors, wqkv, dqkv, ledger] + ([kv_back, so_far] if part else []) + [x_far, xg, dx1, down_weight],
            [((R, D), bf16), ((16, D), f32)] + ([] if part else [((F, D), bf16)]),
            0,
            scratch=[
                pltpu.VMEM((n_rows, D), f32), pltpu.VMEM((n_rows, D), bf16), pltpu.VMEM((2, 8, D), f32),
                pltpu.VMEM((glen, D), bf16), pltpu.VMEM((gpad, D), f32), pltpu.VMEM((n_rows, D), f32),
                pltpu.VMEM((gpad, 3 * D), bf16), pltpu.SemaphoreType.DMA((3,)),
            ],
            far=4,
            vmem=10,
            aliases={5: 0} if part else {},
            wait=wait,
        )

    def output(part, so_far, wait):
        rows = row_halves[part]
        n_rows = rows.stop - rows.start

        def kernel(v_r, w_r, *rest):
            if part:
                _, *rest = rest
            x1_h, *rest = rest
            a_hs, (y_o, a_r, x1_r, sems) = rest[:nf], rest[nf:]
            loads = copies(
                *[(a_hs[f].at[rows], a_r.at[f], sems.at[f]) for f in range(nf)], (x1_h.at[rows], x1_r, sems.at[nf])
            )
            start(loads)
            loads[0].wait()
            y = nn(a_r[0], w_r[0:D, :])
            finish(loads[1:])
            y = y + x1_r[...] + v_r[DB : DB + 1, :]
            for f in range(1, nf):
                y = y + nn(a_r[f], w_r[f * D : (f + 1) * D, :])
            y_o[rows, :] = y.astype(bf16)

        return call(
            kernel,
            [vectors, wd_all] + ([so_far] if part else []) + [x1, *acts],
            [((R, D), bf16)],
            0,
            scratch=[
                pltpu.VMEM((nf, n_rows, D), bf16), pltpu.VMEM((n_rows, D), f32), pltpu.SemaphoreType.DMA((nf + 1,)),
            ],
            far=1 + nf,
            vmem=11,
            aliases={2: 0} if part else {},
            wait=wait,
        )[0]

    def add(a, b):
        return (a.astype(f32) + b.astype(f32)).astype(bf16)

    class Flow:
        def __init__(self, steps):
            self.steps = steps
            self.sends = next(steps)
            self.result = self.got = None

        def launch(self):
            self.got = [swap(v, b) for v, b in self.sends]

        def land(self):
            got, self.got = self.got, None
            try:
                self.sends = self.steps.send(got)
            except StopIteration as end:
                self.result = end.value

    def halves(v):
        h = v.shape[0] // 2
        return v[:h], v[h:]

    def join(*parts):
        return jnp.concatenate(parts, axis=0)

    def sum_two(a, b):
        for bits in (("c", "c"), ("x", "y"), ("y", "x")):
            if bits[0] == "c":
                (a, sa), (b, sb) = a, b
            else:
                (a, sa), (b, sb) = halves(a), halves(b)
            ga, gb = yield [(sa, bits[0]), (sb, bits[1])]
            a, b = add(a, ga), add(b, gb)
        for bit in ("z0", "z1"):
            (a, sa), (b, sb) = halves(a), halves(b)
            (got,) = yield [(join(sa, sb), bit)]
            ga, gb = halves(got)
            a, b = add(a, ga), add(b, gb)
        m = 16
        while m < ndp:
            v = join(a, b)
            (got,) = yield [(v, m)]
            a, b = halves(add(v, got))
            m *= 2
        for bit in ("z1", "z0"):
            (got,) = yield [(join(a, b), bit)]
            ga, gb = halves(got)
            a, b = join(a, ga), join(b, gb)
        for bits in (("y", "x"), ("x", "y"), ("c", "c")):
            ga, gb = yield [(a, bits[0]), (b, bits[1])]
            if bits[0] != "c":
                a, b = join(a, ga), join(b, gb)
        return [a, ga, b, gb]

    def send_once(v, bit):
        (got,) = yield [(v, bit)]
        return got

    def sum_small(v):
        more, m = [], 16
        while m < ndp:
            more.append(m)
            m *= 2
        for bit in (*more, "z1", "c", "z0", "y", "x"):
            v = v.astype(bf16)
            (got,) = yield [(v, bit)]
            v = v.astype(f32) + got.astype(f32)
        return v

    def place(blocks, places, sums, outs, wait=()):
        made = [not isinstance(t, tuple) for t in outs]
        shapes = [t.shape if m else t for t, m in zip(outs, made)]

        def kernel(*refs):
            pos_rs, refs = refs[: len(places)], refs[len(places) :]
            sums_r, refs = refs[: len(sums)], refs[len(sums) + sum(made) :]
            outs_h, (work, sems) = refs[: len(outs)], refs[len(outs) :]
            moves = []
            for n, (which, where, side, half) in enumerate(blocks):
                pos_r, own_r, got_r = pos_rs[side], sums_r[2 * side], sums_r[2 * side + 1]
                if n >= 2:
                    moves[n - 2].wait()
                for j in range(0, 16, 2):
                    mine, here = place_of(pos_r, half * 16 + j)
                    x, y = own_r[here, :].astype(f32), got_r[here, :].astype(f32)
                    work[n % 2, j * CHUNK : (j + 1) * CHUNK, :] = jnp.where(mine, x, y)
                    work[n % 2, (j + 1) * CHUNK : (j + 2) * CHUNK, :] = jnp.where(mine, y, x)
                r, c = (slice(i * D, (i + 1) * D) for i in where)
                moves += copies((work.at[n % 2], outs_h[which].at[r, c], sems.at[n]))
                moves[n].start()
            for t in moves[-2:]:
                t.wait()

        before = [t for t, m in zip(outs, made) if m]
        return call(
            kernel,
            places + sums + before,
            [(s, f32) for s in shapes],
            0,
            scratch=[pltpu.VMEM((2, D, D), f32), pltpu.SemaphoreType.DMA((len(blocks),))],
            vmem=7,
            smem=len(places),
            far=len(before),
            far_out=len(outs),
            aliases={len(places + sums) + i: j for i, j in enumerate(j for j, m in enumerate(made) if m)},
            wait=wait,
        )

    waits = []

    def run(kernel, *flows, hold=()):
        flows = [flow for flow in flows if flow.result is None]
        for flow in (*flows, *hold):
            if flow.got is None:
                flow.launch()
        sends = [v for flow in flows for v, _ in flow.sends]
        out = kernel(waits + sends) if kernel else None
        if kernel and flows:
            out, got = lax.optimization_barrier((out, [flow.got for flow in flows]))
            for flow, t in zip(flows, got):
                flow.got = t
        waits[:] = [t for flow in flows for t in flow.got]
        for flow in flows:
            flow.land()
        return out

    acts, blocks, kept = [], [], []
    state = (wu, wd, x1)

    def hidden(f, *flows):
        nonlocal state
        block, state = run(lambda wait: mlp(f, state, wait), *flows)
        blocks.append(block)

    hidden(0)
    (x1,) = kept
    hidden(1)
    one = Flow(sum_two(*blocks[0:2]))
    hidden(2, one)
    hidden(3, one)
    x1_near, dh2 = state
    two = Flow(sum_two(*blocks[2:4]))
    dx1, do, g_mid, ledger, q_first, p_first = run(second_back, one, two)
    (g_out, dq_g, kv_own, kv_other), ((dqkv, wqkv, h_back), dx1) = run(
        lambda wait: (global_back(wait), local_back(wait)), one, two
    )
    dqkv, ka, sa, kb, sb, ledger = run(qkv_back, one, two)

    three = Flow(sum_two((ka, sa), (kb, sb)))
    nothing = lambda wait: ()

    def place_half(pick, blocks, sums, outs, wait=()):
        made = [not isinstance(t, tuple) for t in outs]
        shapes = [t.shape if m else t for t, m in zip(outs, made)]

        def kernel(pa_r, pb_r, *refs):
            sums_r, refs = refs[:2], refs[2 + sum(made) :]
            outs_h, (work, sems) = refs[: len(outs)], refs[len(outs) :]
            moves = []
            for n, (which, where, side, half) in enumerate(blocks):
                for k in range(8):
                    mine, here = place_of((pa_r, pb_r)[side], half * 16 + 2 * k)
                    j = 2 * k + jnp.where(mine, pick, 1 - pick)
                    work[n, k] = sums_r[side][here, :].astype(f32)
                    rows = pl.ds(pl.multiple_of(where[0] * D + j * CHUNK, 16), CHUNK)
                    cols = slice(where[1] * D, (where[1] + 1) * D)
                    moves += copies((work.at[n, k], outs_h[which].at[rows, cols], sems.at[8 * n + k]))
                    moves[-1].start()
            finish(moves)

        before = [t for t, m in zip(outs, made) if m]
        return call(
            kernel,
            PLACES + sums + before,
            [(s, f32) for s in shapes],
            0,
            scratch=[pltpu.VMEM((len(blocks), 8, CHUNK, D), f32), pltpu.SemaphoreType.DMA((8 * len(blocks),))],
            vmem=7,
            smem=2,
            far=len(before),
            far_out=len(outs),
            aliases={4 + i: i for i in range(len(before))},
            wait=wait,
        )

    def place_pair(k, flow, outs, wait):
        blocks = [(i, (0, f) if i == 0 else (f, 0), f % 2, 1 - i) for f in (2 * k, 2 * k + 1) for i in (1, 0)]
        return place(blocks, PLACES, flow.result, outs, wait)

    run(nothing, three)
    grad, ledger, wd_all = run(lambda wait: first_back(0, None, wait), three, one, two)
    kv = Flow(send_once(lax.optimization_barrier((kv_other, three.sends[0][0]))[0], "y"))
    run(nothing, three, one, two, kv)
    kv_back = kv.result
    grad, ledger = run(lambda wait: first_back(1, grad, wait), three, one, two)
    four = Flow(sum_small(ledger))
    y = run(lambda wait: output(0, None, wait), three, one, two, four)
    local_grad = run(lambda wait: lax.optimization_barrier(unpad(grad)), three, two, four)
    y = run(lambda wait: output(1, y, wait), three, one, two, four)
    local_out = run(lambda wait: lax.optimization_barrier(jnp.where(live, unpad(y), 0)), three, two, four)
    while one.result is None or two.result is None:
        run(nothing, three, one, two, four)

    def places_mlp(wait):
        return place_pair(1, two, place_pair(0, one, [(D, F), (F, D)], wait), wait)

    up_grad, down_grad = run(places_mlp, three, four)
    while four.result is None or len(three.sends) != 2 or three.sends[0][1] != "c":
        run(nothing, three, four)
    total = four.result
    blocks = [(0, (0, 0), 0, 0), (1, (0, 0), 0, 1), (1, (0, 1), 1, 0), (1, (0, 2), 1, 1)]

    def last_rows(wait):
        pieces = [t[LR : LR + glen].reshape(1, glen, D) for t in (y, grad)]
        pieces += [total[i] for i in range(8)] + [total[8 : 8 + nf].reshape(-1)]
        own = [v for v, _ in three.sends]
        return lax.optimization_barrier(tuple(pieces)), place_half(0, blocks, own, [(D, D), (D, 3 * D)], wait)

    pieces, made = run(last_rows, three)
    global_out, global_grad, *total = pieces
    out_grad, qkv_grad = place_half(1, blocks, three.result[1::2], made)

    return (
        global_out,
        local_out,
        global_grad,
        local_grad,
        total[0],
        total[1],
        qkv_grad,
        total[2],
        total[3],
        out_grad,
        total[4],
        total[5],
        total[6],
        up_grad,
        total[8],
        down_grad,
        total[7],
    )


def solution(mesh):
    tokens = (P("dp", "blk", None), P(("blk", "dp"), None, None))
    return jax.shard_map(
        per_device,
        mesh=mesh,
        in_specs=(*tokens, P(("blk", "dp")), *([P()] * 13), *tokens),
        out_specs=(*tokens, *tokens, *([P()] * 13)),
        check_vma=False,
    )
```
